128 devices in a mesh: fsdp: 16 (over y_hi, x, core), ctx: 2 (over y_lo), tp: 4 (over z).
Axes of the slice: x: 4, y: 4 (y_hi: 2, y_lo: 2; y = y_hi * 2 + y_lo), z: 4, core: 2. Of those that a mesh axis runs over, the one named last changes fastest.
Arguments:
- tokens: bfloat16 [4096, 2560], P(('fsdp', 'ctx')), may hold values from -6 to 6
- cotangent: bfloat16 [4096, 2560], P(('fsdp', 'ctx')), may hold values from -6 to 6
- segments: int32 [4096], P('fsdp'), may hold values from 0 to 3, as said below
- owner: int32 [2560], replicated, may hold values from 0 to 15, as said below
- master: float32 [3840, 27904], P(('fsdp', 'ctx'), 'tp'), may hold values from -0.355756237 to 0.355756237
- moment_one: float32 [3840, 27904], P(('fsdp', 'ctx'), 'tp'), may hold values from -960 to 960
- moment_two: float32 [3840, 27904], P(('fsdp', 'ctx'), 'tp'), may hold values from 368.64 to 409600
- gains: float32 [2, 2560], replicated, may hold values from 0.5 to 1.5
- gain_one: float32 [2, 2560], replicated, may hold values from -768 to 768
- gain_two: float32 [2, 2560], replicated, may hold values from 6144 to 147456
Outputs:
- output: bfloat16 [4096, 2560], P(('fsdp', 'ctx'))
- grad_tokens: bfloat16 [4096, 2560], P(('fsdp', 'ctx'))
- new_master: float32 [3840, 27904], P(('fsdp', 'ctx'), 'tp')
- new_moment_one: float32 [3840, 27904], P(('fsdp', 'ctx'), 'tp')
- new_moment_two: float32 [3840, 27904], P(('fsdp', 'ctx'), 'tp')
- new_gains: float32 [2, 2560], replicated
- new_gain_one: float32 [2, 2560], replicated
- new_gain_two: float32 [2, 2560], replicated
The draws below stay inside these ranges and needn't reach their ends.
Inputs may be any that keep to these rules, and one draw needn't show every extreme that they name: `segments`: in each sequence of 256 tokens the numbers start at 0 and never fall. `owner`: each index of fsdp is named at most 240 times, and one is named exactly 240 times.
All inputs are finite; a program needn't handle non-finite values.
Results may differ from the reference program's by a relative error of at most 0.014.
The reference program's roundings to bfloat16 on the way count: a program that leaves them out, or rounds other values in their place, can miss the bound.
Values may be sent and summed in bfloat16 or wider, within the bound.
No kernel may reach another device: no remote copies, remote signals or barrier semaphores. Data moves between devices by JAX's collectives and lax.ppermute only.
A program may use at most 384 MiB of HBM per device.

```python
import math
import jax
import jax.numpy as jnp
from jax import lax

D = 2560
H = 32
KVH = 8
HD = 80
FF = 7168
SEQ_LEN = 256
STEP = 5
TOKENS = 4096
FEAT_SHARE = 160
UNIT_WIDTH = 6976
CAP = 240
SLOTS = 3840
N_FSDP = 16
N_TP = 4


def kind_scale(values):
    query_width = H * HD // N_TP
    kv_width = KVH * HD // N_TP
    ff_width = FF // N_TP
    ends = [query_width, query_width + kv_width, query_width + 2 * kv_width, query_width + 2 * kv_width + ff_width, query_width + 2 * kv_width + 2 * ff_width, 2 * query_width + 2 * kv_width + 2 * ff_width]
    columns = jnp.arange(N_TP * UNIT_WIDTH, dtype=jnp.int32) % UNIT_WIDTH
    scale = jnp.full((N_TP * UNIT_WIDTH,), values[6], jnp.float32)
    for number in range(5, -1, -1):
        scale = jnp.where(columns < ends[number], values[number], scale)
    return scale


def weight_values():
    model = 1.0 / math.sqrt(D)
    return [1.5 * model, 1.5 * model, model, model, model, 6.0 / math.sqrt(H * HD), 1.5 / math.sqrt(FF)]


def grad_values():
    root = math.sqrt(TOKENS)
    return [2.0 * root, 3.0 * root, 5.0 * root, 0.5 * root, 0.5 * root, 0.3 * root, 0.6 * root]


def draw_master(key, part):
    key = jax.random.fold_in(key, 3)
    scale = kind_scale(weight_values())
    base = jax.random.truncated_normal(key, -3.0, 3.0, (SLOTS, N_TP * UNIT_WIDTH), jnp.float32)
    return base * scale[None, :]


def draw_moment_one(key, part):
    key = jax.random.fold_in(key, 5)
    scale = kind_scale(grad_values())
    base = jax.random.truncated_normal(key, -3.0, 3.0, (SLOTS, N_TP * UNIT_WIDTH), jnp.float32)
    return base * scale[None, :]


def draw_moment_two(key, part):
    key = jax.random.fold_in(key, 9)
    scale = kind_scale(grad_values())
    factor = jnp.exp(jax.random.uniform(key, (SLOTS, N_TP * UNIT_WIDTH), jnp.float32, 0.0, math.log(4.0)))
    return factor * (scale * scale)[None, :]


def draw_segments(key, part):
    key = jax.random.fold_in(key, 11)
    key_first, key_second, key_third = jax.random.split(key, 3)
    half = SEQ_LEN // 2
    band = SEQ_LEN // 8
    first = jax.random.randint(key_first, (N_FSDP, 1), 1, half - band + 1)
    second = jax.random.randint(key_second, (N_FSDP, 1), half + band, SEQ_LEN)
    third = jax.random.randint(key_third, (N_FSDP, 1), 1, SEQ_LEN - 2 * band + 1)
    third = third + (third > half - band).astype(jnp.int32) * (2 * band - 1)
    position = jnp.arange(SEQ_LEN, dtype=jnp.int32)[None, :]
    numbers = (position >= first).astype(jnp.int32) + (position >= second).astype(jnp.int32) + (position >= third).astype(jnp.int32)
    return numbers.reshape(N_FSDP * SEQ_LEN)


def draw_owner(key, part):
    key = jax.random.fold_in(key, 13)
    key_rank, key_feature = jax.random.split(key, 2)
    lowest = 2 * FEAT_SHARE - CAP
    ranks = jnp.arange(N_FSDP, dtype=jnp.int32)
    loads = lowest + (CAP - lowest) * ranks // (N_FSDP - 1)
    extra = D - jnp.sum(loads)
    loads = loads + (ranks < extra).astype(jnp.int32)
    bounds = jnp.cumsum(loads)
    position = jnp.arange(D, dtype=jnp.int32)
    rank_of = jnp.sum((position[:, None] >= bounds[None, :]).astype(jnp.int32), axis=1)
    shuffled = jax.random.permutation(key_rank, N_FSDP).astype(jnp.int32)
    owner_by_place = shuffled[rank_of]
    order = jax.random.permutation(key_feature, D).astype(jnp.int32)
    return jnp.zeros((D,), jnp.int32).at[order].set(owner_by_place)


def shard_levels(key, shape, shards, least, largest):
    loudness, own = 1.0, jax.random.fold_in(key, 6)
    for dim, shards_of in shards:
        heights = jnp.exp(jax.random.uniform(jax.random.fold_in(own, dim), (shards_of,), jnp.float32, least / len(shards), largest / len(shards)))
        loudness = loudness * jnp.repeat(heights, shape[dim] // shards_of).reshape([-1 if axis == dim else 1 for axis in range(len(shape))])
    return loudness


def gaussian(stream_key, extent, spread, reach, cuts=(), kind=jnp.bfloat16):
    result = spread * jax.random.normal(stream_key, extent, jnp.float32)
    if cuts:
        result = result * shard_levels(stream_key, extent, cuts, -0.22, 0.18)
    return jnp.clip(result, -reach, reach).astype(kind)


def setup_inputs(seed: int = 0) -> dict:
    key_of = jax.random.split(jax.random.key(seed), 11)
    tokens = gaussian(key_of[0], (TOKENS, D), 1.0, 6.0, ((0, 32),))
    cotangent = gaussian(key_of[1], (TOKENS, D), 1.0, 6.0, ((0, 32),))
    segments = draw_segments(jax.random.fold_in(key_of[10], 71), 0)
    owner = draw_owner(jax.random.fold_in(key_of[10], 71), 0)
    master = draw_master(jax.random.fold_in(key_of[10], 71), 0)
    moment_one = draw_moment_one(jax.random.fold_in(key_of[10], 71), 0)
    moment_two = draw_moment_two(jax.random.fold_in(key_of[10], 71), 0)
    gains = jnp.clip(1.0 + 0.1 * jax.random.normal(key_of[7], (2, D), jnp.float32), 0.5, 1.5)
    gain_one = gaussian(key_of[8], (2, D), (2 * TOKENS ** 0.5), 768.0, (), jnp.float32)
    gain_two = jnp.clip(jnp.exp(jax.random.uniform(key_of[9], (2, D), jnp.float32, math.log(6144.0), math.log(147456.0))), 6144.0, 147456.0)
    return {"tokens": tokens, "cotangent": cotangent, "segments": segments, "owner": owner, "master": master, "moment_one": moment_one, "moment_two": moment_two, "gains": gains, "gain_one": gain_one, "gain_two": gain_two}


EPS_NORM = 1e-05
EPS_ADAM = 1e-08
THETA = 1000000.0
BETA = 0.5
LEARN = 0.05
LEARN_GAIN = 0.2
DECAY = 0.1
NEG_BIG = -1e+30
HIGHEST = lax.Precision.HIGHEST

@jax.custom_vjp
def low(v):
    return lax.optimization_barrier(v.astype(jnp.bfloat16)).astype(jnp.float32)

@jax.custom_vjp
def low_back(v):
    return v

def low_keep(v):
    return (low(v), None)

def low_pass(kept, grad):
    return (grad,)

def back_keep(v):
    return (v, None)

def back_low(kept, grad):
    return (low(grad),)
low.defvjp(low_keep, low_pass)
low_back.defvjp(back_keep, back_low)

def product(left, right):
    return jnp.dot(left, right, precision=HIGHEST, preferred_element_type=jnp.float32)

def product_t(left, right):
    return lax.dot_general(left, right, (((1,), (1,)), ((), ())), precision=HIGHEST, preferred_element_type=jnp.float32)

def rms_normed(values):
    return values * lax.rsqrt(lax.optimization_barrier(jnp.mean(values * values, axis=1, keepdims=True)) + EPS_NORM)

def rotary_tables(positions):
    half = HD // 2
    freq = jnp.exp(-jnp.log(THETA) * (2.0 * jnp.arange(half, dtype=jnp.float32) / HD))
    angle = positions.astype(jnp.float32)[:, None] * freq[None, :]
    return (jnp.cos(angle), jnp.sin(angle))

def rotate(values, cosine, sine, heads, sign):
    half = HD // 2
    shaped = values.reshape(values.shape[0], heads, HD)
    first = shaped[:, :, :half]
    second = shaped[:, :, half:]
    turned_cos = cosine[:, None, :]
    turned_sin = sine[:, None, :] * sign
    joined = jnp.concatenate([first * turned_cos - second * turned_sin, second * turned_cos + first * turned_sin], axis=2)
    return joined.reshape(values.shape)

def slot_of(owner):
    onehot = (owner[:, None] == jnp.arange(N_FSDP, dtype=jnp.int32)[None, :]).astype(jnp.int32)
    rank = lax.optimization_barrier(jnp.sum((jnp.cumsum(onehot, axis=0) - onehot) * onehot, axis=1))
    return (owner * CAP + rank).astype(jnp.int32)

def sequence_attention(block):
    query, keys, values, segment = block
    group = H // KVH
    shaped = query.reshape(SEQ_LEN, KVH, group, HD)
    keyed = keys.reshape(SEQ_LEN, KVH, HD)
    valued = values.reshape(SEQ_LEN, KVH, HD)
    scores = jnp.einsum('ikgd,jkd->kgij', shaped, keyed, precision=HIGHEST) * HD ** (-0.5)
    scores = low_back(scores)
    position = jnp.arange(SEQ_LEN, dtype=jnp.int32)
    mask = (segment[:, None] == segment[None, :]) & (position[None, :] <= position[:, None])
    scores = jnp.where(mask[None, None], scores, NEG_BIG)
    top = lax.optimization_barrier(jnp.max(scores, axis=3, keepdims=True))
    weight = jnp.exp(scores - top)
    probs = low(weight / lax.optimization_barrier(jnp.sum(weight, axis=3, keepdims=True)))
    attended = jnp.einsum('kgij,jkd->ikgd', probs, valued, precision=HIGHEST)
    return attended.reshape(SEQ_LEN, H * HD)

def adam_step(weight, first, second, grad, rate, decay):
    first_new = BETA * first + (1.0 - BETA) * grad
    second_new = BETA * second + (1.0 - BETA) * grad * grad
    correction = 1.0 - BETA ** STEP
    update = first_new / correction / (jnp.sqrt(second_new / correction) + EPS_ADAM)
    return (weight - rate * (update + decay * weight), first_new, second_new)

def reference(tokens, cotangent, segments, owner, master, moment_one, moment_two, gains, gain_one, gain_two):
    query_width = H * HD // N_TP
    kv_width = KVH * HD // N_TP
    ff_width = FF // N_TP
    widths = [query_width, kv_width, kv_width, ff_width, ff_width, query_width, ff_width]
    slot = slot_of(owner)
    unit_rows = master[slot].reshape(D, N_TP, UNIT_WIDTH)
    params = []
    offset = 0
    for width in widths:
        params.append(unit_rows[:, :, offset:offset + width].reshape(D, N_TP * width))
        offset = offset + width
    position = jnp.arange(TOKENS, dtype=jnp.int32) % SEQ_LEN
    cosine, sine = rotary_tables(position)
    sequences = segments.reshape(N_FSDP, SEQ_LEN)

    def forward(inputs, w_query, w_key, w_value, w_gate, w_up, w_out, w_down, gain_pair):
        xn_one = low(rms_normed(inputs) * gain_pair[0])
        query = low(rotate(low_back(product(xn_one, low(w_query))), cosine, sine, H, 1.0))
        keys = low(rotate(low_back(product(xn_one, low(w_key))), cosine, sine, KVH, 1.0))
        values = low_back(low(product(xn_one, low(w_value))))
        attended = lax.map(jax.checkpoint(sequence_attention), (query.reshape(N_FSDP, SEQ_LEN, H * HD), keys.reshape(N_FSDP, SEQ_LEN, KVH * HD), values.reshape(N_FSDP, SEQ_LEN, KVH * HD), sequences))
        attended = low_back(low(attended.reshape(TOKENS, H * HD)))
        hidden = inputs + low_back(product_t(attended, low(w_out)))
        xn_two = low(rms_normed(hidden) * gain_pair[1])
        gate = low_back(product(xn_two, low(w_gate)))
        up = low_back(product(xn_two, low(w_up)))
        act = low(jax.nn.silu(gate) * up)
        return hidden + low_back(product_t(act, low(w_down)))
    output, pull = jax.vjp(forward, tokens.astype(jnp.float32), params[0], params[1], params[2], params[3], params[4], params[5], params[6], gains)
    grads = pull(cotangent.astype(jnp.float32))
    pieces = []
    for number in range(7):
        pieces.append(grads[number + 1].reshape(D, N_TP, widths[number]))
    grad_rows = jnp.concatenate(pieces, axis=2).reshape(D, N_TP * UNIT_WIDTH)
    grad_master = jnp.zeros((SLOTS, N_TP * UNIT_WIDTH), jnp.float32).at[slot].set(grad_rows)
    valid = jnp.zeros((SLOTS,), jnp.bool_).at[slot].set(True)[:, None]
    new_master, new_one, new_two = adam_step(master, moment_one, moment_two, grad_master, LEARN, DECAY)
    zero = jnp.zeros_like(master)
    new_gains, new_gain_one, new_gain_two = adam_step(gains, gain_one, gain_two, grads[8], LEARN_GAIN, 0.0)
    return (output.astype(jnp.bfloat16), grads[0].astype(jnp.bfloat16), jnp.where(valid, new_master, zero), jnp.where(valid, new_one, zero), jnp.where(valid, new_two, zero), new_gains, new_gain_one, new_gain_two)
```

```python
import functools

import jax
import jax.numpy as jnp
from jax import lax
from jax.experimental import pallas as pl
from jax.experimental.pallas import tpu as pltpu
from jax.sharding import Mesh
from jax.sharding import PartitionSpec as P

HD = 80
STEP = 5
D = 2560
CAP = 240
HALF = 120
SEQ = 256
RING = 4

EPS_NORM = 1e-05
EPS_ADAM = 1e-08
THETA = 1000000.0
BETA = 0.5
LEARN = 0.05
LEARN_GAIN = 0.2
DECAY = 0.1
NEG_BIG = -1e30

X = "x"
Y = ("yh", "yl")
OFFSETS = (0, -1, 1, 2)
LOW = jnp.bfloat16
F32 = jnp.float32

HEADS = 4
QW = 320
KW = 80
FW = 896
ATTN = 896
CUT = 512
FFN = 3 * FW
FFN_CUT = 1408
WIDE = ATTN + FFN
WIDE_CUT = 1792
MAP = (
    (0, 320, QW),
    (640, 640, KW),
    (800, 720, KW),
    (960, 1792, FW),
    (2752, 2688, FW),
    (4544, 0, QW),
    (5184, 896, FW),
)
PIECES = 8
BLK = 4 * HALF
LANES = 512
VMEM = 60 * 1024 * 1024


def dot(left, right, left_axis, right_axis):
    return lax.dot_general(
        left, right, (((left_axis,), (right_axis,)), ((), ())), preferred_element_type=F32
    )


def move(block, axis, distance):
    route = [(i, (i + distance) % RING) for i in range(RING)]
    return lax.ppermute(block, axis, route)


def swap_core(block):
    return lax.ppermute(block, "core", [(0, 1), (1, 0)])


def swap_sequences(block):
    return lax.ppermute(block, ("core", "yl"), [(0, 0), (1, 2), (2, 1), (3, 3)])


def near(block, axis):
    return move(block, axis, 1), move(block, axis, -1)


def far(back, ahead, axis):
    return move(back, axis, 1), move(ahead, axis, -1)


def halves(back, ahead, axis, cut):
    return far(back[:, :cut], ahead[:, cut:], axis)


def slot_ids(x, y):
    offsets = jnp.array(OFFSETS, jnp.int32)
    every = jnp.arange(RING, dtype=jnp.int32)
    rows = jnp.arange(HALF, dtype=jnp.int32)

    def slots(xx, yy, core):
        return (((yy // 2) * RING + xx) * 2 + core) * CAP + (yy % 2) * HALF

    first = slots(((x + offsets) % RING)[None, :, None], every[:, None, None], 0) + rows
    second = slots(every[:, None, None], ((y + offsets) % RING)[None, :, None], 1) + rows
    ids = jnp.concatenate([first, second], axis=0).reshape(PIECES, 1, BLK)
    return jnp.pad(ids, ((0, 0), (0, 0), (0, LANES - BLK)), constant_values=-1)


def three_parts(values):
    high = lax.reduce_precision(values, 8, 7)
    rest = values - high
    middle = lax.reduce_precision(rest, 8, 7)
    return jnp.concatenate([high, middle, rest - middle], axis=0).astype(LOW)


def whole():
    return pl.BlockSpec(memory_space=pltpu.VMEM)


def hbm():
    return pl.BlockSpec(memory_space=pl.ANY)


def smem():
    return pl.BlockSpec(memory_space=pltpu.SMEM)


def cost(flops, size):
    return pl.CostEstimate(flops=flops, bytes_accessed=size, transcendentals=0)


def pack_kernel(meta_ref, master_ref, own_ref, send_ref):
    is_low = meta_ref[0] == 0
    valid = lax.broadcasted_iota(jnp.int32, (HALF, 1), 0) < meta_ref[4]
    blank = jnp.zeros((HALF, ATTN - 800), LOW)
    own_ref[:, 800:ATTN] = blank
    send_ref[:, 800:ATTN] = blank
    for start, at, width in MAP:
        low = jnp.where(valid, master_ref[:, start : start + width], 0.0)
        high = jnp.where(valid, master_ref[:, start + width : start + 2 * width], 0.0)
        own_ref[:, at : at + width] = jnp.where(is_low, low, high).astype(LOW)
        send_ref[:, at : at + width] = jnp.where(is_low, high, low).astype(LOW)


def pack(meta, master):
    return pl.pallas_call(
        pack_kernel,
        in_specs=[smem(), whole()],
        out_specs=[whole()] * 2,
        out_shape=[jax.ShapeDtypeStruct((HALF, WIDE), LOW)] * 2,
        compiler_params=pltpu.CompilerParams(vmem_limit_bytes=VMEM),
        name="pack",
    )(meta, master)


def assemble_kernel(*refs):
    for kind in range(2):
        block, back, ahead, one, two = refs[5 * kind : 5 * kind + 5]
        outs = refs[10 + 4 * kind : 14 + 4 * kind]
        for j, out in enumerate(outs):
            at = j * FW
            for k, ref in enumerate((block, back, ahead)):
                out[k * HALF : (k + 1) * HALF, :] = ref[:, at : at + FW]
            last = one if j < 2 else two
            at = at % WIDE_CUT
            out[3 * HALF :, :] = last[:, at : at + FW]


def assemble(*blocks):
    return pl.pallas_call(
        assemble_kernel,
        in_specs=[whole()] * 10,
        out_specs=[whole()] * 8,
        out_shape=[jax.ShapeDtypeStruct((BLK, FW), LOW)] * 8,
        compiler_params=pltpu.CompilerParams(vmem_limit_bytes=VMEM),
        cost_estimate=cost(0, 0),
        name="assemble",
    )(*blocks)


def place_kernel(
    meta_ref, slot_ref, ids_ref, swapped_ref, gains_ref, parts_ref, xc_ref, in_ref, cot_ref, gain_ref, rows
):
    @pl.when(pl.program_id(0) == 0)
    def _():
        at = pl.multiple_of(meta_ref[1] * 32, 32)
        tokens = swapped_ref[:128].astype(F32)
        scale = lax.rsqrt(jnp.sum(tokens * tokens, axis=1, keepdims=True) / D + EPS_NORM)
        rows[:128] = (tokens * scale * gains_ref[0:1]).astype(LOW)
        rows[128:256] = swapped_ref[128:256]
        rows[256:288] = swapped_ref[pl.ds(at, 32)]
        rows[288:320] = swapped_ref[pl.ds(128 + at, 32)]
        rows[320:] = parts_ref[...]

    place = jnp.where(slot_ref[...] == ids_ref[0], 1.0, 0.0).astype(LOW)
    placed = dot(rows[...], place, 1, 0)
    xc_ref[0] = placed[:256].astype(LOW)
    in_ref[0] = placed[256:288]
    cot_ref[0] = placed[288:320]
    gain_ref[0] = placed[320:322] + placed[322:324] + placed[324:326]


def to_slots(meta, slot, ids, swapped, gains, parts):
    def piece(rows):
        return pl.BlockSpec((1, rows, LANES), lambda p: (p, 0, 0))

    def same(shape):
        return pl.BlockSpec(shape, lambda p: (0, 0))

    return pl.pallas_call(
        place_kernel,
        grid=(PIECES,),
        in_specs=[
            smem(),
            same((D, 1)),
            pl.BlockSpec((1, 1, LANES), lambda p: (p, 0, 0)),
            same(swapped.shape),
            same((2, D)),
            same((16, D)),
        ],
        out_specs=[piece(256), piece(32), piece(32), piece(2)],
        out_shape=[
            jax.ShapeDtypeStruct((PIECES, 256, LANES), LOW),
            jax.ShapeDtypeStruct((PIECES, 32, LANES), F32),
            jax.ShapeDtypeStruct((PIECES, 32, LANES), F32),
            jax.ShapeDtypeStruct((PIECES, 2, LANES), F32),
        ],
        scratch_shapes=[pltpu.VMEM((336, D), LOW)],
        compiler_params=pltpu.CompilerParams(vmem_limit_bytes=VMEM),
        cost_estimate=cost(0, 0),
        name="to_slots",
    )(meta, slot, ids, swapped, gains, parts)


def unplace_kernel(slot_ref, ids_ref, rows_ref, out_ref):
    place = jnp.where(slot_ref[...] == ids_ref[0], 1.0, 0.0).astype(LOW)

    @pl.when(pl.program_id(0) == 0)
    def _():
        out_ref[...] = jnp.zeros_like(out_ref)

    out_ref[...] += dot(rows_ref[0], place, 1, 1)


def from_slots(rows, slot, ids):
    n = rows.shape[1]
    return pl.pallas_call(
        unplace_kernel,
        grid=(PIECES,),
        in_specs=[
            pl.BlockSpec((D, 1), lambda p: (0, 0)),
            pl.BlockSpec((1, 1, LANES), lambda p: (p, 0, 0)),
            pl.BlockSpec((1, n, LANES), lambda p: (p, 0, 0)),
        ],
        out_specs=pl.BlockSpec((n, D), lambda p: (0, 0)),
        out_shape=jax.ShapeDtypeStruct((n, D), F32),
        compiler_params=pltpu.CompilerParams(vmem_limit_bytes=VMEM),
        name="from_slots",
    )(slot, ids, rows)


def start_weights(meta_ref, refs, held, sems, cut):
    x = meta_ref[2]
    y = meta_ref[3]
    for base, at, group in ((0, y, refs[:5]), (RING, x, refs[5:])):
        for ref, offset in zip(group[:3], (0, -1, 1)):
            p = base + lax.rem(at + offset + RING, RING)
            pltpu.make_async_copy(ref, held.at[p], sems.at[p]).start()
        p = base + lax.rem(at + 2, RING)
        pltpu.make_async_copy(group[3], held.at[p, :, pl.ds(0, cut)], sems.at[p]).start()
        rest = held.shape[2] - cut
        pltpu.make_async_copy(group[4], held.at[p, :, pl.ds(cut, rest)], sems.at[p]).start()


def wait_weights(held, sems, p):
    pltpu.make_async_copy(held.at[p], held.at[p], sems.at[p]).wait()


def split_rows(value, scratch, core, p, keep_ref, send_ref):
    scratch[:, :BLK] = value
    for z in range(RING):
        keep_ref[z, p] = scratch[pl.ds(pl.multiple_of(core * 128 + 32 * z, 32), 32), :]
        send_ref[z, p] = scratch[pl.ds(pl.multiple_of((1 - core) * 128 + 32 * z, 32), 32), :].astype(
            LOW
        )


def join_rows(is_low, own, got):
    return jnp.concatenate(
        [jnp.where(is_low, own, got), jnp.where(is_low, got, own)], axis=0
    )


def rope(values, cosine, sine):
    half = HD // 2
    turned = jnp.concatenate([-values[:, half:], values[:, :half]], axis=1)
    return values * cosine + turned * sine


def head_probs(query, keys, mask):
    scores = dot(query, keys, 1, 1) * HD ** (-0.5)
    scores = jnp.where(mask, scores, NEG_BIG)
    weight = jnp.exp(scores - jnp.max(scores, axis=1, keepdims=True))
    return weight / jnp.sum(weight, axis=1, keepdims=True)


def causal_mask(seg_col, seg_row):
    rows = lax.broadcasted_iota(jnp.int32, (SEQ, SEQ), 0)
    cols = lax.broadcasted_iota(jnp.int32, (SEQ, SEQ), 1)
    return (seg_col == seg_row) & (cols <= rows)


def attention_kernel(
    meta_ref, own_ref, got_ref, cos_ref, sin_ref, segc_ref, segr_ref, *rest
):
    w_refs = rest[:10]
    q_ref, k_ref, v_ref, o_ref, keep_ref, send_ref, held, acc, part, sems = rest[10:]
    core = meta_ref[0]
    is_low = core == 0
    start_weights(meta_ref, w_refs, held, sems, CUT)
    acc[...] = jnp.zeros_like(acc)
    part[:, BLK:] = jnp.zeros((SEQ, LANES - BLK), F32)

    def project(p, carry):
        wait_weights(held, sems, p)
        rows = join_rows(is_low, own_ref[p, :128], got_ref[p, :128])
        acc[...] += dot(rows[:, :BLK], held[p, :, 256:], 1, 0)
        return carry

    lax.fori_loop(0, PIECES, project, 0)
    cosine = cos_ref[...]
    sine = sin_ref[...]
    mask = causal_mask(segc_ref[...], segr_ref[...])
    projected = acc[...]
    keys = rope(projected[:, 384:464], cosine, sine).astype(LOW)
    values = projected[:, 464:544].astype(LOW)
    k_ref[...] = keys
    v_ref[...] = values
    outs = []
    for h in range(HEADS):
        query = rope(projected[:, 64 + h * HD : 64 + (h + 1) * HD], cosine, sine).astype(LOW)
        q_ref[h] = query
        probs = head_probs(query, keys, mask)
        outs.append(dot(probs.astype(LOW), values, 1, 0))
    outs.append(jnp.zeros((SEQ, 64), F32))
    attended = jnp.concatenate(outs, axis=1).astype(LOW)
    o_ref[...] = attended

    def spread(p, carry):
        split_rows(dot(attended, held[p, :, :384], 1, 1), part, core, p, keep_ref, send_ref)
        return carry

    lax.fori_loop(0, PIECES, spread, 0)


def split_shapes():
    return [
        jax.ShapeDtypeStruct((RING, PIECES, 32, LANES), F32),
        jax.ShapeDtypeStruct((RING, PIECES, 32, LANES), LOW),
    ]


def attention_forward(meta, own, got, tables, segs, w_attn):
    return pl.pallas_call(
        attention_kernel,
        in_specs=[smem()] + [whole()] * 6 + [hbm()] * 10,
        out_specs=[whole()] * 6,
        out_shape=[
            jax.ShapeDtypeStruct((HEADS, SEQ, HD), LOW),
            jax.ShapeDtypeStruct((SEQ, HD), LOW),
            jax.ShapeDtypeStruct((SEQ, HD), LOW),
            jax.ShapeDtypeStruct((SEQ, 384), LOW),
        ]
        + split_shapes(),
        scratch_shapes=[
            pltpu.VMEM((PIECES, BLK, ATTN), LOW),
            pltpu.VMEM((SEQ, ATTN - 256), F32),
            pltpu.VMEM((SEQ, LANES), F32),
            pltpu.SemaphoreType.DMA((PIECES,)),
        ],
        compiler_params=pltpu.CompilerParams(vmem_limit_bytes=VMEM),
        cost_estimate=cost(0, 0),
        name="attention_forward",
    )(meta, own, got, *tables, *segs, *w_attn)


def attention_back_kernel(
    meta_ref, own_ref, got_ref, cos_ref, sin_ref, segc_ref, segr_ref, q_ref, k_ref, v_ref, *rest
):
    w_refs = rest[:10]
    right_ref, keep_ref, send_ref, held, acc, part, sems = rest[10:]
    core = meta_ref[0]
    is_low = core == 0
    start_weights(meta_ref, w_refs, held, sems, CUT)
    acc[...] = jnp.zeros_like(acc)
    part[:, BLK:] = jnp.zeros((SEQ, LANES - BLK), F32)

    def project(p, carry):
        wait_weights(held, sems, p)
        own = jnp.concatenate([own_ref[z, p] for z in range(RING)], axis=0)
        got = jnp.concatenate([got_ref[z, p] for z in range(RING)], axis=0)
        acc[...] += dot(join_rows(is_low, own, got)[:, :BLK], held[p, :, :384], 1, 0)
        return carry

    lax.fori_loop(0, PIECES, project, 0)
    cosine = cos_ref[...]
    sine = -sin_ref[...]
    mask = causal_mask(segc_ref[...], segr_ref[...])
    grad_att = acc[...]
    keys = k_ref[...]
    values = v_ref[...]
    factor = HD ** (-0.5)
    grads = []
    grad_keys = jnp.zeros((SEQ, HD), F32)
    grad_values = jnp.zeros((SEQ, HD), F32)
    for h in range(HEADS):
        query = q_ref[h]
        grad_o = grad_att[:, h * HD : (h + 1) * HD].astype(LOW)
        probs = head_probs(query, keys, mask)
        grad_probs = dot(grad_o, values, 1, 1)
        inner = jnp.sum(probs * grad_probs, axis=1, keepdims=True)
        grad_scores = (probs * (grad_probs - inner)).astype(LOW)
        grads.append(rope(dot(grad_scores, keys, 1, 0) * factor, cosine, sine))
        grad_keys += dot(grad_scores, query, 0, 0)
        grad_values += dot(probs.astype(LOW), grad_o, 0, 0)
    grads.append(rope(grad_keys * factor, cosine, sine))
    grads.append(grad_values)
    zeros = [jnp.zeros((SEQ, 64), F32)]
    ends = [jnp.zeros((SEQ, 96), F32)]
    grad_qkv = jnp.concatenate(zeros + grads + ends, axis=1).astype(LOW)
    right_ref[...] = grad_qkv

    def spread(p, carry):
        split_rows(dot(grad_qkv, held[p, :, 256:], 1, 1), part, core, p, keep_ref, send_ref)
        return carry

    lax.fori_loop(0, PIECES, spread, 0)


def attention_backward(meta, own, got, tables, segs, qkv, w_attn):
    return pl.pallas_call(
        attention_back_kernel,
        in_specs=[smem()] + [whole()] * 9 + [hbm()] * 10,
        out_specs=[whole()] * 3,
        out_shape=[jax.ShapeDtypeStruct((SEQ, ATTN - 256), LOW)] + split_shapes(),
        scratch_shapes=[
            pltpu.VMEM((PIECES, BLK, ATTN), LOW),
            pltpu.VMEM((SEQ, 384), F32),
            pltpu.VMEM((SEQ, LANES), F32),
            pltpu.SemaphoreType.DMA((PIECES,)),
        ],
        compiler_params=pltpu.CompilerParams(vmem_limit_bytes=VMEM),
        cost_estimate=cost(0, 0),
        name="attention_backward",
    )(meta, own, got, *tables, *segs, *qkv, *w_attn)


def start_ffn(meta_ref, refs, held, sems):
    x = meta_ref[2]
    y = meta_ref[3]
    for base, at, group in ((0, y, refs[:13]), (RING, x, refs[13:])):
        for k, offset in enumerate((0, -1, 1)):
            p = base + lax.rem(at + offset + RING, RING)
            for j in range(3):
                into = held.at[p, :, pl.ds(j * FW, FW)]
                pltpu.make_async_copy(group[3 * k + j], into, sems.at[p]).start()
        p = base + lax.rem(at + 2, RING)
        spans = ((0, FW), (FW, CUT), (FW + CUT, FW - CUT), (2 * FW, FW))
        for ref, (start, width) in zip(group[9:], spans):
            pltpu.make_async_copy(ref, held.at[p, :, pl.ds(start, width)], sems.at[p]).start()


def ffn_kernel(meta_ref, own_ref, got_ref, cot_own_ref, cot_got_ref, *rest):
    w_refs = rest[:26]
    act_ref, grad_ref, keep_ref, send_ref, mkeep_ref, msend_ref, held, acc, part, sems = rest[26:]
    core = meta_ref[0]
    is_low = core == 0
    start_ffn(meta_ref, w_refs, held, sems)
    acc[...] = jnp.zeros_like(acc)
    part[:, BLK:] = jnp.zeros((SEQ, LANES - BLK), F32)

    def project(p, carry):
        wait_weights(held, sems, p)
        own = jnp.concatenate([own_ref[z, p] for z in range(RING)], axis=0)
        got = jnp.concatenate([got_ref[z, p] for z in range(RING)], axis=0)
        rows = join_rows(is_low, own, got)
        cot = join_rows(is_low, cot_own_ref[p, 128:], cot_got_ref[p, 128:])
        acc[:, :FW] += dot(cot[:, :BLK], held[p, :, :FW], 1, 0)
        acc[:, FW:] += dot(rows[:, :BLK], held[p, :, FW:], 1, 0)
        return carry

    lax.fori_loop(0, PIECES, project, 0)

    def units(t, carry):
        at = pl.multiple_of(t * 128, 128)
        grad_act = acc[:, pl.ds(at, 128)]
        gate = acc[:, pl.ds(at + FW, 128)]
        up = acc[:, pl.ds(at + 2 * FW, 128)]
        sigmoid = 1.0 / (1.0 + jnp.exp(-gate))
        silu = gate * sigmoid
        act_ref[:, pl.ds(at, 128)] = (silu * up).astype(LOW)
        grad_gate = grad_act * up * sigmoid * (1.0 + gate * (1.0 - sigmoid))
        grad_ref[:, pl.ds(at, 128)] = grad_gate.astype(LOW)
        grad_ref[:, pl.ds(at + FW, 128)] = (grad_act * silu).astype(LOW)
        return carry

    lax.fori_loop(0, FW // 128, units, 0)

    def spread(p, carry):
        split_rows(dot(grad_ref[...], held[p, :, FW:], 1, 1), part, core, p, keep_ref, send_ref)
        split_rows(dot(act_ref[...], held[p, :, :FW], 1, 1), part, core, p, mkeep_ref, msend_ref)
        return carry

    lax.fori_loop(0, PIECES, spread, 0)


def feed_forward(meta, own, got, cot_own, cot_got, w_ffn):
    return pl.pallas_call(
        ffn_kernel,
        in_specs=[smem()] + [whole()] * 4 + [hbm()] * 26,
        out_specs=[whole()] * 6,
        out_shape=[
            jax.ShapeDtypeStruct((SEQ, FW), LOW),
            jax.ShapeDtypeStruct((SEQ, 2 * FW), LOW),
        ]
        + split_shapes()
        + split_shapes(),
        scratch_shapes=[
            pltpu.VMEM((PIECES, BLK, FFN), LOW),
            pltpu.VMEM((SEQ, FFN), F32),
            pltpu.VMEM((SEQ, LANES), F32),
            pltpu.SemaphoreType.DMA((PIECES,)),
        ],
        compiler_params=pltpu.CompilerParams(vmem_limit_bytes=VMEM),
        cost_estimate=cost(0, 0),
        name="feed_forward",
    )(meta, own, got, cot_own, cot_got, *w_ffn)


def halves_of(part_ref, xc_ref, q, at):
    rows = jnp.concatenate([part_ref[z, q] for z in range(RING)], axis=0)
    return rows[:, :BLK], xc_ref[q, at : at + 128][:, :BLK]


def terms_kernel(meta_ref, own_ref, got_ref, xc_ref, xc_got_ref, *rest, attn, wanted):
    is_low = meta_ref[0] == 0
    rights = rest[:2]
    outs = rest[2:-1]
    acc = rest[-1]
    passed = len(wanted) == 2
    count = 4 if passed else (2 if wanted == (3,) else 1)
    if passed:
        far_refs, outs = outs[:4], outs[4:]
    for kind in range(2):
        at = meta_ref[3 - kind]
        group = outs[kind * count : kind * count + count]
        for n, k in enumerate(wanted):
            q = kind * RING + lax.rem(at + OFFSETS[k] + RING, RING)
            own_part, own_xc = halves_of(own_ref, xc_ref, q, 0 if attn else 128)
            got_part, got_xc = halves_of(got_ref, xc_got_ref, q, 0 if attn else 128)
            part = join_rows(is_low, own_part, got_part)
            xc = join_rows(is_low, own_xc, got_xc)
            if attn:
                one = dot(part, rights[0][...], 0, 0)
                two = dot(xc, rights[1][...], 0, 0)
                acc[...] = jnp.concatenate([one[:, :QW], two[:, 64:]], axis=1)
            else:
                acc[:, :FW] = dot(xc, rights[0][...], 0, 0)
                acc[:, FW:] = dot(part, rights[1][...], 0, 0)
            cut = CUT if attn else FFN_CUT
            if passed and k == 1:
                acc[:, cut:] += far_refs[2 * kind + 1][...].astype(F32)
            if passed and k == 2:
                acc[:, :cut] += far_refs[2 * kind][...].astype(F32)
            if wanted == (0,):
                group[0][...] = acc[...].astype(LOW)
            else:
                group[2 * n][...] = acc[:, :cut].astype(LOW)
                group[2 * n + 1][...] = acc[:, cut:].astype(LOW)


def weight_terms(meta, parts, xcs, rights, wanted, fars=()):
    attn = rights[0].shape[1] == 384
    width = ATTN if attn else FFN
    cut = CUT if attn else FFN_CUT
    if wanted == (0,):
        shapes = [(BLK, width)] * 2
    else:
        shapes = [(BLK, cut), (BLK, width - cut)] * (2 * len(wanted))
    return pl.pallas_call(
        functools.partial(terms_kernel, attn=attn, wanted=wanted),
        in_specs=[smem()] + [whole()] * (6 + len(fars)),
        out_specs=[whole()] * len(shapes),
        out_shape=[jax.ShapeDtypeStruct(shape, LOW) for shape in shapes],
        scratch_shapes=[pltpu.VMEM((BLK, width), F32)],
        compiler_params=pltpu.CompilerParams(vmem_limit_bytes=VMEM),
        cost_estimate=cost(0, 0),
        name="terms_attention" if attn else "terms_feed_forward",
    )(meta, *parts, *xcs, *rights, *fars)


def middle_kernel(*refs):
    for kind in range(2):
        attn = refs[5 * kind : 5 * kind + 5]
        ffn = refs[10 + 5 * kind : 15 + 5 * kind]
        own_ref, back_ref, ahead_ref, one_ref, two_ref = refs[20 + 5 * kind : 25 + 5 * kind]

        def total(own, nears, start, stop, first, last):
            value = own[first:last, start:stop].astype(F32)
            for n in nears:
                value = value + n[first:last].astype(F32)
            return value

        for k, ref in enumerate((own_ref, back_ref, ahead_ref, None)):
            first = k * HALF
            last = first + HALF
            parts = (
                (0, total(attn[0], (attn[1], attn[3]), 0, CUT, first, last)),
                (CUT, total(attn[0], (attn[2], attn[4]), CUT, ATTN, first, last)),
                (ATTN, total(ffn[0], (ffn[1], ffn[3]), 0, FFN_CUT, first, last)),
                (ATTN + FFN_CUT, total(ffn[0], (ffn[2], ffn[4]), FFN_CUT, FFN, first, last)),
            )
            for start, value in parts:
                stop = start + value.shape[1]
                if ref is not None:
                    ref[:, start:stop] = value
                elif stop <= WIDE_CUT:
                    one_ref[:, start:stop] = value.astype(LOW)
                elif start >= WIDE_CUT:
                    two_ref[:, start - WIDE_CUT : stop - WIDE_CUT] = value.astype(LOW)
                else:
                    cut = WIDE_CUT - start
                    one_ref[:, start:] = value[:, :cut].astype(LOW)
                    two_ref[:, : stop - WIDE_CUT] = value[:, cut:].astype(LOW)


def middle(attn, ffn):
    args = []
    for group in (attn, ffn):
        for kind in range(2):
            own, nears = group[kind]
            args += [own, *nears]
    shapes = [jax.ShapeDtypeStruct((HALF, WIDE), F32)] * 3
    shapes += [jax.ShapeDtypeStruct((HALF, WIDE_CUT), LOW)] * 2
    outs = pl.pallas_call(
        middle_kernel,
        in_specs=[whole()] * 20,
        out_specs=[whole()] * 10,
        out_shape=shapes * 2,
        compiler_params=pltpu.CompilerParams(vmem_limit_bytes=VMEM),
        cost_estimate=cost(0, 0),
        name="middle",
    )(*args)
    return outs[:5], outs[5:]


def add_far_kernel(*refs):
    for kind in range(2):
        back, ahead, one, two = refs[4 * kind : 4 * kind + 4]
        up, down = refs[8 + 2 * kind : 10 + 2 * kind]
        cut = one.shape[1]
        up[:, :cut] = (ahead[:, :cut] + one[...].astype(F32)).astype(LOW)
        up[:, cut:] = ahead[:, cut:].astype(LOW)
        down[:, :cut] = back[:, :cut].astype(LOW)
        down[:, cut:] = (back[:, cut:] + two[...].astype(F32)).astype(LOW)


def add_far(terms, fars):
    width = terms[0][0].shape[1]
    args = []
    for t, f in zip(terms, fars):
        args += [t[1], t[2], *f]
    outs = pl.pallas_call(
        add_far_kernel,
        in_specs=[whole()] * 8,
        out_specs=[whole()] * 4,
        out_shape=[jax.ShapeDtypeStruct((HALF, width), LOW)] * 4,
        compiler_params=pltpu.CompilerParams(vmem_limit_bytes=VMEM),
        cost_estimate=cost(0, 0),
        name="add_far",
    )(*args)
    return outs[:2], outs[2:]


def finish_kernel(meta_ref, *refs):
    is_low = meta_ref[0] == 0
    sums = []
    for kind in range(2):
        own, one, two = refs[3 * kind : 3 * kind + 3]
        sums.append(own[...] + one[...].astype(F32) + two[...].astype(F32))
    stay_ref, send_ref = refs[6:]
    stay_ref[...] = jnp.where(is_low, sums[0], sums[1])
    send_ref[...] = jnp.where(is_low, sums[1], sums[0]).astype(LOW)


def finish(meta, terms, nears):
    width = terms[0][0].shape[1]
    args = []
    for t, n in zip(terms, nears):
        args += [t[0], *n]
    return pl.pallas_call(
        finish_kernel,
        in_specs=[smem()] + [whole()] * 6,
        out_specs=[whole()] * 2,
        out_shape=[
            jax.ShapeDtypeStruct((HALF, width), F32),
            jax.ShapeDtypeStruct((HALF, width), LOW),
        ],
        compiler_params=pltpu.CompilerParams(vmem_limit_bytes=VMEM),
        cost_estimate=cost(0, 0),
        name="finish",
    )(meta, *args)


def adam_kernel(meta_ref, w_ref, m_ref, v_ref, stay, came, wo_ref, mo_ref, vo_ref, grad):
    is_low = meta_ref[0] == 0
    rows = w_ref.shape[0]
    for start, at, width in MAP:
        mine = stay[:, at : at + width]
        other = came[:, at : at + width]
        grad[:, start : start + width] = jnp.where(is_low, mine, other)
        grad[:, start + width : start + 2 * width] = jnp.where(is_low, other, mine)
    row = pl.program_id(0) * rows + lax.broadcasted_iota(jnp.int32, (rows, 1), 0)
    valid = row < meta_ref[4]
    weight, first, second = adam_step(
        w_ref[...], m_ref[...], v_ref[...], grad[...], LEARN, DECAY
    )
    wo_ref[...] = jnp.where(valid, weight, 0.0)
    mo_ref[...] = jnp.where(valid, first, 0.0)
    vo_ref[...] = jnp.where(valid, second, 0.0)


def adam(meta, master, moment_one, moment_two, stay, came):
    rows = 24
    units = master.shape[1]

    def block(width):
        return pl.BlockSpec((rows, width), lambda i: (i, 0))

    return pl.pallas_call(
        adam_kernel,
        grid=(HALF // rows,),
        in_specs=[smem()] + [block(units)] * 3 + [block(WIDE)] * 2,
        out_specs=[block(units)] * 3,
        out_shape=[jax.ShapeDtypeStruct(master.shape, F32)] * 3,
        scratch_shapes=[pltpu.VMEM((rows, units), F32)],
        compiler_params=pltpu.CompilerParams(vmem_limit_bytes=VMEM),
        name="adam",
    )(meta, master, moment_one, moment_two, stay, came)


def rms_scale(values):
    return lax.rsqrt(jnp.sum(values * values, axis=(0, 2), keepdims=True) / D + EPS_NORM)


def rms_backward(grad_out, normed, scale, gain):
    grad_normed = grad_out * gain
    inner = jnp.sum(grad_normed * normed, axis=(0, 2), keepdims=True) / D
    return scale * (grad_normed - normed * inner), jnp.sum(grad_out * normed, axis=1)


def adam_step(weight, first, second, grad, rate, decay):
    first_new = BETA * first + (1.0 - BETA) * grad
    second_new = BETA * second + (1.0 - BETA) * grad * grad
    correction = 1.0 - BETA**STEP
    update = first_new / correction / (jnp.sqrt(second_new / correction) + EPS_ADAM)
    return (weight - rate * (update + decay * weight), first_new, second_new)


def stage(*values):
    return lax.optimization_barrier(values)


def shards(
    tokens, cotangent, segments, owner, master, moment_one, moment_two, gains, gain_one, gain_two
):
    core = lax.axis_index("core")
    yl = lax.axis_index("yl")
    z = lax.axis_index("z")
    x = lax.axis_index(X)
    y = lax.axis_index("yh") * 2 + yl
    count = jnp.sum((owner == (y // 2 * RING + x) * 2 + core).astype(jnp.int32)) - yl * HALF
    meta = jnp.stack([core, z, x, y, count]).astype(jnp.int32)
    along = (Y, X)
    across = (X, Y)

    def add_core(keep, other):
        return (keep + other.astype(F32)).astype(LOW)

    def split_z(block):
        return lax.all_to_all(block, "z", split_axis=0, concat_axis=0, tiled=True)

    def sum_z(block):
        return jnp.sum(block.astype(F32), axis=0)

    def all_z(block):
        return split_z(jnp.broadcast_to(block[None], (RING, *block.shape)))

    own, send = pack(meta, master)
    got = swap_core(send)
    numbers = jnp.zeros((8, D), LOW).at[0, :SEQ].set(segments.astype(LOW))
    swapped = swap_sequences(jnp.concatenate([tokens, cotangent, numbers], axis=0))
    first = jnp.where(core == 0, own, got)
    second = jnp.where(core == 0, got, own)
    first, second, swapped, owner = stage(first, second, swapped, owner)

    near_first = near(first, X)
    near_second = near(second, Y)
    onehot = (owner[:, None] == jnp.arange(16, dtype=jnp.int32)[None, :]).astype(jnp.int32)
    rank = jnp.sum((jnp.cumsum(onehot, axis=0) - onehot) * onehot, axis=1)
    slot = (owner * CAP + rank)[:, None]
    ids = slot_ids(x, y)
    segment = swapped[256, :SEQ].astype(jnp.int32)
    segs = (segment[:, None], segment[None, :])
    parts = jnp.concatenate([three_parts(gains), jnp.zeros((10, D), LOW)], axis=0)
    xc_own, inputs, cot_z, gain = to_slots(meta, slot, ids, swapped, gains, parts)
    near_first, near_second, xc_own, inputs, cot_z, gain, segs = stage(
        near_first, near_second, xc_own, inputs, cot_z, gain, segs
    )

    far_first = halves(*near_first, X, WIDE_CUT)
    far_second = halves(*near_second, Y, WIDE_CUT)
    xc_got = swap_core(xc_own)
    far_first, far_second, xc_got = stage(far_first, far_second, xc_got)
    blocks = assemble(first, *near_first, *far_first, second, *near_second, *far_second)
    attn, down, gate, up = ([blocks[j], blocks[4 + j]] for j in range(4))

    attn_near = [near(b, axis) for b, axis in zip(attn, along)]
    position = jnp.arange(SEQ, dtype=F32)
    freq = jnp.exp(-jnp.log(THETA) * (2.0 * jnp.arange(HD // 2, dtype=F32) / HD))
    angle = position[:, None] * freq[None, :]
    tables = (
        jnp.concatenate([jnp.cos(angle)] * 2, axis=1),
        jnp.concatenate([jnp.sin(angle)] * 2, axis=1),
    )
    attn_near, tables = stage(attn_near, tables)
    attn_far = [halves(*n, axis, CUT) for n, axis in zip(attn_near, along)]
    attn_far, down = stage(attn_far, down)
    w_attn = (attn[0], *attn_near[0], *attn_far[0], attn[1], *attn_near[1], *attn_far[1])

    down_near = [near(b, axis) for b, axis in zip(down, along)]
    *qkv, attended, keep, send = attention_forward(meta, xc_own, xc_got, tables, segs, w_attn)
    down_near, gate, keep, send = stage(down_near, gate, keep, send)

    gate_near = [near(b, axis) for b, axis in zip(gate, along)]
    got = split_z(add_core(keep, swap_core(send)))
    gate_near, up, got = stage(gate_near, up, got)

    up_near = [near(b, axis) for b, axis in zip(up, along)]
    hidden = inputs + sum_z(got)
    scale_two = rms_scale(hidden)
    normed_two = hidden * scale_two
    xn_two = all_z((normed_two * gain[:, 1:2]).astype(LOW))
    xn_two_got = swap_core(xn_two)
    gate_cut = [(n[0][:, :CUT], n[1][:, CUT:]) for n in gate_near]
    up_near, down_near, gate_cut, xn_two, xn_two_got = stage(
        up_near, down_near, gate_cut, xn_two, xn_two_got
    )

    far_ends = [far(d[0], u[1], axis) for d, u, axis in zip(down_near, up_near, along)]
    far_ends, gate_cut = stage(far_ends, gate_cut)
    gate_far = [far(*g, axis) for g, axis in zip(gate_cut, along)]
    gate_far, xn_two = stage(gate_far, xn_two)
    w_ffn = []
    for kind in range(2):
        own_blocks = (down[kind], gate[kind], up[kind])
        nears = (down_near[kind], gate_near[kind], up_near[kind])
        w_ffn += [*own_blocks, *(n[0] for n in nears), *(n[1] for n in nears)]
        w_ffn += [far_ends[kind][0], *gate_far[kind], far_ends[kind][1]]

    act, grad_gu, keep, send, keep_mlp, send_mlp = feed_forward(
        meta, xn_two, xn_two_got, xc_own, xc_got, w_ffn
    )
    xn_twos = (xn_two, xn_two_got)
    xcs = (xc_own, xc_got)
    ffn_fars = weight_terms(meta, xn_twos, xcs, (act, grad_gu), (3,))
    send_got = swap_core(send)
    ffn_fars, send_got = stage(ffn_fars, send_got)
    ffn_fars = [far(*ffn_fars[2 * k : 2 * k + 2], axis) for k, axis in enumerate(along)]
    got = split_z(add_core(keep, send_got))
    ffn_own = weight_terms(meta, xn_twos, xcs, (act, grad_gu), (0,))
    ffn_fars, got, ffn_own, send_mlp = stage(ffn_fars, got, ffn_own, send_mlp)

    def sends(terms, part):
        return [
            (move(terms[4 * k + 2 + part], axis, 1), move(terms[4 * k + part], axis, -1))
            for k, axis in enumerate(along)
        ]

    ffn_terms = weight_terms(
        meta, xn_twos, xcs, (act, grad_gu), (1, 2), (*ffn_fars[0], *ffn_fars[1])
    )
    ffn_one = sends(ffn_terms, 0)
    grad_xn_two = sum_z(got)
    grad_norm_two, gain_grad_two = rms_backward(grad_xn_two, normed_two, scale_two, gain[:, 1:2])
    grad_hidden = cot_z + grad_norm_two
    grad_branch = all_z(grad_hidden.astype(LOW))
    grad_branch_got = swap_core(grad_branch)
    ffn_one, ffn_terms, grad_branch, grad_branch_got, send_mlp = stage(
        ffn_one, ffn_terms, grad_branch, grad_branch_got, send_mlp
    )

    ffn_two = sends(ffn_terms, 1)
    grad_qkv, keep, send = attention_backward(
        meta, grad_branch, grad_branch_got, tables, segs, qkv, w_attn
    )
    branches = (grad_branch, grad_branch_got)
    attn_fars = weight_terms(meta, branches, xcs, (attended, grad_qkv), (3,))
    attn_own = weight_terms(meta, branches, xcs, (attended, grad_qkv), (0,))
    mlp_got = swap_core(send_mlp)
    ffn_two, attn_fars, attn_own, keep, send, mlp_got = stage(
        ffn_two, attn_fars, attn_own, keep, send, mlp_got
    )
    attn_fars = [far(*attn_fars[2 * k : 2 * k + 2], axis) for k, axis in enumerate(along)]
    send_got = swap_core(send)
    attn_fars, send_got, mlp_got = stage(attn_fars, send_got, mlp_got)
    attn_terms = weight_terms(
        meta, branches, xcs, (attended, grad_qkv), (1, 2), (*attn_fars[0], *attn_fars[1])
    )
    attn_one = [
        (move(attn_terms[4 * k + 2], axis, 1), move(attn_terms[4 * k], axis, -1))
        for k, axis in enumerate(along)
    ]
    got = split_z(add_core(keep, send_got))
    attn_one, attn_terms, got, mlp_got = stage(attn_one, attn_terms, got, mlp_got)
    attn_two = sends(attn_terms, 1)
    grad_xn_one = sum_z(got)
    scale_one = rms_scale(inputs)
    grad_norm_one, gain_grad_one = rms_backward(
        grad_xn_one, inputs * scale_one, scale_one, gain[:, 0:1]
    )
    grad_tokens_z = (grad_hidden + grad_norm_one).astype(LOW)
    got_mlp = split_z(add_core(keep_mlp, mlp_got))
    attn_two, grad_tokens_z, gain_grad_one, got_mlp = stage(
        attn_two, grad_tokens_z, gain_grad_one, got_mlp
    )

    def both(own, one, two):
        return [(own[k], (one[k][0], two[k][0], one[k][1], two[k][1])) for k in range(2)]

    blocks = middle(both(attn_own, attn_one, attn_two), both(ffn_own, ffn_one, ffn_two))
    fars = [far(b[3], b[4], axis) for b, axis in zip(blocks, across)]
    output_z = (hidden + sum_z(got_mlp)).astype(LOW)
    gain_grads = three_parts(jnp.stack([gain_grad_one, gain_grad_two], axis=0))
    gain_grads = jnp.swapaxes(gain_grads, 0, 1)
    blank = jnp.zeros((PIECES, 10, LANES), LOW)
    last = from_slots(
        jnp.concatenate([output_z, grad_tokens_z, gain_grads, blank], axis=1), slot, ids
    )
    fars, blocks, last = stage(fars, blocks, last)
    nears = [
        (move(up, axis, 1), move(down, axis, -1))
        for (up, down), axis in zip(add_far(blocks, fars), across)
    ]
    part = lax.all_gather(last.astype(LOW), "z", axis=0, tiled=False)
    nears, blocks, part = stage(nears, blocks, part)
    stay, send = finish(meta, blocks, nears)
    came = swap_core(send).astype(F32)
    moved = swap_sequences(jnp.swapaxes(part[:, :64].reshape(RING, 2, 32, D), 0, 1))
    output = moved[0].reshape(128, D)
    grad_tokens = moved[1].reshape(128, D)

    gain_grads = part[:, 64:70].astype(F32).sum(axis=0)
    gain_grads = gain_grads[:2] + gain_grads[2:4] + gain_grads[4:6]
    gain_grads = gain_grads + swap_core(gain_grads)

    def sum_along(value, axis, at):
        back, ahead = near(value, axis)
        blocks = (value, back, ahead, move(back, axis, 1))
        every = jnp.zeros((RING, *value.shape), F32)
        for offset, block in zip(OFFSETS, blocks):
            every = lax.dynamic_update_slice_in_dim(every, block[None], (at + offset) % RING, 0)
        return jnp.sum(every, axis=0)

    gain_grads = sum_along(sum_along(gain_grads, X, x), Y, y)
    new_gains, new_gain_one, new_gain_two = adam_step(
        gains, gain_one, gain_two, gain_grads, LEARN_GAIN, 0.0
    )
    new_master, new_one, new_two = adam(meta, master, moment_one, moment_two, stay, came)
    return (
        output,
        grad_tokens,
        new_master,
        new_one,
        new_two,
        new_gains,
        new_gain_one,
        new_gain_two,
    )


def solution(mesh):
    fine = Mesh(mesh.devices.reshape(2, 4, 2, 2, 4), ("yh", "x", "core", "yl", "z"))
    rows = ("yh", "x", "core", "yl")
    in_specs = (
        P(rows, None),
        P(rows, None),
        P(("yh", "x", "core")),
        P(),
        P(rows, "z"),
        P(rows, "z"),
        P(rows, "z"),
        P(),
        P(),
        P(),
    )
    out_specs = (
        P(rows, None),
        P(rows, None),
        P(rows, "z"),
        P(rows, "z"),
        P(rows, "z"),
        P(),
        P(),
        P(),
    )
    return jax.shard_map(shards, mesh=fine, in_specs=in_specs, out_specs=out_specs, check_vma=False)
```

```python
import functools

import jax
import jax.numpy as jnp
from jax import lax
from jax.experimental import pallas as pl
from jax.experimental.pallas import tpu as pltpu
from jax.sharding import Mesh
from jax.sharding import PartitionSpec as P

HD = 80
STEP = 5
D = 2560
CAP = 240
HALF = 120
SEQ = 256
RING = 4

EPS_NORM = 1e-05
EPS_ADAM = 1e-08
THETA = 1000000.0
BETA = 0.5
LEARN = 0.05
LEARN_GAIN = 0.2
DECAY = 0.1
NEG_BIG = -1e30

X = "x"
Y = ("yh", "yl")
OFFSETS = (0, -1, 1, 2)
LOW = jnp.bfloat16
F32 = jnp.float32

HEADS = 4
QW = 320
KW = 80
FW = 896
ATTN = 896
GU = 2 * FW
WIDE = ATTN + 3 * FW
WIDE_CUT = 1792
MAP = (
    (0, 320, QW),
    (640, 640, KW),
    (800, 720, KW),
    (960, 1792, FW),
    (2752, 2688, FW),
    (4544, 0, QW),
    (5184, 896, FW),
)
PIECES = 8
BLK = 4 * HALF
LANES = 512
VMEM = 60 * 1024 * 1024


def dot(left, right, left_axis, right_axis):
    return lax.dot_general(
        left, right, (((left_axis,), (right_axis,)), ((), ())), preferred_element_type=F32
    )


def move(block, axis, distance):
    route = [(i, (i + distance) % RING) for i in range(RING)]
    return lax.ppermute(block, axis, route)


def swap_core(block):
    return lax.ppermute(block, "core", [(0, 1), (1, 0)])


def swap_sequences(block):
    return lax.ppermute(block, ("core", "yl"), [(0, 0), (1, 2), (2, 1), (3, 3)])


def near(block, axis):
    return move(block, axis, 1), move(block, axis, -1)


def far(back, ahead, axis):
    return move(back, axis, 1), move(ahead, axis, -1)


def halves(back, ahead, axis, cut):
    return far(back[:, :cut], ahead[:, cut:], axis)


def slot_ids(x, y):
    offsets = jnp.array(OFFSETS, jnp.int32)
    every = jnp.arange(RING, dtype=jnp.int32)
    rows = jnp.arange(HALF, dtype=jnp.int32)

    def slots(xx, yy, core):
        return (((yy // 2) * RING + xx) * 2 + core) * CAP + (yy % 2) * HALF

    first = slots(((x + offsets) % RING)[None, :, None], every[:, None, None], 0) + rows
    second = slots(every[:, None, None], ((y + offsets) % RING)[None, :, None], 1) + rows
    ids = jnp.concatenate([first, second], axis=0).reshape(PIECES, 1, BLK)
    return jnp.pad(ids, ((0, 0), (0, 0), (0, LANES - BLK)), constant_values=-1)


def three_parts(values):
    high = lax.reduce_precision(values, 8, 7)
    rest = values - high
    middle = lax.reduce_precision(rest, 8, 7)
    return jnp.concatenate([high, middle, rest - middle], axis=0).astype(LOW)


def whole():
    return pl.BlockSpec(memory_space=pltpu.VMEM)


def hbm():
    return pl.BlockSpec(memory_space=pl.ANY)


def smem():
    return pl.BlockSpec(memory_space=pltpu.SMEM)


def cost(flops, size):
    return pl.CostEstimate(flops=flops, bytes_accessed=size, transcendentals=0)


def pack_kernel(meta_ref, master_ref, own_ref, send_ref):
    is_low = meta_ref[0] == 0
    valid = lax.broadcasted_iota(jnp.int32, (HALF, 1), 0) < meta_ref[4]
    blank = jnp.zeros((HALF, ATTN - 800), LOW)
    own_ref[:, 800:ATTN] = blank
    send_ref[:, 800:ATTN] = blank
    for start, at, width in MAP:
        low = jnp.where(valid, master_ref[:, start : start + width], 0.0)
        high = jnp.where(valid, master_ref[:, start + width : start + 2 * width], 0.0)
        own_ref[:, at : at + width] = jnp.where(is_low, low, high).astype(LOW)
        send_ref[:, at : at + width] = jnp.where(is_low, high, low).astype(LOW)


def pack(meta, master):
    return pl.pallas_call(
        pack_kernel,
        in_specs=[smem(), whole()],
        out_specs=[whole()] * 2,
        out_shape=[jax.ShapeDtypeStruct((HALF, WIDE), LOW)] * 2,
        compiler_params=pltpu.CompilerParams(vmem_limit_bytes=VMEM),
        name="pack",
    )(meta, master)


def assemble_kernel(*refs):
    for kind in range(2):
        out = refs[8 + kind]
        for k, ref in enumerate(refs[4 * kind : 4 * kind + 4]):
            out[k * HALF : (k + 1) * HALF, :] = ref[...]


def assemble(blocks, groups):
    outs = []
    for j in groups:
        args = []
        specs = []
        for kind in range(2):
            block, back, ahead, one, two = blocks[5 * kind : 5 * kind + 5]
            args += [block, back, ahead, one if j < 2 else two]
            specs += [pl.BlockSpec((HALF, FW), lambda i, j=j: (0, j))] * 3
            specs += [pl.BlockSpec((HALF, FW), lambda i, j=j: (0, j % 2))]
        outs.append(
            pl.pallas_call(
                assemble_kernel,
                grid=(1,),
                in_specs=specs,
                out_specs=[pl.BlockSpec((BLK, FW), lambda i: (0, 0))] * 2,
                out_shape=[jax.ShapeDtypeStruct((BLK, FW), LOW)] * 2,
                compiler_params=pltpu.CompilerParams(vmem_limit_bytes=VMEM),
                cost_estimate=cost(0, 0),
                name="assemble",
            )(*args)
        )
    return outs


def place_kernel(
    meta_ref, slot_ref, ids_ref, swapped_ref, gains_ref, parts_ref, xc_ref, in_ref, cot_ref, gain_ref, rows
):
    @pl.when(pl.program_id(0) == 0)
    def _():
        at = pl.multiple_of(meta_ref[1] * 32, 32)
        tokens = swapped_ref[:128].astype(F32)
        scale = lax.rsqrt(jnp.sum(tokens * tokens, axis=1, keepdims=True) / D + EPS_NORM)
        rows[:128] = (tokens * scale * gains_ref[0:1]).astype(LOW)
        rows[128:256] = swapped_ref[128:256]
        rows[256:288] = swapped_ref[pl.ds(at, 32)]
        rows[288:320] = swapped_ref[pl.ds(128 + at, 32)]
        rows[320:] = parts_ref[...]

    place = jnp.where(slot_ref[...] == ids_ref[0], 1.0, 0.0).astype(LOW)
    placed = dot(rows[...], place, 1, 0)
    xc_ref[0] = placed[:256].astype(LOW)
    in_ref[0] = placed[256:288]
    cot_ref[0] = placed[288:320]
    gain_ref[0] = placed[320:322] + placed[322:324] + placed[324:326]


def to_slots(meta, slot, ids, swapped, gains, parts):
    def piece(rows):
        return pl.BlockSpec((1, rows, LANES), lambda p: (p, 0, 0))

    def same(shape):
        return pl.BlockSpec(shape, lambda p: (0, 0))

    return pl.pallas_call(
        place_kernel,
        grid=(PIECES,),
        in_specs=[
            smem(),
            same((D, 1)),
            pl.BlockSpec((1, 1, LANES), lambda p: (p, 0, 0)),
            same(swapped.shape),
            same((2, D)),
            same((16, D)),
        ],
        out_specs=[piece(256), piece(32), piece(32), piece(2)],
        out_shape=[
            jax.ShapeDtypeStruct((PIECES, 256, LANES), LOW),
            jax.ShapeDtypeStruct((PIECES, 32, LANES), F32),
            jax.ShapeDtypeStruct((PIECES, 32, LANES), F32),
            jax.ShapeDtypeStruct((PIECES, 2, LANES), F32),
        ],
        scratch_shapes=[pltpu.VMEM((336, D), LOW)],
        compiler_params=pltpu.CompilerParams(vmem_limit_bytes=VMEM),
        cost_estimate=cost(0, 0),
        name="to_slots",
    )(meta, slot, ids, swapped, gains, parts)


def unplace_kernel(slot_ref, ids_ref, rows_ref, out_ref, acc):
    place = jnp.where(ids_ref[0] == slot_ref[...], 1.0, 0.0).astype(LOW)

    @pl.when(pl.program_id(0) == 0)
    def _():
        acc[...] = jnp.zeros_like(acc)

    acc[...] += dot(rows_ref[0], place, 1, 0)

    @pl.when(pl.program_id(0) == PIECES - 1)
    def _():
        out_ref[...] = acc[...].astype(LOW)


def from_slots(rows, slot, ids):
    n = rows.shape[1]
    return pl.pallas_call(
        unplace_kernel,
        grid=(PIECES,),
        in_specs=[
            pl.BlockSpec((1, D), lambda p: (0, 0)),
            pl.BlockSpec((1, LANES, 1), lambda p: (p, 0, 0)),
            pl.BlockSpec((1, n, LANES), lambda p: (p, 0, 0)),
        ],
        out_specs=pl.BlockSpec((n, D), lambda p: (0, 0)),
        out_shape=jax.ShapeDtypeStruct((n, D), LOW),
        scratch_shapes=[pltpu.VMEM((n, D), F32)],
        compiler_params=pltpu.CompilerParams(vmem_limit_bytes=VMEM),
        cost_estimate=cost(0, 0),
        name="from_slots",
    )(slot, ids, rows)


def start_weights(meta_ref, refs, held, sems):
    x = meta_ref[2]
    y = meta_ref[3]
    for base, at, group in ((0, y, refs[:4]), (RING, x, refs[4:])):
        for ref, offset in zip(group, OFFSETS):
            p = base + lax.rem(at + offset + RING, RING)
            pltpu.make_async_copy(ref, held.at[p], sems.at[p]).start()


def wait_weights(held, sems, p):
    pltpu.make_async_copy(held.at[p], held.at[p], sems.at[p]).wait()


def split_rows(value, scratch, core, p, keep_ref, send_ref):
    scratch[:, :BLK] = value
    for z in range(RING):
        keep_ref[z, p] = scratch[pl.ds(pl.multiple_of(core * 128 + 32 * z, 32), 32), :]
        send_ref[z, p] = scratch[pl.ds(pl.multiple_of((1 - core) * 128 + 32 * z, 32), 32), :].astype(
            LOW
        )


def join_rows(is_low, own, got):
    return jnp.concatenate(
        [jnp.where(is_low, own, got), jnp.where(is_low, got, own)], axis=0
    )


def rope(values, cosine, sine):
    half = HD // 2
    turned = jnp.concatenate([-values[:, half:], values[:, :half]], axis=1)
    return values * cosine + turned * sine


def head_probs(query, keys, mask):
    scores = dot(query, keys, 1, 1) * HD ** (-0.5)
    scores = jnp.where(mask, scores, NEG_BIG)
    weight = jnp.exp(scores - jnp.max(scores, axis=1, keepdims=True))
    return weight / jnp.sum(weight, axis=1, keepdims=True)


def causal_mask(seg_col, seg_row):
    rows = lax.broadcasted_iota(jnp.int32, (SEQ, SEQ), 0)
    cols = lax.broadcasted_iota(jnp.int32, (SEQ, SEQ), 1)
    return (seg_col == seg_row) & (cols <= rows)


def attention_kernel(
    meta_ref, own_ref, got_ref, cos_ref, sin_ref, segc_ref, segr_ref, *rest
):
    w_refs = rest[:8]
    q_ref, k_ref, v_ref, o_ref, keep_ref, send_ref, held, acc, part, sems = rest[8:]
    core = meta_ref[0]
    is_low = core == 0
    start_weights(meta_ref, w_refs, held, sems)
    acc[...] = jnp.zeros_like(acc)
    part[:, BLK:] = jnp.zeros((SEQ, LANES - BLK), F32)

    def project(p, carry):
        wait_weights(held, sems, p)
        rows = join_rows(is_low, own_ref[p, :128], got_ref[p, :128])
        acc[...] += dot(rows[:, :BLK], held[p, :, 256:], 1, 0)
        return carry

    lax.fori_loop(0, PIECES, project, 0)
    cosine = cos_ref[...]
    sine = sin_ref[...]
    mask = causal_mask(segc_ref[...], segr_ref[...])
    projected = acc[...]
    keys = rope(projected[:, 384:464], cosine, sine).astype(LOW)
    values = projected[:, 464:544].astype(LOW)
    k_ref[...] = keys
    v_ref[...] = values
    outs = []
    for h in range(HEADS):
        query = rope(projected[:, 64 + h * HD : 64 + (h + 1) * HD], cosine, sine).astype(LOW)
        q_ref[h] = query
        probs = head_probs(query, keys, mask)
        outs.append(dot(probs.astype(LOW), values, 1, 0))
    outs.append(jnp.zeros((SEQ, 64), F32))
    attended = jnp.concatenate(outs, axis=1).astype(LOW)
    o_ref[...] = attended

    def spread(p, carry):
        split_rows(dot(attended, held[p, :, :384], 1, 1), part, core, p, keep_ref, send_ref)
        return carry

    lax.fori_loop(0, PIECES, spread, 0)


def split_shapes():
    return [
        jax.ShapeDtypeStruct((RING, PIECES, 32, LANES), F32),
        jax.ShapeDtypeStruct((RING, PIECES, 32, LANES), LOW),
    ]


def attention_forward(meta, own, got, tables, segs, w_attn):
    return pl.pallas_call(
        attention_kernel,
        in_specs=[smem()] + [whole()] * 6 + [hbm()] * 8,
        out_specs=[whole()] * 6,
        out_shape=[
            jax.ShapeDtypeStruct((HEADS, SEQ, HD), LOW),
            jax.ShapeDtypeStruct((SEQ, HD), LOW),
            jax.ShapeDtypeStruct((SEQ, HD), LOW),
            jax.ShapeDtypeStruct((SEQ, 384), LOW),
        ]
        + split_shapes(),
        scratch_shapes=[
            pltpu.VMEM((PIECES, BLK, ATTN), LOW),
            pltpu.VMEM((SEQ, ATTN - 256), F32),
            pltpu.VMEM((SEQ, LANES), F32),
            pltpu.SemaphoreType.DMA((PIECES,)),
        ],
        compiler_params=pltpu.CompilerParams(vmem_limit_bytes=VMEM),
        cost_estimate=cost(0, 0),
        name="attention_forward",
    )(meta, own, got, *tables, *segs, *w_attn)


def put_blocks(ref, value):
    for k in range(RING):
        ref[k] = value[k * HALF : (k + 1) * HALF].astype(LOW)


def attention_back_kernel(
    meta_ref, own_ref, got_ref, cos_ref, sin_ref, segc_ref, segr_ref, q_ref, k_ref, v_ref, o_ref, xc_ref, xc_got_ref, *rest
):
    w_refs = rest[:8]
    keep_ref, send_ref = rest[8:10]
    outs = rest[10:18]
    held, acc, part, sems = rest[18:]
    core = meta_ref[0]
    is_low = core == 0
    start_weights(meta_ref, w_refs, held, sems)
    acc[...] = jnp.zeros_like(acc)
    part[:, BLK:] = jnp.zeros((SEQ, LANES - BLK), F32)

    def project(p, carry):
        wait_weights(held, sems, p)
        own = jnp.concatenate([own_ref[z, p] for z in range(RING)], axis=0)
        got = jnp.concatenate([got_ref[z, p] for z in range(RING)], axis=0)
        acc[...] += dot(join_rows(is_low, own, got)[:, :BLK], held[p, :, :384], 1, 0)
        return carry

    lax.fori_loop(0, PIECES, project, 0)
    cosine = cos_ref[...]
    sine = -sin_ref[...]
    mask = causal_mask(segc_ref[...], segr_ref[...])
    grad_att = acc[...]
    keys = k_ref[...]
    values = v_ref[...]
    factor = HD ** (-0.5)
    grads = []
    grad_keys = jnp.zeros((SEQ, HD), F32)
    grad_values = jnp.zeros((SEQ, HD), F32)
    for h in range(HEADS):
        query = q_ref[h]
        grad_o = grad_att[:, h * HD : (h + 1) * HD].astype(LOW)
        probs = head_probs(query, keys, mask)
        grad_probs = dot(grad_o, values, 1, 1)
        inner = jnp.sum(probs * grad_probs, axis=1, keepdims=True)
        grad_scores = (probs * (grad_probs - inner)).astype(LOW)
        grads.append(rope(dot(grad_scores, keys, 1, 0) * factor, cosine, sine))
        grad_keys += dot(grad_scores, query, 0, 0)
        grad_values += dot(probs.astype(LOW), grad_o, 0, 0)
    grads.append(rope(grad_keys * factor, cosine, sine))
    grads.append(grad_values)
    zeros = [jnp.zeros((SEQ, 64), F32)]
    ends = [jnp.zeros((SEQ, 96), F32)]
    grad_qkv = jnp.concatenate(zeros + grads + ends, axis=1).astype(LOW)

    def spread(p, carry):
        split_rows(dot(grad_qkv, held[p, :, 256:], 1, 1), part, core, p, keep_ref, send_ref)
        return carry

    lax.fori_loop(0, PIECES, spread, 0)

    for kind in range(2):
        for k in range(RING):
            q = kind * RING + lax.rem(meta_ref[3 - kind] + OFFSETS[k] + RING, RING)
            own = jnp.concatenate([own_ref[z, q] for z in range(RING)], axis=0)
            got = jnp.concatenate([got_ref[z, q] for z in range(RING)], axis=0)
            grad = join_rows(is_low, own, got)[:, :BLK]
            xn = join_rows(is_low, xc_ref[q, :128], xc_got_ref[q, :128])[:, :BLK]
            one = dot(grad, o_ref[...], 0, 0)
            two = dot(xn, grad_qkv, 0, 0)
            terms = jnp.concatenate([one[:, :QW], two[:, 64:]], axis=1)
            put_blocks(outs[RING * kind + k], terms)


def attention_backward(meta, own, got, tables, segs, qkvo, xcs, w_attn):
    return pl.pallas_call(
        attention_back_kernel,
        in_specs=[smem()] + [whole()] * 12 + [hbm()] * 8,
        out_specs=[whole()] * 10,
        out_shape=split_shapes() + [jax.ShapeDtypeStruct((RING, HALF, ATTN), LOW)] * 8,
        scratch_shapes=[
            pltpu.VMEM((PIECES, BLK, ATTN), LOW),
            pltpu.VMEM((SEQ, 384), F32),
            pltpu.VMEM((SEQ, LANES), F32),
            pltpu.SemaphoreType.DMA((PIECES,)),
        ],
        compiler_params=pltpu.CompilerParams(vmem_limit_bytes=VMEM),
        cost_estimate=cost(0, 0),
        name="attention_backward",
    )(meta, own, got, *tables, *segs, *qkvo, *xcs, *w_attn)


def down_back_kernel(meta_ref, cot_own_ref, cot_got_ref, *rest):
    w_refs = rest[:8]
    out_ref, held, sems = rest[8:]
    is_low = meta_ref[0] == 0
    start_weights(meta_ref, w_refs, held, sems)
    out_ref[...] = jnp.zeros_like(out_ref)

    def project(p, carry):
        wait_weights(held, sems, p)
        cot = join_rows(is_low, cot_own_ref[p, 128:], cot_got_ref[p, 128:])
        out_ref[...] += dot(cot[:, :BLK], held[p], 1, 0)
        return carry

    lax.fori_loop(0, PIECES, project, 0)


def down_back(meta, cot_own, cot_got, w_down):
    return pl.pallas_call(
        down_back_kernel,
        in_specs=[smem()] + [whole()] * 2 + [hbm()] * 8,
        out_specs=whole(),
        out_shape=jax.ShapeDtypeStruct((SEQ, FW), F32),
        scratch_shapes=[
            pltpu.VMEM((PIECES, BLK, FW), LOW),
            pltpu.SemaphoreType.DMA((PIECES,)),
        ],
        compiler_params=pltpu.CompilerParams(vmem_limit_bytes=VMEM),
        cost_estimate=cost(0, 0),
        name="down_backward",
    )(meta, cot_own, cot_got, *w_down)


def down_kernel(meta_ref, act_ref, *rest):
    w_refs = rest[:8]
    keep_ref, send_ref, held, part, sems = rest[8:]
    core = meta_ref[0]
    start_weights(meta_ref, w_refs, held, sems)
    part[:, BLK:] = jnp.zeros((SEQ, LANES - BLK), F32)

    def spread(p, carry):
        wait_weights(held, sems, p)
        split_rows(dot(act_ref[...], held[p], 1, 1), part, core, p, keep_ref, send_ref)
        return carry

    lax.fori_loop(0, PIECES, spread, 0)


def down_forward(meta, act, w_down):
    return pl.pallas_call(
        down_kernel,
        in_specs=[smem(), whole()] + [hbm()] * 8,
        out_specs=[whole()] * 2,
        out_shape=split_shapes(),
        scratch_shapes=[
            pltpu.VMEM((PIECES, BLK, FW), LOW),
            pltpu.VMEM((SEQ, LANES), F32),
            pltpu.SemaphoreType.DMA((PIECES,)),
        ],
        compiler_params=pltpu.CompilerParams(vmem_limit_bytes=VMEM),
        cost_estimate=cost(0, 0),
        name="down_forward",
    )(meta, act, *w_down)


def start_ffn(meta_ref, refs, held, sems):
    x = meta_ref[2]
    y = meta_ref[3]
    for base, at, group in ((0, y, refs[:8]), (RING, x, refs[8:])):
        for k, offset in enumerate(OFFSETS):
            p = base + lax.rem(at + offset + RING, RING)
            for j in range(2):
                into = held.at[p, :, pl.ds(j * FW, FW)]
                pltpu.make_async_copy(group[2 * k + j], into, sems.at[p]).start()


def ffn_kernel(meta_ref, own_ref, got_ref, grad_act_ref, *rest):
    w_refs = rest[:16]
    act_ref, grad_ref, keep_ref, send_ref, held, acc, part, sems = rest[16:]
    core = meta_ref[0]
    is_low = core == 0
    start_ffn(meta_ref, w_refs, held, sems)
    acc[...] = jnp.zeros_like(acc)
    part[:, BLK:] = jnp.zeros((SEQ, LANES - BLK), F32)

    def project(p, carry):
        wait_weights(held, sems, p)
        own = jnp.concatenate([own_ref[z, p] for z in range(RING)], axis=0)
        got = jnp.concatenate([got_ref[z, p] for z in range(RING)], axis=0)
        acc[...] += dot(join_rows(is_low, own, got)[:, :BLK], held[p], 1, 0)
        return carry

    lax.fori_loop(0, PIECES, project, 0)

    def units(t, carry):
        at = pl.multiple_of(t * 128, 128)
        grad_act = grad_act_ref[:, pl.ds(at, 128)]
        gate = acc[:, pl.ds(at, 128)]
        up = acc[:, pl.ds(at + FW, 128)]
        sigmoid = 1.0 / (1.0 + jnp.exp(-gate))
        silu = gate * sigmoid
        act_ref[:, pl.ds(at, 128)] = (silu * up).astype(LOW)
        grad_gate = grad_act * up * sigmoid * (1.0 + gate * (1.0 - sigmoid))
        grad_ref[:, pl.ds(at, 128)] = grad_gate.astype(LOW)
        grad_ref[:, pl.ds(at + FW, 128)] = (grad_act * silu).astype(LOW)
        return carry

    lax.fori_loop(0, FW // 128, units, 0)

    def spread(p, carry):
        split_rows(dot(grad_ref[...], held[p], 1, 1), part, core, p, keep_ref, send_ref)
        return carry

    lax.fori_loop(0, PIECES, spread, 0)


def feed_forward(meta, own, got, grad_act, w_gu):
    return pl.pallas_call(
        ffn_kernel,
        in_specs=[smem()] + [whole()] * 3 + [hbm()] * 16,
        out_specs=[whole()] * 4,
        out_shape=[
            jax.ShapeDtypeStruct((SEQ, FW), LOW),
            jax.ShapeDtypeStruct((SEQ, GU), LOW),
        ]
        + split_shapes(),
        scratch_shapes=[
            pltpu.VMEM((PIECES, BLK, GU), LOW),
            pltpu.VMEM((SEQ, GU), F32),
            pltpu.VMEM((SEQ, LANES), F32),
            pltpu.SemaphoreType.DMA((PIECES,)),
        ],
        compiler_params=pltpu.CompilerParams(vmem_limit_bytes=VMEM),
        cost_estimate=cost(0, 0),
        name="feed_forward",
    )(meta, own, got, grad_act, *w_gu)


def halves_of(part_ref, xc_ref, q, at):
    rows = jnp.concatenate([part_ref[z, q] for z in range(RING)], axis=0)
    return rows[:, :BLK], xc_ref[q, at : at + 128][:, :BLK]


def merge_kernel(part_ref, xc_ref, one_ref, two_ref):
    for p in range(RING):
        for ref, q in ((one_ref, p), (two_ref, RING + p)):
            for z in range(RING):
                ref[p, 32 * z : 32 * z + 32] = part_ref[z, q]
            ref[p, 128:] = xc_ref[q]


def merge(part, xc):
    return pl.pallas_call(
        merge_kernel,
        grid=(1,),
        in_specs=[
            pl.BlockSpec(part.shape, lambda i: (0, 0, 0, 0)),
            pl.BlockSpec((PIECES, 128, LANES), lambda i: (0, 1, 0)),
        ],
        out_specs=[pl.BlockSpec((RING, 256, LANES), lambda i: (0, 0, 0))] * 2,
        out_shape=[jax.ShapeDtypeStruct((RING, 256, LANES), LOW)] * 2,
        compiler_params=pltpu.CompilerParams(vmem_limit_bytes=VMEM),
        cost_estimate=cost(0, 0),
        name="merge",
    )(part, xc)


def ffn_terms_kernel(meta_ref, own_ref, got_ref, *rest, axis):
    rights = rest[:8]
    outs = rest[8:12]
    acc = rest[12]
    is_low = meta_ref[0] == 0
    at = meta_ref[axis]
    for k, offset in enumerate(OFFSETS):
        source = lax.rem(at + offset + RING, RING)
        xn = join_rows(is_low, own_ref[source, :128], got_ref[source, :128])[:, :BLK]
        cot = join_rows(is_low, own_ref[source, 128:], got_ref[source, 128:])[:, :BLK]
        down = dot(cot, rights[2 * k][...], 0, 0)
        both = dot(xn, rights[2 * k + 1][...], 0, 0)
        if k == 0:
            acc[:, :FW] = down
            acc[:, FW:] = both
        else:
            acc[:, :FW] += down
            acc[:, FW:] += both
    for k, ref in enumerate(outs):
        ref[:, ATTN:] = acc[k * HALF : (k + 1) * HALF, :].astype(LOW)


def ffn_terms(meta, own, got, rights, axis):
    return pl.pallas_call(
        functools.partial(ffn_terms_kernel, axis=axis),
        in_specs=[smem()] + [whole()] * 10,
        out_specs=[whole()] * 4,
        out_shape=[jax.ShapeDtypeStruct((HALF, WIDE), LOW)] * 4,
        scratch_shapes=[pltpu.VMEM((BLK, 3 * FW), F32)],
        compiler_params=pltpu.CompilerParams(vmem_limit_bytes=VMEM),
        cost_estimate=cost(0, 0),
        name="terms_feed_forward",
    )(meta, own, got, *rights)


def fill_kernel(*refs):
    for kind in range(2):
        parts = refs[4 * kind : 4 * kind + 4]
        outs = refs[16 + 4 * kind : 20 + 4 * kind]
        for k, ref in enumerate(outs):
            total = parts[0][k].astype(F32)
            for part in parts[1:]:
                total = total + part[k].astype(F32)
            ref[...] = total.astype(LOW)


def fill(attn, ffn):
    args = [*attn[0], *attn[1], *ffn[0], *ffn[1]]
    outs = pl.pallas_call(
        fill_kernel,
        grid=(1,),
        in_specs=[pl.BlockSpec((RING, HALF, ATTN), lambda i: (0, 0, 0))] * 8 + [hbm()] * 8,
        out_specs=[pl.BlockSpec((HALF, ATTN), lambda i: (0, 0))] * 8,
        out_shape=[jax.ShapeDtypeStruct(a.shape, LOW) for a in args[8:]],
        input_output_aliases={8 + k: k for k in range(8)},
        compiler_params=pltpu.CompilerParams(vmem_limit_bytes=VMEM),
        cost_estimate=cost(0, 0),
        name="fill",
    )(*args)
    return outs[:4], outs[4:]


def finish_kernel(meta_ref, *refs):
    is_low = meta_ref[0] == 0
    sums = []
    for kind in range(2):
        total = refs[4 * kind][...].astype(F32)
        for ref in refs[4 * kind + 1 : 4 * kind + 4]:
            total = total + ref[...].astype(F32)
        sums.append(total)
    stay_ref, send_ref = refs[8:]
    stay_ref[...] = jnp.where(is_low, sums[0], sums[1])
    send_ref[...] = jnp.where(is_low, sums[1], sums[0]).astype(LOW)


def finish(meta, parts):
    return pl.pallas_call(
        finish_kernel,
        in_specs=[smem()] + [whole()] * 8,
        out_specs=[whole()] * 2,
        out_shape=[
            jax.ShapeDtypeStruct((HALF, WIDE), F32),
            jax.ShapeDtypeStruct((HALF, WIDE), LOW),
        ],
        compiler_params=pltpu.CompilerParams(vmem_limit_bytes=VMEM),
        cost_estimate=cost(0, 0),
        name="finish",
    )(meta, *parts[0], *parts[1])


def adam_kernel(meta_ref, w_ref, m_ref, v_ref, stay, came, wo_ref, mo_ref, vo_ref, grad):
    is_low = meta_ref[0] == 0
    rows = w_ref.shape[0]
    for start, at, width in MAP:
        mine = stay[:, at : at + width]
        other = came[:, at : at + width].astype(F32)
        grad[:, start : start + width] = jnp.where(is_low, mine, other)
        grad[:, start + width : start + 2 * width] = jnp.where(is_low, other, mine)
    row = pl.program_id(0) * rows + lax.broadcasted_iota(jnp.int32, (rows, 1), 0)
    valid = row < meta_ref[4]
    weight, first, second = adam_step(
        w_ref[...], m_ref[...], v_ref[...], grad[...], LEARN, DECAY
    )
    wo_ref[...] = jnp.where(valid, weight, 0.0)
    mo_ref[...] = jnp.where(valid, first, 0.0)
    vo_ref[...] = jnp.where(valid, second, 0.0)


def adam(meta, master, moment_one, moment_two, stay, came):
    rows = 32
    units = master.shape[1]

    def block(width):
        return pl.BlockSpec((rows, width), lambda i: (i, 0))

    return pl.pallas_call(
        adam_kernel,
        grid=(pl.cdiv(HALF, rows),),
        in_specs=[smem()] + [block(units)] * 3 + [block(WIDE)] * 2,
        out_specs=[block(units)] * 3,
        out_shape=[jax.ShapeDtypeStruct(master.shape, F32)] * 3,
        scratch_shapes=[pltpu.VMEM((rows, units), F32)],
        compiler_params=pltpu.CompilerParams(vmem_limit_bytes=VMEM),
        name="adam",
    )(meta, master, moment_one, moment_two, stay, came)


def rms_scale(values):
    return lax.rsqrt(jnp.sum(values * values, axis=(0, 2), keepdims=True) / D + EPS_NORM)


def rms_backward(grad_out, normed, scale, gain):
    grad_normed = grad_out * gain
    inner = jnp.sum(grad_normed * normed, axis=(0, 2), keepdims=True) / D
    return scale * (grad_normed - normed * inner), jnp.sum(grad_out * normed, axis=1)


def adam_step(weight, first, second, grad, rate, decay):
    first_new = BETA * first + (1.0 - BETA) * grad
    second_new = BETA * second + (1.0 - BETA) * grad * grad
    inverse = 1.0 / (1.0 - BETA**STEP)
    update = (first_new * inverse) / (jnp.sqrt(second_new * inverse) + EPS_ADAM)
    return (weight - rate * (update + decay * weight), first_new, second_new)


def stage(*values):
    return lax.optimization_barrier(values)


def shards(
    tokens, cotangent, segments, owner, master, moment_one, moment_two, gains, gain_one, gain_two
):
    core = lax.axis_index("core")
    yl = lax.axis_index("yl")
    z = lax.axis_index("z")
    x = lax.axis_index(X)
    y = lax.axis_index("yh") * 2 + yl
    count = jnp.sum((owner == (y // 2 * RING + x) * 2 + core).astype(jnp.int32)) - yl * HALF
    meta = jnp.stack([core, z, x, y, count]).astype(jnp.int32)
    along = (Y, X)
    across = (X, Y)

    def add_core(keep, other):
        return (keep + other.astype(F32)).astype(LOW)

    def split_z(block):
        return lax.all_to_all(block, "z", split_axis=0, concat_axis=0, tiled=True)

    def sum_z(block):
        return jnp.sum(block.astype(F32), axis=0)

    def all_z(block):
        return split_z(jnp.broadcast_to(block[None], (RING, *block.shape)))

    own, send = pack(meta, master)
    got = swap_core(send)
    first = jnp.where(core == 0, own, got)
    second = jnp.where(core == 0, got, own)
    first, second, owner, tokens = stage(first, second, owner, tokens)

    near_first = near(first, X)
    near_second = near(second, Y)
    numbers = jnp.zeros((8, D), LOW).at[0, :SEQ].set(segments.astype(LOW))
    swapped = swap_sequences(jnp.concatenate([tokens, cotangent, numbers], axis=0))
    onehot = (owner[:, None] == jnp.arange(16, dtype=jnp.int32)[None, :]).astype(jnp.int32)
    rank = jnp.sum((jnp.cumsum(onehot, axis=0) - onehot) * onehot, axis=1)
    slot = (owner * CAP + rank)[:, None]
    ids = slot_ids(x, y)
    parts = jnp.concatenate([three_parts(gains), jnp.zeros((10, D), LOW)], axis=0)
    near_first, near_second, slot, ids, parts, swapped = stage(
        near_first, near_second, slot, ids, parts, swapped
    )

    segment = swapped[256, :SEQ].astype(jnp.int32)
    segs = (segment[:, None], segment[None, :])
    far_first = halves(*near_first, X, WIDE_CUT)
    far_second = halves(*near_second, Y, WIDE_CUT)
    far_first, far_second = stage(far_first, far_second)
    blocks = (first, *near_first, *far_first, second, *near_second, *far_second)
    (attn,) = assemble(blocks, (0,))

    attn_near = [near(b, axis) for b, axis in zip(attn, along)]
    position = jnp.arange(SEQ, dtype=F32)
    freq = jnp.exp(-jnp.log(THETA) * (2.0 * jnp.arange(HD // 2, dtype=F32) / HD))
    angle = position[:, None] * freq[None, :]
    tables = (
        jnp.concatenate([jnp.cos(angle)] * 2, axis=1),
        jnp.concatenate([jnp.sin(angle)] * 2, axis=1),
    )
    xc_own, inputs, cot_z, gain = to_slots(meta, slot, ids, swapped, gains, parts)
    (down,) = assemble(blocks, (1,))
    attn_near, tables, down, xc_own, inputs, cot_z, gain = stage(
        attn_near, tables, down, xc_own, inputs, cot_z, gain
    )
    down_near = [near(b, axis) for b, axis in zip(down, along)]
    xc_got = swap_core(xc_own)
    (gate,) = assemble(blocks, (2,))
    turned = (slot.reshape(1, D), ids.reshape(PIECES, LANES, 1))
    down_near, xc_got, blocks, gate, turned = stage(down_near, xc_got, blocks, gate, turned)
    pair_far = [far(q[0], d[1], axis) for q, d, axis in zip(attn_near, down_near, along)]
    (up,) = assemble(blocks, (3,))
    pair_far, gate, up = stage(pair_far, gate, up)
    w_attn = []
    w_down = []
    for kind in range(2):
        w_attn += [attn[kind], *attn_near[kind], pair_far[kind][0]]
        w_down += [down[kind], *down_near[kind], pair_far[kind][1]]

    gate_near = [near(b, axis) for b, axis in zip(gate, along)]
    *qkv, attended, keep, send = attention_forward(meta, xc_own, xc_got, tables, segs, w_attn)
    gate_near, up, keep, send = stage(gate_near, up, keep, send)
    up_near = [near(b, axis) for b, axis in zip(up, along)]
    got = split_z(add_core(keep, swap_core(send)))
    grad_act = down_back(meta, xc_own, xc_got, w_down)
    up_near, gate_near, got, grad_act = stage(up_near, gate_near, got, grad_act)
    gu_far = [far(g[0], u[1], axis) for g, u, axis in zip(gate_near, up_near, along)]
    hidden = inputs + sum_z(got)
    scale_two = rms_scale(hidden)
    normed_two = hidden * scale_two
    xn_two = all_z((normed_two * gain[:, 1:2]).astype(LOW))
    gu_far, xn_two = stage(gu_far, xn_two)
    xn_two_got = swap_core(xn_two)
    left_sent = merge(xn_two, xc_own)
    xn_two, xn_two_got, grad_act, left_sent = stage(xn_two, xn_two_got, grad_act, left_sent)
    w_gu = []
    for kind in range(2):
        w_gu += [gate[kind], up[kind]]
        w_gu += [gate_near[kind][0], up_near[kind][0], gate_near[kind][1], up_near[kind][1]]
        w_gu += [*gu_far[kind]]

    act, grad_gu, keep, send = feed_forward(meta, xn_two, xn_two_got, grad_act, w_gu)
    def exchange(block, axis):
        return lax.all_to_all(block, axis, split_axis=0, concat_axis=0, tiled=True)

    lefts = [exchange(left_sent[0], Y)]
    act, grad_gu, keep, send, lefts = stage(act, grad_gu, keep, send, lefts)
    gu_near = [near(grad_gu, axis) for axis in along]
    got = split_z(add_core(keep, swap_core(send)))
    keep_mlp, send_mlp = down_forward(meta, act, w_down)
    gu_near, got, keep_mlp, send_mlp, act = stage(gu_near, got, keep_mlp, send_mlp, act)
    act_near = [near(act, axis) for axis in along]
    lefts_got = [swap_core(lefts[0])]
    mlp_both = add_core(keep_mlp, swap_core(send_mlp))
    grad_xn_two = sum_z(got)
    grad_norm_two, gain_grad_two = rms_backward(grad_xn_two, normed_two, scale_two, gain[:, 1:2])
    grad_hidden = cot_z + grad_norm_two
    grad_branch = all_z(grad_hidden.astype(LOW))
    act_near, grad_branch, grad_hidden, gain_grad_two, left_sent, lefts_got, gu_near, mlp_both = stage(
        act_near, grad_branch, grad_hidden, gain_grad_two, left_sent, lefts_got, gu_near, mlp_both
    )
    grad_branch_got = swap_core(grad_branch)
    ends = [far(a[0], g[1], axis) for a, g, axis in zip(act_near, gu_near, along)]
    lefts.append(exchange(left_sent[1], X))

    xcs = (xc_own, xc_got)
    keep, send, *terms = attention_backward(
        meta, grad_branch, grad_branch_got, tables, segs, (*qkv, attended), xcs, w_attn
    )
    attn_terms = (terms[:4], terms[4:])
    ends, keep, send, attn_terms, lefts, lefts_got, mlp_both = stage(
        ends, keep, send, attn_terms, lefts, lefts_got, mlp_both
    )
    lefts_got.append(swap_core(lefts[1]))
    both = add_core(keep, swap_core(send))
    ends, both, mlp_both, attn_terms, lefts, lefts_got = stage(
        ends, both, mlp_both, attn_terms, lefts, lefts_got
    )

    def direct(first, second, axes):
        _, back, ahead, last = first
        _, back_two, ahead_two, last_two = second
        one = (move(ahead, axes[0], 1), move(back, axes[0], -1), move(last, axes[0], 2))
        up = move(ahead_two, axes[1], 1)
        down = move(back_two, axes[1], -1)
        return one, up, down, last_two

    one, up, down, last_two = direct(*attn_terms, along)
    def rights_of(kind):
        rights = (act, grad_gu)
        for n in range(2):
            rights += (act_near[kind][n], gu_near[kind][n])
        return rights + tuple(ends[kind])

    got = split_z(both)
    ffn_sums = [ffn_terms(meta, lefts[0], lefts_got[0], rights_of(0), 3)]
    up, down, last_two, lefts, lefts_got, ffn_sums = stage(
        up, down, last_two, lefts, lefts_got, ffn_sums
    )
    attn_others = (one, (up, down, move(last_two, along[1], 2)))
    ffn_sums.append(ffn_terms(meta, lefts[1], lefts_got[1], rights_of(1), 2))
    grad_xn_one = sum_z(got)
    scale_one = rms_scale(inputs)
    grad_norm_one, gain_grad_one = rms_backward(
        grad_xn_one, inputs * scale_one, scale_one, gain[:, 0:1]
    )
    grad_tokens_z = (grad_hidden + grad_norm_one).astype(LOW)
    mlp = lax.psum_scatter(mlp_both, "z", scatter_dimension=0, tiled=True)[0]
    output_z = (hidden + mlp.astype(F32)).astype(LOW)
    gain_grads = three_parts(jnp.stack([gain_grad_one, gain_grad_two], axis=0))
    gain_grads = jnp.swapaxes(gain_grads, 0, 1)
    blank = jnp.zeros((PIECES, 10, LANES), LOW)
    last = from_slots(
        jnp.concatenate([output_z, grad_tokens_z, gain_grads, blank], axis=1), *turned
    )
    attn_others, ffn_sums, last = stage(attn_others, ffn_sums, last)
    blocks = fill([(t[0], *o) for t, o in zip(attn_terms, attn_others)], ffn_sums)
    part = lax.all_gather(last, "z", axis=0, tiled=False)
    one, up, down, last_two = direct(*blocks, across)
    up, down, last_two = stage(up, down, last_two)
    others = (one, (up, down, move(last_two, across[1], 2)))
    others, owns, part = stage(others, [b[0] for b in blocks], part)
    stay, send = finish(meta, [(b, *o) for b, o in zip(owns, others)])
    stay, send, part = stage(stay, send, part)
    came = swap_core(send)
    moved = swap_sequences(jnp.swapaxes(part[:, :64].reshape(RING, 2, 32, D), 0, 1))
    gain_grads = part[:, 64:70].astype(F32).sum(axis=0)
    gain_grads = gain_grads[:2] + gain_grads[2:4] + gain_grads[4:6]
    gain_other = swap_core(gain_grads)
    came, gain_other = stage(came, gain_other)

    def sum_along(value, axis):
        back, ahead = near(value, axis)
        return (value + move(value, axis, 2)) + (back + ahead)

    gain_grads = sum_along(gain_grads + gain_other, X)
    new_master, new_one, new_two = adam(meta, master, moment_one, moment_two, stay, came)
    gain_grads, new_master, moved = stage(gain_grads, new_master, moved)
    gain_grads = sum_along(gain_grads, Y)
    output = moved[0].reshape(128, D)
    grad_tokens = moved[1].reshape(128, D)
    new_gains, new_gain_one, new_gain_two = adam_step(
        gains, gain_one, gain_two, gain_grads, LEARN_GAIN, 0.0
    )
    return (
        output,
        grad_tokens,
        new_master,
        new_one,
        new_two,
        new_gains,
        new_gain_one,
        new_gain_two,
    )


def solution(mesh):
    fine = Mesh(mesh.devices.reshape(2, 4, 2, 2, 4), ("yh", "x", "core", "yl", "z"))
    rows = ("yh", "x", "core", "yl")
    in_specs = (
        P(rows, None),
        P(rows, None),
        P(("yh", "x", "core")),
        P(),
        P(rows, "z"),
        P(rows, "z"),
        P(rows, "z"),
        P(),
        P(),
        P(),
    )
    out_specs = (
        P(rows, None),
        P(rows, None),
        P(rows, "z"),
        P(rows, "z"),
        P(rows, "z"),
        P(),
        P(),
        P(),
    )
    return jax.shard_map(shards, mesh=fine, in_specs=in_specs, out_specs=out_specs, check_vma=False)
```

```python
import functools

import jax
import jax.numpy as jnp
from jax import lax
from jax.experimental import pallas as pl
from jax.experimental.pallas import tpu as pltpu
from jax.sharding import Mesh
from jax.sharding import PartitionSpec as P

HD = 80
STEP = 5
D = 2560
CAP = 240
HALF = 120
SEQ = 256
RING = 4

EPS_NORM = 1e-05
EPS_ADAM = 1e-08
THETA = 1000000.0
BETA = 0.5
LEARN = 0.05
LEARN_GAIN = 0.2
DECAY = 0.1
NEG_BIG = -1e30

X = "x"
Y = ("yh", "yl")
OFFSETS = (0, -1, 1, 2)
LOW = jnp.bfloat16
F32 = jnp.float32

HEADS = 4
QW = 320
KW = 80
FW = 896
ATTN = 896
GU = 2 * FW
WIDE = ATTN + 3 * FW
WIDE_CUT = 1792
MAP = (
    (0, 320, QW),
    (640, 640, KW),
    (800, 720, KW),
    (960, 1792, FW),
    (2752, 2688, FW),
    (4544, 0, QW),
    (5184, 896, FW),
)
PIECES = 8
BLK = 4 * HALF
LANES = 512
VMEM = 60 * 1024 * 1024


def dot(left, right, left_axis, right_axis):
    return lax.dot_general(
        left, right, (((left_axis,), (right_axis,)), ((), ())), preferred_element_type=F32
    )


def move(block, axis, distance):
    route = [(i, (i + distance) % RING) for i in range(RING)]
    return lax.ppermute(block, axis, route)


def swap_core(block):
    return lax.ppermute(block, "core", [(0, 1), (1, 0)])


def swap_sequences(block):
    return lax.ppermute(block, ("core", "yl"), [(0, 0), (1, 2), (2, 1), (3, 3)])


def near(block, axis):
    return move(block, axis, 1), move(block, axis, -1)


def far(back, ahead, axis):
    return move(back, axis, 1), move(ahead, axis, -1)


def halves(back, ahead, axis, cut):
    return far(back[:, :cut], ahead[:, cut:], axis)


def slot_ids(x, y):
    offsets = jnp.array(OFFSETS, jnp.int32)
    every = jnp.arange(RING, dtype=jnp.int32)
    rows = jnp.arange(HALF, dtype=jnp.int32)

    def slots(xx, yy, core):
        return (((yy // 2) * RING + xx) * 2 + core) * CAP + (yy % 2) * HALF

    first = slots(((x + offsets) % RING)[None, :, None], every[:, None, None], 0) + rows
    second = slots(every[:, None, None], ((y + offsets) % RING)[None, :, None], 1) + rows
    ids = jnp.concatenate([first, second], axis=0).reshape(PIECES, 1, BLK)
    return jnp.pad(ids, ((0, 0), (0, 0), (0, LANES - BLK)), constant_values=-1)


def three_parts(values):
    high = lax.reduce_precision(values, 8, 7)
    rest = values - high
    middle = lax.reduce_precision(rest, 8, 7)
    return jnp.concatenate([high, middle, rest - middle], axis=0).astype(LOW)


def whole():
    return pl.BlockSpec(memory_space=pltpu.VMEM)


def hbm():
    return pl.BlockSpec(memory_space=pl.ANY)


def smem():
    return pl.BlockSpec(memory_space=pltpu.SMEM)


def cost(flops, size):
    return pl.CostEstimate(flops=flops, bytes_accessed=size, transcendentals=0)


def pack_kernel(meta_ref, owner_ref, master_ref, own_ref, send_ref):
    is_low = meta_ref[0] == 0
    share = (meta_ref[3] // 2 * RING + meta_ref[2]) * 2 + meta_ref[0]
    count = jnp.sum((owner_ref[...] == share).astype(jnp.int32)) - lax.rem(meta_ref[3], 2) * HALF
    valid = lax.broadcasted_iota(jnp.int32, (HALF, 1), 0) < count
    blank = jnp.zeros((HALF, ATTN - 800), LOW)
    own_ref[:, 800:ATTN] = blank
    send_ref[:, 800:ATTN] = blank
    for start, at, width in MAP:
        low = jnp.where(valid, master_ref[:, start : start + width], 0.0)
        high = jnp.where(valid, master_ref[:, start + width : start + 2 * width], 0.0)
        own_ref[:, at : at + width] = jnp.where(is_low, low, high).astype(LOW)
        send_ref[:, at : at + width] = jnp.where(is_low, high, low).astype(LOW)


def pack(meta, owner, master):
    return pl.pallas_call(
        pack_kernel,
        in_specs=[smem(), whole(), whole()],
        out_specs=[whole()] * 2,
        out_shape=[jax.ShapeDtypeStruct((HALF, WIDE), LOW)] * 2,
        compiler_params=pltpu.CompilerParams(vmem_limit_bytes=VMEM),
        name="pack",
    )(meta, owner.reshape(20, 128), master)


def assemble_kernel(*refs):
    out = refs[4]
    for k, ref in enumerate(refs[:4]):
        out[k * HALF : (k + 1) * HALF, :] = ref[...]


def assemble(blocks, j):
    block, back, ahead, one, two = blocks
    specs = [pl.BlockSpec((HALF, FW), lambda i: (0, j))] * 3
    specs += [pl.BlockSpec((HALF, FW), lambda i: (0, j % 2))]
    return pl.pallas_call(
        assemble_kernel,
        grid=(1,),
        in_specs=specs,
        out_specs=pl.BlockSpec((BLK, FW), lambda i: (0, 0)),
        out_shape=jax.ShapeDtypeStruct((BLK, FW), LOW),
        compiler_params=pltpu.CompilerParams(vmem_limit_bytes=VMEM),
        cost_estimate=cost(0, 0),
        name="assemble",
    )(block, back, ahead, one if j < 2 else two)


def one_hot(slot_ref, ids_ref):
    return jnp.where(slot_ref[...] == ids_ref[0], 1.0, 0.0).astype(LOW)


def tokens_kernel(meta_ref, slot_ref, ids_ref, tokens_ref, gains_ref, parts_ref, xn_ref, in_ref, gain_ref, rows):
    @pl.when(pl.program_id(0) == 0)
    def _():
        at = pl.multiple_of(meta_ref[1] * 32, 32)
        tokens = tokens_ref[:128].astype(F32)
        scale = lax.rsqrt(jnp.sum(tokens * tokens, axis=1, keepdims=True) / D + EPS_NORM)
        rows[:128] = (tokens * scale * gains_ref[0:1]).astype(LOW)
        rows[128:160] = tokens_ref[pl.ds(at, 32)]
        rows[160:] = parts_ref[...]

    placed = dot(rows[...], one_hot(slot_ref, ids_ref), 1, 0)
    xn_ref[0] = placed[:128].astype(LOW)
    in_ref[0] = placed[128:160]
    gain_ref[0] = placed[160:162] + placed[162:164] + placed[164:166]


def cot_kernel(meta_ref, slot_ref, ids_ref, cot_ref, out_ref, z_ref, rows):
    @pl.when(pl.program_id(0) == 0)
    def _():
        rows[:128] = cot_ref[...]
        rows[128:] = cot_ref[pl.ds(pl.multiple_of(meta_ref[1] * 32, 32), 32)]

    placed = dot(rows[...], one_hot(slot_ref, ids_ref), 1, 0)
    out_ref[0] = placed[:128].astype(LOW)
    z_ref[0] = placed[128:]


def to_slots(kernel, meta, slot, ids, args, outs, rows, name):
    def same(shape):
        return pl.BlockSpec(shape, lambda p: (0, 0))

    return pl.pallas_call(
        kernel,
        grid=(PIECES,),
        in_specs=[
            smem(),
            same((D, 1)),
            pl.BlockSpec((1, 1, LANES), lambda p: (p, 0, 0)),
            *(same(a.shape) for a in args),
        ],
        out_specs=[pl.BlockSpec((1, n, LANES), lambda p: (p, 0, 0)) for n, _ in outs],
        out_shape=[jax.ShapeDtypeStruct((PIECES, n, LANES), kind) for n, kind in outs],
        scratch_shapes=[pltpu.VMEM((rows, D), LOW)],
        compiler_params=pltpu.CompilerParams(vmem_limit_bytes=VMEM),
        cost_estimate=cost(0, 0),
        name=name,
    )(meta, slot, ids, *args)


def tokens_to_slots(meta, slot, ids, tokens, gains, parts):
    outs = [(128, LOW), (32, F32), (2, F32)]
    args = (tokens, gains, parts)
    return to_slots(tokens_kernel, meta, slot, ids, args, outs, 176, "tokens_to_slots")


def cot_to_slots(meta, slot, ids, cotangent):
    outs = [(128, LOW), (32, F32)]
    return to_slots(cot_kernel, meta, slot, ids, (cotangent,), outs, 160, "cotangent_to_slots")


def unplace_kernel(slot_ref, ids_ref, rows_ref, out_ref, acc):
    ids = jnp.transpose(jnp.broadcast_to(ids_ref[0], (8, LANES)))[:, :1]
    place = jnp.where(ids == slot_ref[...], 1.0, 0.0).astype(LOW)

    @pl.when(pl.program_id(0) == 0)
    def _():
        acc[...] = jnp.zeros_like(acc)

    acc[...] += dot(rows_ref[0], place, 1, 0)

    @pl.when(pl.program_id(0) == PIECES - 1)
    def _():
        out_ref[...] = acc[...].astype(LOW)


def from_slots(rows, slot, ids):
    n = rows.shape[1]
    return pl.pallas_call(
        unplace_kernel,
        grid=(PIECES,),
        in_specs=[
            pl.BlockSpec((1, D), lambda p: (0, 0)),
            pl.BlockSpec((1, 1, LANES), lambda p: (p, 0, 0)),
            pl.BlockSpec((1, n, LANES), lambda p: (p, 0, 0)),
        ],
        out_specs=pl.BlockSpec((n, D), lambda p: (0, 0)),
        out_shape=jax.ShapeDtypeStruct((n, D), LOW),
        scratch_shapes=[pltpu.VMEM((n, D), F32)],
        compiler_params=pltpu.CompilerParams(vmem_limit_bytes=VMEM),
        cost_estimate=cost(0, 0),
        name="from_slots",
    )(slot, ids, rows)


def start_weights(meta_ref, refs, held, sems):
    x = meta_ref[2]
    y = meta_ref[3]
    for base, at, group in ((0, y, refs[:4]), (RING, x, refs[4:])):
        for ref, offset in zip(group, OFFSETS):
            p = base + lax.rem(at + offset + RING, RING)
            pltpu.make_async_copy(ref, held.at[p], sems.at[p]).start()


def piece_at(meta_ref, n):
    kind = n // RING
    k = lax.rem(n, RING)
    offset = jnp.where(k == 1, 3, jnp.where(k == 2, 1, jnp.where(k == 3, 2, 0)))
    at = jnp.where(kind == 0, meta_ref[3], meta_ref[2])
    return kind * RING + lax.rem(at + offset, RING)


def wait_weights(held, sems, p):
    pltpu.make_async_copy(held.at[p], held.at[p], sems.at[p]).wait()


def split_rows(value, scratch, core, p, keep_ref, send_ref):
    scratch[:, :BLK] = value.astype(LOW)
    for z in range(RING):
        keep_ref[z, p] = scratch[pl.ds(pl.multiple_of(core * 128 + 32 * z, 32), 32), :]
        send_ref[z, p] = scratch[pl.ds(pl.multiple_of((1 - core) * 128 + 32 * z, 32), 32), :]


def join_rows(is_low, own, got):
    return jnp.concatenate(
        [jnp.where(is_low, own, got), jnp.where(is_low, got, own)], axis=0
    )


def rope(values, cosine, sine):
    half = HD // 2
    turned = jnp.concatenate([-values[:, half:], values[:, :half]], axis=1)
    return values * cosine + turned * sine


def head_probs(query, keys, mask):
    scores = dot(query, keys, 1, 1) * HD ** (-0.5)
    scores = jnp.where(mask, scores, NEG_BIG)
    weight = jnp.exp(scores - jnp.max(scores, axis=1, keepdims=True))
    return weight / jnp.sum(weight, axis=1, keepdims=True)


def causal_mask(seg_col, seg_row):
    rows = lax.broadcasted_iota(jnp.int32, (SEQ, SEQ), 0)
    cols = lax.broadcasted_iota(jnp.int32, (SEQ, SEQ), 1)
    return (seg_col == seg_row) & (cols <= rows)


def attention_kernel(
    meta_ref, own_ref, got_ref, cos_ref, sin_ref, segc_ref, segr_ref, *rest
):
    w_refs = rest[:8]
    q_ref, k_ref, v_ref, o_ref, keep_ref, send_ref, held, acc, part, sems = rest[8:]
    core = meta_ref[0]
    is_low = core == 0
    start_weights(meta_ref, w_refs, held, sems)
    acc[...] = jnp.zeros_like(acc)
    part[:, BLK:] = jnp.zeros((SEQ, LANES - BLK), LOW)

    def project(n, carry):
        p = piece_at(meta_ref, n)
        wait_weights(held, sems, p)
        rows = join_rows(is_low, own_ref[p], got_ref[p])
        acc[...] += dot(rows[:, :BLK], held[p, :, 256:], 1, 0)
        return carry

    lax.fori_loop(0, PIECES, project, 0)
    cosine = cos_ref[...]
    sine = sin_ref[...]
    mask = causal_mask(segc_ref[...], segr_ref[...])
    projected = acc[...]
    keys = rope(projected[:, 384:464], cosine, sine).astype(LOW)
    values = projected[:, 464:544].astype(LOW)
    k_ref[...] = keys
    v_ref[...] = values
    outs = []
    for h in range(HEADS):
        query = rope(projected[:, 64 + h * HD : 64 + (h + 1) * HD], cosine, sine).astype(LOW)
        q_ref[h] = query
        probs = head_probs(query, keys, mask)
        outs.append(dot(probs.astype(LOW), values, 1, 0))
    outs.append(jnp.zeros((SEQ, 64), F32))
    attended = jnp.concatenate(outs, axis=1).astype(LOW)
    o_ref[...] = attended

    def spread(p, carry):
        split_rows(dot(attended, held[p, :, :384], 1, 1), part, core, p, keep_ref, send_ref)
        return carry

    lax.fori_loop(0, PIECES, spread, 0)


def split_shapes():
    return [
        jax.ShapeDtypeStruct((RING, PIECES, 32, LANES), LOW),
        jax.ShapeDtypeStruct((RING, PIECES, 32, LANES), LOW),
    ]


def attention_forward(meta, own, got, tables, segs, w_attn):
    return pl.pallas_call(
        attention_kernel,
        in_specs=[smem()] + [whole()] * 6 + [hbm()] * 8,
        out_specs=[whole()] * 6,
        out_shape=[
            jax.ShapeDtypeStruct((HEADS, SEQ, HD), LOW),
            jax.ShapeDtypeStruct((SEQ, HD), LOW),
            jax.ShapeDtypeStruct((SEQ, HD), LOW),
            jax.ShapeDtypeStruct((SEQ, 384), LOW),
        ]
        + split_shapes(),
        scratch_shapes=[
            pltpu.VMEM((PIECES, BLK, ATTN), LOW),
            pltpu.VMEM((SEQ, ATTN - 256), F32),
            pltpu.VMEM((SEQ, LANES), LOW),
            pltpu.SemaphoreType.DMA((PIECES,)),
        ],
        compiler_params=pltpu.CompilerParams(vmem_limit_bytes=VMEM),
        cost_estimate=cost(0, 0),
        name="attention_forward",
    )(meta, own, got, *tables, *segs, *w_attn)


def put_blocks(ref, value):
    for k in range(RING):
        ref[k] = value[k * HALF : (k + 1) * HALF].astype(LOW)


def attention_back_kernel(
    meta_ref, own_ref, got_ref, cos_ref, sin_ref, segc_ref, segr_ref, q_ref, k_ref, v_ref, o_ref, xc_ref, xc_got_ref, *rest
):
    w_refs = rest[:8]
    keep_ref, send_ref = rest[8:10]
    outs = rest[10:18]
    held, acc, part, sems = rest[18:]
    core = meta_ref[0]
    is_low = core == 0
    start_weights(meta_ref, w_refs, held, sems)
    acc[...] = jnp.zeros_like(acc)
    part[:, BLK:] = jnp.zeros((SEQ, LANES - BLK), LOW)

    def project(n, carry):
        p = piece_at(meta_ref, n)
        wait_weights(held, sems, p)
        own = jnp.concatenate([own_ref[z, p] for z in range(RING)], axis=0)
        got = jnp.concatenate([got_ref[z, p] for z in range(RING)], axis=0)
        acc[...] += dot(join_rows(is_low, own, got)[:, :BLK], held[p, :, :384], 1, 0)
        return carry

    lax.fori_loop(0, PIECES, project, 0)
    cosine = cos_ref[...]
    sine = -sin_ref[...]
    mask = causal_mask(segc_ref[...], segr_ref[...])
    grad_att = acc[...]
    keys = k_ref[...]
    values = v_ref[...]
    factor = HD ** (-0.5)
    grads = []
    grad_keys = jnp.zeros((SEQ, HD), F32)
    grad_values = jnp.zeros((SEQ, HD), F32)
    for h in range(HEADS):
        query = q_ref[h]
        grad_o = grad_att[:, h * HD : (h + 1) * HD].astype(LOW)
        probs = head_probs(query, keys, mask)
        grad_probs = dot(grad_o, values, 1, 1)
        inner = jnp.sum(probs * grad_probs, axis=1, keepdims=True)
        grad_scores = (probs * (grad_probs - inner)).astype(LOW)
        grads.append(rope(dot(grad_scores, keys, 1, 0) * factor, cosine, sine))
        grad_keys += dot(grad_scores, query, 0, 0)
        grad_values += dot(probs.astype(LOW), grad_o, 0, 0)
    grads.append(rope(grad_keys * factor, cosine, sine))
    grads.append(grad_values)
    zeros = [jnp.zeros((SEQ, 64), F32)]
    ends = [jnp.zeros((SEQ, 96), F32)]
    grad_qkv = jnp.concatenate(zeros + grads + ends, axis=1).astype(LOW)

    def spread(p, carry):
        split_rows(dot(grad_qkv, held[p, :, 256:], 1, 1), part, core, p, keep_ref, send_ref)
        return carry

    lax.fori_loop(0, PIECES, spread, 0)

    for kind in range(2):
        for k in range(RING):
            q = kind * RING + lax.rem(meta_ref[3 - kind] + OFFSETS[k] + RING, RING)
            own = jnp.concatenate([own_ref[z, q] for z in range(RING)], axis=0)
            got = jnp.concatenate([got_ref[z, q] for z in range(RING)], axis=0)
            grad = join_rows(is_low, own, got)[:, :BLK]
            xn = join_rows(is_low, xc_ref[q], xc_got_ref[q])[:, :BLK]
            one = dot(grad, o_ref[...], 0, 0)
            two = dot(xn, grad_qkv, 0, 0)
            terms = jnp.concatenate([one[:, :QW], two[:, 64:]], axis=1)
            put_blocks(outs[RING * kind + k], terms)


def attention_backward(meta, own, got, tables, segs, qkvo, xcs, w_attn):
    return pl.pallas_call(
        attention_back_kernel,
        in_specs=[smem()] + [whole()] * 12 + [hbm()] * 8,
        out_specs=[whole()] * 10,
        out_shape=split_shapes() + [jax.ShapeDtypeStruct((RING, HALF, ATTN), LOW)] * 8,
        scratch_shapes=[
            pltpu.VMEM((PIECES, BLK, ATTN), LOW),
            pltpu.VMEM((SEQ, 384), F32),
            pltpu.VMEM((SEQ, LANES), LOW),
            pltpu.SemaphoreType.DMA((PIECES,)),
        ],
        compiler_params=pltpu.CompilerParams(vmem_limit_bytes=VMEM),
        cost_estimate=cost(0, 0),
        name="attention_backward",
    )(meta, own, got, *tables, *segs, *qkvo, *xcs, *w_attn)


def down_back_kernel(meta_ref, cot_own_ref, cot_got_ref, *rest):
    w_refs = rest[:8]
    out_ref, held, sems = rest[8:]
    is_low = meta_ref[0] == 0
    start_weights(meta_ref, w_refs, held, sems)
    out_ref[...] = jnp.zeros_like(out_ref)

    def project(n, carry):
        p = piece_at(meta_ref, n)
        wait_weights(held, sems, p)
        cot = join_rows(is_low, cot_own_ref[p], cot_got_ref[p])
        out_ref[...] += dot(cot[:, :BLK], held[p], 1, 0)
        return carry

    lax.fori_loop(0, PIECES, project, 0)


def down_back(meta, cot_own, cot_got, w_down):
    return pl.pallas_call(
        down_back_kernel,
        in_specs=[smem()] + [whole()] * 2 + [hbm()] * 8,
        out_specs=whole(),
        out_shape=jax.ShapeDtypeStruct((SEQ, FW), F32),
        scratch_shapes=[
            pltpu.VMEM((PIECES, BLK, FW), LOW),
            pltpu.SemaphoreType.DMA((PIECES,)),
        ],
        compiler_params=pltpu.CompilerParams(vmem_limit_bytes=VMEM),
        cost_estimate=cost(0, 0),
        name="down_backward",
    )(meta, cot_own, cot_got, *w_down)


def down_kernel(meta_ref, act_ref, *rest):
    w_refs = rest[:8]
    keep_ref, send_ref, held, part, sems = rest[8:]
    core = meta_ref[0]
    start_weights(meta_ref, w_refs, held, sems)
    part[:, BLK:] = jnp.zeros((SEQ, LANES - BLK), LOW)

    def spread(n, carry):
        p = piece_at(meta_ref, n)
        wait_weights(held, sems, p)
        split_rows(dot(act_ref[...], held[p], 1, 1), part, core, p, keep_ref, send_ref)
        return carry

    lax.fori_loop(0, PIECES, spread, 0)


def down_forward(meta, act, w_down):
    return pl.pallas_call(
        down_kernel,
        in_specs=[smem(), whole()] + [hbm()] * 8,
        out_specs=[whole()] * 2,
        out_shape=split_shapes(),
        scratch_shapes=[
            pltpu.VMEM((PIECES, BLK, FW), LOW),
            pltpu.VMEM((SEQ, LANES), LOW),
            pltpu.SemaphoreType.DMA((PIECES,)),
        ],
        compiler_params=pltpu.CompilerParams(vmem_limit_bytes=VMEM),
        cost_estimate=cost(0, 0),
        name="down_forward",
    )(meta, act, *w_down)


def start_ffn(meta_ref, refs, held, sems):
    x = meta_ref[2]
    y = meta_ref[3]
    for base, at, group in ((0, y, refs[:8]), (RING, x, refs[8:])):
        for k, offset in enumerate(OFFSETS):
            p = base + lax.rem(at + offset + RING, RING)
            for j in range(2):
                into = held.at[p, :, pl.ds(j * FW, FW)]
                pltpu.make_async_copy(group[2 * k + j], into, sems.at[p]).start()


def ffn_kernel(meta_ref, own_ref, got_ref, grad_act_ref, *rest):
    w_refs = rest[:16]
    act_ref, grad_ref, keep_ref, send_ref, held, acc, part, sems = rest[16:]
    core = meta_ref[0]
    is_low = core == 0
    start_ffn(meta_ref, w_refs, held, sems)
    acc[...] = jnp.zeros_like(acc)
    part[:, BLK:] = jnp.zeros((SEQ, LANES - BLK), LOW)

    def project(n, carry):
        p = piece_at(meta_ref, n)
        wait_weights(held, sems, p)
        own = jnp.concatenate([own_ref[z, p] for z in range(RING)], axis=0)
        got = jnp.concatenate([got_ref[z, p] for z in range(RING)], axis=0)
        acc[...] += dot(join_rows(is_low, own, got)[:, :BLK], held[p], 1, 0)
        return carry

    lax.fori_loop(0, PIECES, project, 0)

    def units(t, carry):
        at = pl.multiple_of(t * 128, 128)
        grad_act = grad_act_ref[:, pl.ds(at, 128)]
        gate = acc[:, pl.ds(at, 128)]
        up = acc[:, pl.ds(at + FW, 128)]
        sigmoid = 1.0 / (1.0 + jnp.exp(-gate))
        silu = gate * sigmoid
        act_ref[:, pl.ds(at, 128)] = (silu * up).astype(LOW)
        grad_gate = grad_act * up * sigmoid * (1.0 + gate * (1.0 - sigmoid))
        grad_ref[:, pl.ds(at, 128)] = grad_gate.astype(LOW)
        grad_ref[:, pl.ds(at + FW, 128)] = (grad_act * silu).astype(LOW)
        return carry

    lax.fori_loop(0, FW // 128, units, 0)

    def spread(p, carry):
        split_rows(dot(grad_ref[...], held[p], 1, 1), part, core, p, keep_ref, send_ref)
        return carry

    lax.fori_loop(0, PIECES, spread, 0)


def feed_forward(meta, own, got, grad_act, w_gu):
    return pl.pallas_call(
        ffn_kernel,
        in_specs=[smem()] + [whole()] * 3 + [hbm()] * 16,
        out_specs=[whole()] * 4,
        out_shape=[
            jax.ShapeDtypeStruct((SEQ, FW), LOW),
            jax.ShapeDtypeStruct((SEQ, GU), LOW),
        ]
        + split_shapes(),
        scratch_shapes=[
            pltpu.VMEM((PIECES, BLK, GU), LOW),
            pltpu.VMEM((SEQ, GU), F32),
            pltpu.VMEM((SEQ, LANES), LOW),
            pltpu.SemaphoreType.DMA((PIECES,)),
        ],
        compiler_params=pltpu.CompilerParams(vmem_limit_bytes=VMEM),
        cost_estimate=cost(0, 0),
        name="feed_forward",
    )(meta, own, got, grad_act, *w_gu)


def halves_of(part_ref, xc_ref, q, at):
    rows = jnp.concatenate([part_ref[z, q] for z in range(RING)], axis=0)
    return rows[:, :BLK], xc_ref[q, at : at + 128][:, :BLK]


def merge_kernel(part_ref, xc_ref, one_ref, two_ref):
    for p in range(RING):
        for ref, q in ((one_ref, p), (two_ref, RING + p)):
            for z in range(RING):
                ref[p, 32 * z : 32 * z + 32] = part_ref[z, q]
            ref[p, 128:] = xc_ref[q]


def merge(part, cot):
    return pl.pallas_call(
        merge_kernel,
        in_specs=[whole()] * 2,
        out_specs=[whole()] * 2,
        out_shape=[jax.ShapeDtypeStruct((RING, 256, LANES), LOW)] * 2,
        compiler_params=pltpu.CompilerParams(vmem_limit_bytes=VMEM),
        cost_estimate=cost(0, 0),
        name="merge",
    )(part, cot)


def ffn_terms_kernel(meta_ref, own_ref, got_ref, *rest, axis):
    rights = rest[:8]
    outs = rest[8:12]
    acc = rest[12]
    is_low = meta_ref[0] == 0
    at = meta_ref[axis]
    for k, offset in enumerate(OFFSETS):
        source = lax.rem(at + offset + RING, RING)
        xn = join_rows(is_low, own_ref[source, :128], got_ref[source, :128])[:, :BLK]
        cot = join_rows(is_low, own_ref[source, 128:], got_ref[source, 128:])[:, :BLK]
        down = dot(cot, rights[2 * k][...], 0, 0)
        both = dot(xn, rights[2 * k + 1][...], 0, 0)
        if k == 0:
            acc[:, :FW] = down
            acc[:, FW:] = both
        else:
            acc[:, :FW] += down
            acc[:, FW:] += both
    for k, ref in enumerate(outs):
        ref[:, ATTN:] = acc[k * HALF : (k + 1) * HALF, :].astype(LOW)


def ffn_terms(meta, own, got, rights, axis):
    return pl.pallas_call(
        functools.partial(ffn_terms_kernel, axis=axis),
        in_specs=[smem()] + [whole()] * 10,
        out_specs=[whole()] * 4,
        out_shape=[jax.ShapeDtypeStruct((HALF, WIDE), LOW)] * 4,
        scratch_shapes=[pltpu.VMEM((BLK, 3 * FW), F32)],
        compiler_params=pltpu.CompilerParams(vmem_limit_bytes=VMEM),
        cost_estimate=cost(0, 0),
        name="terms_feed_forward",
    )(meta, own, got, *rights)


def fill_kernel(*refs):
    for k, ref in enumerate(refs[8:]):
        total = refs[0][k].astype(F32)
        for part in refs[1:4]:
            total = total + part[k].astype(F32)
        ref[...] = total.astype(LOW)


def fill(attn, ffn):
    return pl.pallas_call(
        fill_kernel,
        grid=(1,),
        in_specs=[pl.BlockSpec((RING, HALF, ATTN), lambda i: (0, 0, 0))] * 4 + [hbm()] * 4,
        out_specs=[pl.BlockSpec((HALF, ATTN), lambda i: (0, 0))] * 4,
        out_shape=[jax.ShapeDtypeStruct((HALF, WIDE), LOW)] * 4,
        input_output_aliases={4 + k: k for k in range(4)},
        compiler_params=pltpu.CompilerParams(vmem_limit_bytes=VMEM),
        cost_estimate=cost(0, 0),
        name="fill",
    )(*attn, *ffn)


def finish_kernel(meta_ref, *refs):
    out_ref = refs[8]
    out_ref[...] = pick_sum(meta_ref[0] == 1, refs).astype(LOW)


def pick_sum(is_first, refs):
    total = jnp.where(is_first, refs[0][...], refs[4][...]).astype(F32)
    for k in range(1, 4):
        total = total + jnp.where(is_first, refs[k][...], refs[4 + k][...]).astype(F32)
    return total


def finish(meta, parts):
    return pl.pallas_call(
        finish_kernel,
        in_specs=[smem()] + [whole()] * 8,
        out_specs=whole(),
        out_shape=jax.ShapeDtypeStruct((HALF, WIDE), LOW),
        compiler_params=pltpu.CompilerParams(vmem_limit_bytes=VMEM),
        cost_estimate=cost(0, 0),
        name="finish_other",
    )(meta, *parts[0], *parts[1])


def adam_kernel(meta_ref, w_ref, m_ref, v_ref, came, *rest):
    parts = rest[:8]
    wo_ref, mo_ref, vo_ref, grad, stay = rest[8:]
    is_low = meta_ref[0] == 0
    stay[...] = pick_sum(is_low, parts)
    rows = w_ref.shape[0]
    for start, at, width in MAP:
        mine = stay[:, at : at + width]
        other = came[:, at : at + width].astype(F32)
        grad[:, start : start + width] = jnp.where(is_low, mine, other)
        grad[:, start + width : start + 2 * width] = jnp.where(is_low, other, mine)
    row = pl.program_id(0) * rows + lax.broadcasted_iota(jnp.int32, (rows, 1), 0)
    valid = row < meta_ref[4]
    weight, first, second = adam_step(
        w_ref[...], m_ref[...], v_ref[...], grad[...], LEARN, DECAY
    )
    wo_ref[...] = jnp.where(valid, weight, 0.0)
    mo_ref[...] = jnp.where(valid, first, 0.0)
    vo_ref[...] = jnp.where(valid, second, 0.0)


def adam(meta, master, moment_one, moment_two, came, parts):
    rows = 32
    units = master.shape[1]

    def block(width):
        return pl.BlockSpec((rows, width), lambda i: (i, 0))

    return pl.pallas_call(
        adam_kernel,
        grid=(pl.cdiv(HALF, rows),),
        in_specs=[smem()] + [block(units)] * 3 + [block(WIDE)] * 9,
        out_specs=[block(units)] * 3,
        out_shape=[jax.ShapeDtypeStruct(master.shape, F32)] * 3,
        scratch_shapes=[pltpu.VMEM((rows, units), F32), pltpu.VMEM((rows, WIDE), F32)],
        compiler_params=pltpu.CompilerParams(vmem_limit_bytes=VMEM),
        name="adam",
    )(meta, master, moment_one, moment_two, came, *parts[0], *parts[1])


def rms_scale(values):
    return lax.rsqrt(jnp.sum(values * values, axis=(0, 2), keepdims=True) / D + EPS_NORM)


def rms_backward(grad_out, normed, scale, gain):
    grad_normed = grad_out * gain
    inner = jnp.sum(grad_normed * normed, axis=(0, 2), keepdims=True) / D
    return scale * (grad_normed - normed * inner), jnp.sum(grad_out * normed, axis=1)


def adam_step(weight, first, second, grad, rate, decay):
    first_new = BETA * first + (1.0 - BETA) * grad
    second_new = BETA * second + (1.0 - BETA) * grad * grad
    inverse = 1.0 / (1.0 - BETA**STEP)
    update = (first_new * inverse) / (jnp.sqrt(second_new * inverse) + EPS_ADAM)
    return (weight - rate * (update + decay * weight), first_new, second_new)


def stage(*values):
    return lax.optimization_barrier(values)


def shards(
    tokens, cotangent, segments, owner, master, moment_one, moment_two, gains, gain_one, gain_two
):
    core = lax.axis_index("core")
    yl = lax.axis_index("yl")
    z = lax.axis_index("z")
    x = lax.axis_index(X)
    y = lax.axis_index("yh") * 2 + yl
    count = jnp.sum((owner == (y // 2 * RING + x) * 2 + core).astype(jnp.int32)) - yl * HALF
    place = jnp.stack([core, z, x, y]).astype(jnp.int32)
    meta = jnp.stack([core, z, x, y, count]).astype(jnp.int32)
    along = (Y, X)
    across = (X, Y)

    def add_core(keep, other):
        return (keep.astype(F32) + other.astype(F32)).astype(LOW)

    def split_z(block):
        return lax.all_to_all(block, "z", split_axis=0, concat_axis=0, tiled=True)

    def sum_z(block):
        return jnp.sum(block.astype(F32), axis=0)

    def all_z(block):
        return split_z(jnp.broadcast_to(block[None], (RING, *block.shape)))

    own, send = pack(place, owner, master)
    got = swap_core(send)
    first = jnp.where(core == 0, own, got)
    second = jnp.where(core == 0, got, own)
    first, second, owner, tokens, cotangent = stage(first, second, owner, tokens, cotangent)

    near_first = near(first, X)
    near_second = near(second, Y)
    numbers = jnp.zeros((8, D), LOW).at[0, :SEQ].set(segments.astype(LOW))
    tokens = swap_sequences(jnp.concatenate([tokens, numbers], axis=0))
    onehot = (owner[:, None] == jnp.arange(16, dtype=jnp.int32)[None, :]).astype(jnp.int32)
    rank = jnp.sum((jnp.cumsum(onehot, axis=0) - onehot) * onehot, axis=1)
    slot = (owner * CAP + rank)[:, None]
    ids = slot_ids(x, y)
    parts = jnp.concatenate([three_parts(gains), jnp.zeros((10, D), LOW)], axis=0)
    near_first, near_second, slot, ids, parts, cotangent = stage(
        near_first, near_second, slot, ids, parts, cotangent
    )

    blocks = [
        (first, *near_first, *halves(*near_first, X, WIDE_CUT)),
        (second, *near_second, *halves(*near_second, Y, WIDE_CUT)),
    ]
    attn = [assemble(b, 0) for b in blocks]
    attn, blocks, tokens, cotangent = stage(attn, blocks, tokens, cotangent)

    attn_near = [near(b, axis) for b, axis in zip(attn, along)]
    position = jnp.arange(SEQ, dtype=F32)
    freq = jnp.exp(-jnp.log(THETA) * (2.0 * jnp.arange(HD // 2, dtype=F32) / HD))
    angle = position[:, None] * freq[None, :]
    tables = (
        jnp.concatenate([jnp.cos(angle)] * 2, axis=1),
        jnp.concatenate([jnp.sin(angle)] * 2, axis=1),
    )
    segment = tokens[128, :SEQ].astype(jnp.int32)
    segs = (segment[:, None], segment[None, :])
    xn_own, inputs, gain = tokens_to_slots(meta, slot, ids, tokens, gains, parts)
    down = [assemble(b, 1) for b in blocks]
    cotangent = swap_sequences(cotangent)
    attn_near, tables, segs, down, xn_own, inputs, gain, cotangent = stage(
        attn_near, tables, segs, down, xn_own, inputs, gain, cotangent
    )
    down_near = [near(b, axis) for b, axis in zip(down, along)]
    xn_got = swap_core(xn_own)
    cot_own, cot_z = cot_to_slots(meta, slot, ids, cotangent)
    gate = [assemble(b, 2) for b in blocks]
    turned = (slot.reshape(1, D), ids)
    down_near, xn_got, blocks, gate, turned, cot_own, cot_z = stage(
        down_near, xn_got, blocks, gate, turned, cot_own, cot_z
    )
    pair_far = [far(q[0], d[1], axis) for q, d, axis in zip(attn_near, down_near, along)]
    up = [assemble(b, 3) for b in blocks]
    cot_got = swap_core(cot_own)
    pair_far, gate, up, cot_got = stage(pair_far, gate, up, cot_got)
    w_attn = []
    w_down = []
    for kind in range(2):
        w_attn += [attn[kind], *attn_near[kind], pair_far[kind][0]]
        w_down += [down[kind], *down_near[kind], pair_far[kind][1]]

    gate_near = [near(b, axis) for b, axis in zip(gate, along)]
    *qkv, attended, keep, send = attention_forward(meta, xn_own, xn_got, tables, segs, w_attn)
    gate_near, up, keep, send = stage(gate_near, up, keep, send)
    up_near = [near(b, axis) for b, axis in zip(up, along)]
    got = split_z(add_core(keep, swap_core(send)))
    grad_act = down_back(meta, cot_own, cot_got, w_down)
    up_near, gate_near, got, grad_act = stage(up_near, gate_near, got, grad_act)
    gu_far = [far(g[0], u[1], axis) for g, u, axis in zip(gate_near, up_near, along)]
    hidden = inputs + sum_z(got)
    scale_two = rms_scale(hidden)
    normed_two = hidden * scale_two
    xn_two = all_z((normed_two * gain[:, 1:2]).astype(LOW))
    gu_far, xn_two = stage(gu_far, xn_two)
    xn_two_got = swap_core(xn_two)
    left_sent = merge(xn_two, cot_own)
    xn_two, xn_two_got, grad_act, left_sent = stage(xn_two, xn_two_got, grad_act, left_sent)
    w_gu = []
    for kind in range(2):
        w_gu += [gate[kind], up[kind]]
        w_gu += [gate_near[kind][0], up_near[kind][0], gate_near[kind][1], up_near[kind][1]]
        w_gu += [*gu_far[kind]]

    act, grad_gu, keep, send = feed_forward(meta, xn_two, xn_two_got, grad_act, w_gu)
    def exchange(block, axis):
        return lax.all_to_all(block, axis, split_axis=0, concat_axis=0, tiled=True)

    lefts = [exchange(left_sent[0], Y)]
    act, grad_gu, keep, send, lefts = stage(act, grad_gu, keep, send, lefts)
    gu_near = [near(grad_gu, axis) for axis in along]
    got = split_z(add_core(keep, swap_core(send)))
    keep_mlp, send_mlp = down_forward(meta, act, w_down)
    gu_near, got, keep_mlp, send_mlp, act = stage(gu_near, got, keep_mlp, send_mlp, act)
    act_near = [near(act, axis) for axis in along]
    lefts_got = [swap_core(lefts[0])]
    mlp_both = add_core(keep_mlp, swap_core(send_mlp))
    grad_xn_two = sum_z(got)
    grad_norm_two, gain_grad_two = rms_backward(grad_xn_two, normed_two, scale_two, gain[:, 1:2])
    grad_hidden = cot_z + grad_norm_two
    grad_branch = all_z(grad_hidden.astype(LOW))
    act_near, grad_branch, grad_hidden, gain_grad_two, left_sent, lefts_got, gu_near, mlp_both = stage(
        act_near, grad_branch, grad_hidden, gain_grad_two, left_sent, lefts_got, gu_near, mlp_both
    )
    grad_branch_got = swap_core(grad_branch)
    ends = [far(a[0], g[1], axis) for a, g, axis in zip(act_near, gu_near, along)]
    lefts.append(exchange(left_sent[1], X))

    xns = (xn_own, xn_got)
    keep, send, *terms = attention_backward(
        meta, grad_branch, grad_branch_got, tables, segs, (*qkv, attended), xns, w_attn
    )
    attn_terms = (terms[:4], terms[4:])
    mlp = lax.psum_scatter(mlp_both, "z", scatter_dimension=0, tiled=True)[0]
    ends, keep, send, attn_terms, lefts, mlp = stage(ends, keep, send, attn_terms, lefts, mlp)

    def direct(first, second, axes):
        _, back, ahead, last = first
        _, back_two, ahead_two, last_two = second
        one = (move(ahead, axes[0], 1), move(back, axes[0], -1), move(last, axes[0], 2))
        up = move(ahead_two, axes[1], 1)
        down = move(back_two, axes[1], -1)
        return one, up, down, last_two

    attn_nears = [
        (move(t[2], axis, 1), move(t[1], axis, -1)) for t, axis in zip(attn_terms, along)
    ]

    def rights_of(kind):
        rights = (act, grad_gu)
        for n in range(2):
            rights += (act_near[kind][n], gu_near[kind][n])
        return rights + tuple(ends[kind])

    ffn_sums = [ffn_terms(meta, lefts[0], lefts_got[0], rights_of(0), 3)]
    lefts_got.append(swap_core(lefts[1]))
    got = split_z(add_core(keep, swap_core(send)))
    attn_nears, attn_terms, lefts, lefts_got, ffn_sums, got = stage(
        attn_nears, attn_terms, lefts, lefts_got, ffn_sums, got
    )
    attn_others = [
        (*n, move(t[3], axis, 2)) for n, t, axis in zip(attn_nears, attn_terms, along)
    ]
    ffn_sums.append(ffn_terms(meta, lefts[1], lefts_got[1], rights_of(1), 2))
    grad_xn_one = sum_z(got)
    scale_one = rms_scale(inputs)
    grad_norm_one, gain_grad_one = rms_backward(
        grad_xn_one, inputs * scale_one, scale_one, gain[:, 0:1]
    )
    grad_tokens_z = (grad_hidden + grad_norm_one).astype(LOW)
    output_z = (hidden + mlp.astype(F32)).astype(LOW)
    gain_grads = three_parts(jnp.stack([gain_grad_one, gain_grad_two], axis=0))
    gain_grads = jnp.swapaxes(gain_grads, 0, 1)
    blank = jnp.zeros((PIECES, 10, LANES), LOW)
    last = from_slots(
        jnp.concatenate([output_z, grad_tokens_z, gain_grads, blank], axis=1), *turned
    )
    attn_others, ffn_sums, last = stage(attn_others, ffn_sums, last)
    blocks = [fill((t[0], *o), f) for t, o, f in zip(attn_terms, attn_others, ffn_sums)]
    part = lax.all_gather(last, "z", axis=0, tiled=False)
    one, up, down, last_two = direct(*blocks, across)
    up, down, last_two = stage(up, down, last_two)
    others = (one, (up, down, move(last_two, across[1], 2)))
    others, owns = stage(others, [b[0] for b in blocks])
    totals = [(b, *o) for b, o in zip(owns, others)]
    send, totals = stage(finish(meta, totals), totals)
    came = swap_core(send)
    moved = swap_sequences(jnp.swapaxes(part[:, :64].reshape(RING, 2, 32, D), 0, 1))
    gain_grads = part[:, 64:70].astype(F32).sum(axis=0)
    gain_grads = gain_grads[:2] + gain_grads[2:4] + gain_grads[4:6]
    gain_grads = gain_grads + swap_core(gain_grads)

    def sum_along(value, axis):
        back, ahead = near(value, axis)
        return (value + move(value, axis, 2)) + (back + ahead)

    new_master, new_one, new_two = adam(meta, master, moment_one, moment_two, came, totals)
    gain_grads, new_master, moved = stage(gain_grads, new_master, moved)
    gain_grads = sum_along(sum_along(gain_grads, X), Y)
    output = moved[0].reshape(128, D)
    grad_tokens = moved[1].reshape(128, D)
    new_gains, new_gain_one, new_gain_two = adam_step(
        gains, gain_one, gain_two, gain_grads, LEARN_GAIN, 0.0
    )
    return (
        output,
        grad_tokens,
        new_master,
        new_one,
        new_two,
        new_gains,
        new_gain_one,
        new_gain_two,
    )


def solution(mesh):
    fine = Mesh(mesh.devices.reshape(2, 4, 2, 2, 4), ("yh", "x", "core", "yl", "z"))
    rows = ("yh", "x", "core", "yl")
    in_specs = (
        P(rows, None),
        P(rows, None),
        P(("yh", "x", "core")),
        P(),
        P(rows, "z"),
        P(rows, "z"),
        P(rows, "z"),
        P(),
        P(),
        P(),
    )
    out_specs = (
        P(rows, None),
        P(rows, None),
        P(rows, "z"),
        P(rows, "z"),
        P(rows, "z"),
        P(),
        P(),
        P(),
    )
    return jax.shard_map(shards, mesh=fine, in_specs=in_specs, out_specs=out_specs, check_vma=False)
```

```python
import functools

import jax
import jax.numpy as jnp
from jax import lax
from jax.experimental import pallas as pl
from jax.experimental.pallas import tpu as pltpu
from jax.sharding import Mesh
from jax.sharding import PartitionSpec as P

HD = 80
STEP = 5
D = 2560
CAP = 240
HALF = 120
SEQ = 256
RING = 4

EPS_NORM = 1e-05
EPS_ADAM = 1e-08
THETA = 1000000.0
BETA = 0.5
LEARN = 0.05
LEARN_GAIN = 0.2
DECAY = 0.1
NEG_BIG = -1e30

X = "x"
Y = ("yh", "yl")
OFFSETS = (0, -1, 1, 2)
LOW = jnp.bfloat16
F32 = jnp.float32

HEADS = 4
QW = 320
KW = 80
FW = 896
ATTN = 896
GU = 2 * FW
WIDE = ATTN + 3 * FW
WIDE_CUT = 1792
MAP = (
    (0, 320, QW),
    (640, 640, KW),
    (800, 720, KW),
    (960, 1792, FW),
    (2752, 2688, FW),
    (4544, 0, QW),
    (5184, 896, FW),
)
PIECES = 8
BLK = 4 * HALF
LANES = 512
VMEM = 60 * 1024 * 1024


def dot(left, right, left_axis, right_axis):
    return lax.dot_general(
        left, right, (((left_axis,), (right_axis,)), ((), ())), preferred_element_type=F32
    )


def move(block, axis, distance):
    route = [(i, (i + distance) % RING) for i in range(RING)]
    return lax.ppermute(block, axis, route)


def swap_core(block):
    return lax.ppermute(block, "core", [(0, 1), (1, 0)])


def swap_sequences(block):
    return lax.ppermute(block, ("core", "yl"), [(0, 0), (1, 2), (2, 1), (3, 3)])


def near(block, axis):
    return move(block, axis, 1), move(block, axis, -1)


def far(back, ahead, axis):
    return move(back, axis, 1), move(ahead, axis, -1)


def halves(back, ahead, axis, cut):
    return far(back[:, :cut], ahead[:, cut:], axis)


def slot_ids(x, y):
    offsets = jnp.array(OFFSETS, jnp.int32)
    every = jnp.arange(RING, dtype=jnp.int32)
    rows = jnp.arange(HALF, dtype=jnp.int32)

    def slots(xx, yy, core):
        return (((yy // 2) * RING + xx) * 2 + core) * CAP + (yy % 2) * HALF

    first = slots(((x + offsets) % RING)[None, :, None], every[:, None, None], 0) + rows
    second = slots(every[:, None, None], ((y + offsets) % RING)[None, :, None], 1) + rows
    ids = jnp.concatenate([first, second], axis=0).reshape(PIECES, 1, BLK)
    return jnp.pad(ids, ((0, 0), (0, 0), (0, LANES - BLK)), constant_values=-1)


def three_parts(values):
    high = lax.reduce_precision(values, 8, 7)
    rest = values - high
    middle = lax.reduce_precision(rest, 8, 7)
    return jnp.concatenate([high, middle, rest - middle], axis=0).astype(LOW)


def whole():
    return pl.BlockSpec(memory_space=pltpu.VMEM)


def hbm():
    return pl.BlockSpec(memory_space=pl.ANY)


def smem():
    return pl.BlockSpec(memory_space=pltpu.SMEM)


def cost(flops, size):
    return pl.CostEstimate(flops=flops, bytes_accessed=size, transcendentals=0)


def pack_kernel(meta_ref, owner_ref, master_ref, own_ref, send_ref):
    is_low = meta_ref[0] == 0
    share = (meta_ref[3] // 2 * RING + meta_ref[2]) * 2 + meta_ref[0]
    count = jnp.sum((owner_ref[...] == share).astype(jnp.int32)) - lax.rem(meta_ref[3], 2) * HALF
    valid = lax.broadcasted_iota(jnp.int32, (HALF, 1), 0) < count
    blank = jnp.zeros((HALF, ATTN - 800), LOW)
    own_ref[:, 800:ATTN] = blank
    send_ref[:, 800:ATTN] = blank
    for start, at, width in MAP:
        low = jnp.where(valid, master_ref[:, start : start + width], 0.0)
        high = jnp.where(valid, master_ref[:, start + width : start + 2 * width], 0.0)
        own_ref[:, at : at + width] = jnp.where(is_low, low, high).astype(LOW)
        send_ref[:, at : at + width] = jnp.where(is_low, high, low).astype(LOW)


def pack(meta, owner, master):
    return pl.pallas_call(
        pack_kernel,
        in_specs=[smem(), whole(), whole()],
        out_specs=[whole()] * 2,
        out_shape=[jax.ShapeDtypeStruct((HALF, WIDE), LOW)] * 2,
        compiler_params=pltpu.CompilerParams(vmem_limit_bytes=VMEM),
        name="pack",
    )(meta, owner.reshape(20, 128), master)


def assemble_kernel(*refs):
    out = refs[4]
    for k, ref in enumerate(refs[:4]):
        out[k * HALF : (k + 1) * HALF, :] = ref[...]


def assemble(blocks, j):
    block, back, ahead, one, two = blocks
    specs = [pl.BlockSpec((HALF, FW), lambda i: (0, j))] * 3
    specs += [pl.BlockSpec((HALF, FW), lambda i: (0, j % 2))]
    return pl.pallas_call(
        assemble_kernel,
        grid=(1,),
        in_specs=specs,
        out_specs=pl.BlockSpec((BLK, FW), lambda i: (0, 0)),
        out_shape=jax.ShapeDtypeStruct((BLK, FW), LOW),
        compiler_params=pltpu.CompilerParams(vmem_limit_bytes=VMEM),
        cost_estimate=cost(0, 0),
        name="assemble",
    )(block, back, ahead, one if j < 2 else two)


def one_hot(slot_ref, ids_ref):
    return jnp.where(slot_ref[...] == ids_ref[0], 1.0, 0.0).astype(LOW)


def tokens_kernel(meta_ref, slot_ref, ids_ref, tokens_ref, gains_ref, parts_ref, xn_ref, in_ref, gain_ref, rows):
    @pl.when(pl.program_id(0) == 0)
    def _():
        at = pl.multiple_of(meta_ref[1] * 32, 32)
        tokens = tokens_ref[:128].astype(F32)
        scale = lax.rsqrt(jnp.sum(tokens * tokens, axis=1, keepdims=True) / D + EPS_NORM)
        rows[:128] = (tokens * scale * gains_ref[0:1]).astype(LOW)
        rows[128:160] = tokens_ref[pl.ds(at, 32)]
        rows[160:] = parts_ref[...]

    placed = dot(rows[...], one_hot(slot_ref, ids_ref), 1, 0)
    xn_ref[0] = placed[:128].astype(LOW)
    in_ref[0] = placed[128:160]
    gain_ref[0] = placed[160:162] + placed[162:164] + placed[164:166]


def cot_kernel(meta_ref, slot_ref, ids_ref, cot_ref, out_ref, z_ref, rows):
    @pl.when(pl.program_id(0) == 0)
    def _():
        rows[:128] = cot_ref[...]
        rows[128:] = cot_ref[pl.ds(pl.multiple_of(meta_ref[1] * 32, 32), 32)]

    placed = dot(rows[...], one_hot(slot_ref, ids_ref), 1, 0)
    out_ref[0] = placed[:128].astype(LOW)
    z_ref[0] = placed[128:]


def to_slots(kernel, meta, slot, ids, args, outs, rows, name):
    def same(shape):
        return pl.BlockSpec(shape, lambda p: (0, 0))

    return pl.pallas_call(
        kernel,
        grid=(PIECES,),
        in_specs=[
            smem(),
            same((D, 1)),
            pl.BlockSpec((1, 1, LANES), lambda p: (p, 0, 0)),
            *(same(a.shape) for a in args),
        ],
        out_specs=[pl.BlockSpec((1, n, LANES), lambda p: (p, 0, 0)) for n, _ in outs],
        out_shape=[jax.ShapeDtypeStruct((PIECES, n, LANES), kind) for n, kind in outs],
        scratch_shapes=[pltpu.VMEM((rows, D), LOW)],
        compiler_params=pltpu.CompilerParams(vmem_limit_bytes=VMEM),
        cost_estimate=cost(0, 0),
        name=name,
    )(meta, slot, ids, *args)


def tokens_to_slots(meta, slot, ids, tokens, gains, parts):
    outs = [(128, LOW), (32, F32), (2, F32)]
    args = (tokens, gains, parts)
    return to_slots(tokens_kernel, meta, slot, ids, args, outs, 176, "tokens_to_slots")


def cot_to_slots(meta, slot, ids, cotangent):
    outs = [(128, LOW), (32, F32)]
    return to_slots(cot_kernel, meta, slot, ids, (cotangent,), outs, 160, "cotangent_to_slots")


def unplace_kernel(slot_ref, ids_ref, rows_ref, out_ref, acc):
    ids = jnp.transpose(jnp.broadcast_to(ids_ref[0], (8, LANES)))[:, :1]
    place = jnp.where(ids == slot_ref[...], 1.0, 0.0).astype(LOW)

    @pl.when(pl.program_id(0) == 0)
    def _():
        acc[...] = jnp.zeros_like(acc)

    acc[...] += dot(rows_ref[0], place, 1, 0)

    @pl.when(pl.program_id(0) == PIECES - 1)
    def _():
        out_ref[...] = acc[...].astype(LOW)


def from_slots(rows, slot, ids):
    n = rows.shape[1]
    return pl.pallas_call(
        unplace_kernel,
        grid=(PIECES,),
        in_specs=[
            pl.BlockSpec((1, D), lambda p: (0, 0)),
            pl.BlockSpec((1, 1, LANES), lambda p: (p, 0, 0)),
            pl.BlockSpec((1, n, LANES), lambda p: (p, 0, 0)),
        ],
        out_specs=pl.BlockSpec((n, D), lambda p: (0, 0)),
        out_shape=jax.ShapeDtypeStruct((n, D), LOW),
        scratch_shapes=[pltpu.VMEM((n, D), F32)],
        compiler_params=pltpu.CompilerParams(vmem_limit_bytes=VMEM),
        cost_estimate=cost(0, 0),
        name="from_slots",
    )(slot, ids, rows)


def start_weights(meta_ref, refs, held, sems):
    x = meta_ref[2]
    y = meta_ref[3]
    for base, at, group in ((0, y, refs[:4]), (RING, x, refs[4:])):
        for ref, offset in zip(group, OFFSETS):
            p = base + lax.rem(at + offset + RING, RING)
            pltpu.make_async_copy(ref, held.at[p], sems.at[p]).start()


def piece_at(meta_ref, n):
    kind = n // RING
    k = lax.rem(n, RING)
    offset = jnp.where(k == 1, 3, jnp.where(k == 2, 1, jnp.where(k == 3, 2, 0)))
    at = jnp.where(kind == 0, meta_ref[3], meta_ref[2])
    return kind * RING + lax.rem(at + offset, RING)


def wait_weights(held, sems, p):
    pltpu.make_async_copy(held.at[p], held.at[p], sems.at[p]).wait()


def split_rows(value, scratch, core, p, keep_ref, send_ref):
    scratch[:, :BLK] = value.astype(LOW)
    for z in range(RING):
        keep_ref[z, p] = scratch[pl.ds(pl.multiple_of(core * 128 + 32 * z, 32), 32), :]
        send_ref[z, p] = scratch[pl.ds(pl.multiple_of((1 - core) * 128 + 32 * z, 32), 32), :]


def join_rows(is_low, own, got):
    return jnp.concatenate(
        [jnp.where(is_low, own, got), jnp.where(is_low, got, own)], axis=0
    )


def rope(values, cosine, sine):
    half = HD // 2
    turned = jnp.concatenate([-values[:, half:], values[:, :half]], axis=1)
    return values * cosine + turned * sine


def head_probs(query, keys, mask):
    scores = dot(query, keys, 1, 1) * HD ** (-0.5)
    scores = jnp.where(mask, scores, NEG_BIG)
    weight = jnp.exp(scores - jnp.max(scores, axis=1, keepdims=True))
    return weight / jnp.sum(weight, axis=1, keepdims=True)


def causal_mask(seg_col, seg_row):
    rows = lax.broadcasted_iota(jnp.int32, (SEQ, SEQ), 0)
    cols = lax.broadcasted_iota(jnp.int32, (SEQ, SEQ), 1)
    return (seg_col == seg_row) & (cols <= rows)


def attention_kernel(
    meta_ref, own_ref, got_ref, cos_ref, sin_ref, segc_ref, segr_ref, *rest
):
    w_refs = rest[:8]
    q_ref, k_ref, v_ref, o_ref, keep_ref, send_ref, held, acc, part, sems = rest[8:]
    core = meta_ref[0]
    is_low = core == 0
    start_weights(meta_ref, w_refs, held, sems)
    acc[...] = jnp.zeros_like(acc)
    part[:, BLK:] = jnp.zeros((SEQ, LANES - BLK), LOW)

    def project(n, carry):
        p = piece_at(meta_ref, n)
        wait_weights(held, sems, p)
        rows = join_rows(is_low, own_ref[p], got_ref[p])
        acc[...] += dot(rows[:, :BLK], held[p, :, 256:], 1, 0)
        return carry

    lax.fori_loop(0, PIECES, project, 0)
    cosine = cos_ref[...]
    sine = sin_ref[...]
    mask = causal_mask(segc_ref[...], segr_ref[...])
    projected = acc[...]
    keys = rope(projected[:, 384:464], cosine, sine).astype(LOW)
    values = projected[:, 464:544].astype(LOW)
    k_ref[...] = keys
    v_ref[...] = values
    outs = []
    for h in range(HEADS):
        query = rope(projected[:, 64 + h * HD : 64 + (h + 1) * HD], cosine, sine).astype(LOW)
        q_ref[h] = query
        probs = head_probs(query, keys, mask)
        outs.append(dot(probs.astype(LOW), values, 1, 0))
    outs.append(jnp.zeros((SEQ, 64), F32))
    attended = jnp.concatenate(outs, axis=1).astype(LOW)
    o_ref[...] = attended

    def spread(p, carry):
        split_rows(dot(attended, held[p, :, :384], 1, 1), part, core, p, keep_ref, send_ref)
        return carry

    lax.fori_loop(0, PIECES, spread, 0)


def split_shapes():
    return [
        jax.ShapeDtypeStruct((RING, PIECES, 32, LANES), LOW),
        jax.ShapeDtypeStruct((RING, PIECES, 32, LANES), LOW),
    ]


def attention_forward(meta, own, got, tables, segs, w_attn):
    return pl.pallas_call(
        attention_kernel,
        in_specs=[smem()] + [whole()] * 6 + [hbm()] * 8,
        out_specs=[whole()] * 6,
        out_shape=[
            jax.ShapeDtypeStruct((HEADS, SEQ, HD), LOW),
            jax.ShapeDtypeStruct((SEQ, HD), LOW),
            jax.ShapeDtypeStruct((SEQ, HD), LOW),
            jax.ShapeDtypeStruct((SEQ, 384), LOW),
        ]
        + split_shapes(),
        scratch_shapes=[
            pltpu.VMEM((PIECES, BLK, ATTN), LOW),
            pltpu.VMEM((SEQ, ATTN - 256), F32),
            pltpu.VMEM((SEQ, LANES), LOW),
            pltpu.SemaphoreType.DMA((PIECES,)),
        ],
        compiler_params=pltpu.CompilerParams(vmem_limit_bytes=VMEM),
        cost_estimate=cost(0, 0),
        name="attention_forward",
    )(meta, own, got, *tables, *segs, *w_attn)


def put_blocks(ref, value):
    for k in range(RING):
        ref[k] = value[k * HALF : (k + 1) * HALF].astype(LOW)


def attention_back_kernel(
    meta_ref, own_ref, got_ref, cos_ref, sin_ref, segc_ref, segr_ref, q_ref, k_ref, v_ref, o_ref, xc_ref, xc_got_ref, *rest
):
    w_refs = rest[:8]
    keep_ref, send_ref = rest[8:10]
    outs = rest[10:18]
    held, acc, part, sems = rest[18:]
    core = meta_ref[0]
    is_low = core == 0
    start_weights(meta_ref, w_refs, held, sems)
    acc[...] = jnp.zeros_like(acc)
    part[:, BLK:] = jnp.zeros((SEQ, LANES - BLK), LOW)

    def project(n, carry):
        p = piece_at(meta_ref, n)
        wait_weights(held, sems, p)
        own = jnp.concatenate([own_ref[z, p] for z in range(RING)], axis=0)
        got = jnp.concatenate([got_ref[z, p] for z in range(RING)], axis=0)
        acc[...] += dot(join_rows(is_low, own, got)[:, :BLK], held[p, :, :384], 1, 0)
        return carry

    lax.fori_loop(0, PIECES, project, 0)
    cosine = cos_ref[...]
    sine = -sin_ref[...]
    mask = causal_mask(segc_ref[...], segr_ref[...])
    grad_att = acc[...]
    keys = k_ref[...]
    values = v_ref[...]
    factor = HD ** (-0.5)
    grads = []
    grad_keys = jnp.zeros((SEQ, HD), F32)
    grad_values = jnp.zeros((SEQ, HD), F32)
    for h in range(HEADS):
        query = q_ref[h]
        grad_o = grad_att[:, h * HD : (h + 1) * HD].astype(LOW)
        probs = head_probs(query, keys, mask)
        grad_probs = dot(grad_o, values, 1, 1)
        inner = jnp.sum(probs * grad_probs, axis=1, keepdims=True)
        grad_scores = (probs * (grad_probs - inner)).astype(LOW)
        grads.append(rope(dot(grad_scores, keys, 1, 0) * factor, cosine, sine))
        grad_keys += dot(grad_scores, query, 0, 0)
        grad_values += dot(probs.astype(LOW), grad_o, 0, 0)
    grads.append(rope(grad_keys * factor, cosine, sine))
    grads.append(grad_values)
    zeros = [jnp.zeros((SEQ, 64), F32)]
    ends = [jnp.zeros((SEQ, 96), F32)]
    grad_qkv = jnp.concatenate(zeros + grads + ends, axis=1).astype(LOW)

    def spread(p, carry):
        split_rows(dot(grad_qkv, held[p, :, 256:], 1, 1), part, core, p, keep_ref, send_ref)
        return carry

    lax.fori_loop(0, PIECES, spread, 0)

    for kind in range(2):
        for k in range(RING):
            q = kind * RING + lax.rem(meta_ref[3 - kind] + OFFSETS[k] + RING, RING)
            own = jnp.concatenate([own_ref[z, q] for z in range(RING)], axis=0)
            got = jnp.concatenate([got_ref[z, q] for z in range(RING)], axis=0)
            grad = join_rows(is_low, own, got)[:, :BLK]
            xn = join_rows(is_low, xc_ref[q], xc_got_ref[q])[:, :BLK]
            one = dot(grad, o_ref[...], 0, 0)
            two = dot(xn, grad_qkv, 0, 0)
            terms = jnp.concatenate([one[:, :QW], two[:, 64:]], axis=1)
            put_blocks(outs[RING * kind + k], terms)


def attention_backward(meta, own, got, tables, segs, qkvo, xcs, w_attn):
    return pl.pallas_call(
        attention_back_kernel,
        in_specs=[smem()] + [whole()] * 12 + [hbm()] * 8,
        out_specs=[whole()] * 10,
        out_shape=split_shapes() + [jax.ShapeDtypeStruct((RING, HALF, ATTN), LOW)] * 8,
        scratch_shapes=[
            pltpu.VMEM((PIECES, BLK, ATTN), LOW),
            pltpu.VMEM((SEQ, 384), F32),
            pltpu.VMEM((SEQ, LANES), LOW),
            pltpu.SemaphoreType.DMA((PIECES,)),
        ],
        compiler_params=pltpu.CompilerParams(vmem_limit_bytes=VMEM),
        cost_estimate=cost(0, 0),
        name="attention_backward",
    )(meta, own, got, *tables, *segs, *qkvo, *xcs, *w_attn)


def down_back_kernel(meta_ref, cot_own_ref, cot_got_ref, *rest):
    w_refs = rest[:8]
    out_ref, held, sems = rest[8:]
    is_low = meta_ref[0] == 0
    start_weights(meta_ref, w_refs, held, sems)
    out_ref[...] = jnp.zeros_like(out_ref)

    def project(n, carry):
        p = piece_at(meta_ref, n)
        wait_weights(held, sems, p)
        cot = join_rows(is_low, cot_own_ref[p], cot_got_ref[p])
        out_ref[...] += dot(cot[:, :BLK], held[p], 1, 0)
        return carry

    lax.fori_loop(0, PIECES, project, 0)


def down_back(meta, cot_own, cot_got, w_down):
    return pl.pallas_call(
        down_back_kernel,
        in_specs=[smem()] + [whole()] * 2 + [hbm()] * 8,
        out_specs=whole(),
        out_shape=jax.ShapeDtypeStruct((SEQ, FW), F32),
        scratch_shapes=[
            pltpu.VMEM((PIECES, BLK, FW), LOW),
            pltpu.SemaphoreType.DMA((PIECES,)),
        ],
        compiler_params=pltpu.CompilerParams(vmem_limit_bytes=VMEM),
        cost_estimate=cost(0, 0),
        name="down_backward",
    )(meta, cot_own, cot_got, *w_down)


def down_kernel(meta_ref, act_ref, *rest):
    w_refs = rest[:8]
    keep_ref, send_ref, held, part, sems = rest[8:]
    core = meta_ref[0]
    start_weights(meta_ref, w_refs, held, sems)
    part[:, BLK:] = jnp.zeros((SEQ, LANES - BLK), LOW)

    def spread(n, carry):
        p = piece_at(meta_ref, n)
        wait_weights(held, sems, p)
        split_rows(dot(act_ref[...], held[p], 1, 1), part, core, p, keep_ref, send_ref)
        return carry

    lax.fori_loop(0, PIECES, spread, 0)


def down_forward(meta, act, w_down):
    return pl.pallas_call(
        down_kernel,
        in_specs=[smem(), whole()] + [hbm()] * 8,
        out_specs=[whole()] * 2,
        out_shape=split_shapes(),
        scratch_shapes=[
            pltpu.VMEM((PIECES, BLK, FW), LOW),
            pltpu.VMEM((SEQ, LANES), LOW),
            pltpu.SemaphoreType.DMA((PIECES,)),
        ],
        compiler_params=pltpu.CompilerParams(vmem_limit_bytes=VMEM),
        cost_estimate=cost(0, 0),
        name="down_forward",
    )(meta, act, *w_down)


def start_ffn(meta_ref, refs, held, sems):
    x = meta_ref[2]
    y = meta_ref[3]
    for base, at, group in ((0, y, refs[:8]), (RING, x, refs[8:])):
        for k, offset in enumerate(OFFSETS):
            p = base + lax.rem(at + offset + RING, RING)
            for j in range(2):
                into = held.at[p, :, pl.ds(j * FW, FW)]
                pltpu.make_async_copy(group[2 * k + j], into, sems.at[p]).start()


def ffn_kernel(meta_ref, own_ref, got_ref, grad_act_ref, *rest):
    w_refs = rest[:16]
    act_ref, grad_ref, keep_ref, send_ref, held, acc, part, sems = rest[16:]
    core = meta_ref[0]
    is_low = core == 0
    start_ffn(meta_ref, w_refs, held, sems)
    acc[...] = jnp.zeros_like(acc)
    part[:, BLK:] = jnp.zeros((SEQ, LANES - BLK), LOW)

    def project(n, carry):
        p = piece_at(meta_ref, n)
        wait_weights(held, sems, p)
        own = jnp.concatenate([own_ref[z, p] for z in range(RING)], axis=0)
        got = jnp.concatenate([got_ref[z, p] for z in range(RING)], axis=0)
        acc[...] += dot(join_rows(is_low, own, got)[:, :BLK], held[p], 1, 0)
        return carry

    lax.fori_loop(0, PIECES, project, 0)

    def units(t, carry):
        at = pl.multiple_of(t * 128, 128)
        grad_act = grad_act_ref[:, pl.ds(at, 128)]
        gate = acc[:, pl.ds(at, 128)]
        up = acc[:, pl.ds(at + FW, 128)]
        sigmoid = 1.0 / (1.0 + jnp.exp(-gate))
        silu = gate * sigmoid
        act_ref[:, pl.ds(at, 128)] = (silu * up).astype(LOW)
        grad_gate = grad_act * up * sigmoid * (1.0 + gate * (1.0 - sigmoid))
        grad_ref[:, pl.ds(at, 128)] = grad_gate.astype(LOW)
        grad_ref[:, pl.ds(at + FW, 128)] = (grad_act * silu).astype(LOW)
        return carry

    lax.fori_loop(0, FW // 128, units, 0)

    def spread(p, carry):
        split_rows(dot(grad_ref[...], held[p], 1, 1), part, core, p, keep_ref, send_ref)
        return carry

    lax.fori_loop(0, PIECES, spread, 0)


def feed_forward(meta, own, got, grad_act, w_gu):
    return pl.pallas_call(
        ffn_kernel,
        in_specs=[smem()] + [whole()] * 3 + [hbm()] * 16,
        out_specs=[whole()] * 4,
        out_shape=[
            jax.ShapeDtypeStruct((SEQ, FW), LOW),
            jax.ShapeDtypeStruct((SEQ, GU), LOW),
        ]
        + split_shapes(),
        scratch_shapes=[
            pltpu.VMEM((PIECES, BLK, GU), LOW),
            pltpu.VMEM((SEQ, GU), F32),
            pltpu.VMEM((SEQ, LANES), LOW),
            pltpu.SemaphoreType.DMA((PIECES,)),
        ],
        compiler_params=pltpu.CompilerParams(vmem_limit_bytes=VMEM),
        cost_estimate=cost(0, 0),
        name="feed_forward",
    )(meta, own, got, grad_act, *w_gu)


def halves_of(part_ref, xc_ref, q, at):
    rows = jnp.concatenate([part_ref[z, q] for z in range(RING)], axis=0)
    return rows[:, :BLK], xc_ref[q, at : at + 128][:, :BLK]


def merge_kernel(part_ref, xc_ref, one_ref, two_ref):
    for p in range(RING):
        for ref, q in ((one_ref, p), (two_ref, RING + p)):
            for z in range(RING):
                ref[p, 32 * z : 32 * z + 32] = part_ref[z, q]
            ref[p, 128:] = xc_ref[q]


def merge(part, cot):
    return pl.pallas_call(
        merge_kernel,
        in_specs=[whole()] * 2,
        out_specs=[whole()] * 2,
        out_shape=[jax.ShapeDtypeStruct((RING, 256, LANES), LOW)] * 2,
        compiler_params=pltpu.CompilerParams(vmem_limit_bytes=VMEM),
        cost_estimate=cost(0, 0),
        name="merge",
    )(part, cot)


def ffn_terms_kernel(meta_ref, own_ref, got_ref, *rest, axis):
    rights = rest[:8]
    outs = rest[8:12]
    acc = rest[12]
    is_low = meta_ref[0] == 0
    at = meta_ref[axis]
    for k, offset in enumerate(OFFSETS):
        source = lax.rem(at + offset + RING, RING)
        xn = join_rows(is_low, own_ref[source, :128], got_ref[source, :128])[:, :BLK]
        cot = join_rows(is_low, own_ref[source, 128:], got_ref[source, 128:])[:, :BLK]
        down = dot(cot, rights[2 * k][...], 0, 0)
        both = dot(xn, rights[2 * k + 1][...], 0, 0)
        if k == 0:
            acc[:, :FW] = down
            acc[:, FW:] = both
        else:
            acc[:, :FW] += down
            acc[:, FW:] += both
    for k, ref in enumerate(outs):
        ref[:, ATTN:] = acc[k * HALF : (k + 1) * HALF, :].astype(LOW)


def ffn_terms(meta, own, got, rights, axis):
    return pl.pallas_call(
        functools.partial(ffn_terms_kernel, axis=axis),
        in_specs=[smem()] + [whole()] * 10,
        out_specs=[whole()] * 4,
        out_shape=[jax.ShapeDtypeStruct((HALF, WIDE), LOW)] * 4,
        scratch_shapes=[pltpu.VMEM((BLK, 3 * FW), F32)],
        compiler_params=pltpu.CompilerParams(vmem_limit_bytes=VMEM),
        cost_estimate=cost(0, 0),
        name="terms_feed_forward",
    )(meta, own, got, *rights)


def fill_kernel(*refs):
    for k, ref in enumerate(refs[8:]):
        total = refs[0][k].astype(F32)
        for part in refs[1:4]:
            total = total + part[k].astype(F32)
        ref[...] = total.astype(LOW)


def fill(attn, ffn):
    return pl.pallas_call(
        fill_kernel,
        grid=(1,),
        in_specs=[pl.BlockSpec((RING, HALF, ATTN), lambda i: (0, 0, 0))] * 4 + [hbm()] * 4,
        out_specs=[pl.BlockSpec((HALF, ATTN), lambda i: (0, 0))] * 4,
        out_shape=[jax.ShapeDtypeStruct((HALF, WIDE), LOW)] * 4,
        input_output_aliases={4 + k: k for k in range(4)},
        compiler_params=pltpu.CompilerParams(vmem_limit_bytes=VMEM),
        cost_estimate=cost(0, 0),
        name="fill",
    )(*attn, *ffn)


def fetch_kind(is_first, refs, held, sem):
    for kind in range(2):

        @pl.when(is_first if kind == 0 else jnp.logical_not(is_first))
        def _():
            for k in range(RING):
                pltpu.make_async_copy(refs[RING * kind + k], held.at[k], sem).start()

    pltpu.make_async_copy(held, held, sem).wait()


def finish_kernel(meta_ref, *refs):
    out_ref, held, sem = refs[8:]
    fetch_kind(meta_ref[0] == 1, refs[:8], held, sem)
    total = held[0].astype(F32)
    for k in range(1, RING):
        total = total + held[k].astype(F32)
    out_ref[...] = total.astype(LOW)


def finish(meta, parts):
    return pl.pallas_call(
        finish_kernel,
        in_specs=[smem()] + [hbm()] * 8,
        out_specs=whole(),
        out_shape=jax.ShapeDtypeStruct((HALF, WIDE), LOW),
        scratch_shapes=[pltpu.VMEM((RING, HALF, WIDE), LOW), pltpu.SemaphoreType.DMA],
        compiler_params=pltpu.CompilerParams(vmem_limit_bytes=VMEM),
        cost_estimate=cost(0, 0),
        name="finish_other",
    )(meta, *parts[0], *parts[1])


def pick_sum(is_first, refs):
    total = jnp.where(is_first, refs[0][...], refs[4][...]).astype(F32)
    for k in range(1, 4):
        total = total + jnp.where(is_first, refs[k][...], refs[4 + k][...]).astype(F32)
    return total


def adam_kernel(meta_ref, w_ref, m_ref, v_ref, came, *rest):
    parts = rest[:8]
    wo_ref, mo_ref, vo_ref, grad, stay = rest[8:]
    is_low = meta_ref[0] == 0
    stay[...] = pick_sum(is_low, parts)
    rows = w_ref.shape[0]
    for start, at, width in MAP:
        mine = stay[:, at : at + width]
        other = came[:, at : at + width].astype(F32)
        grad[:, start : start + width] = jnp.where(is_low, mine, other)
        grad[:, start + width : start + 2 * width] = jnp.where(is_low, other, mine)
    row = pl.program_id(0) * rows + lax.broadcasted_iota(jnp.int32, (rows, 1), 0)
    valid = row < meta_ref[4]
    weight, first, second = adam_step(
        w_ref[...], m_ref[...], v_ref[...], grad[...], LEARN, DECAY
    )
    wo_ref[...] = jnp.where(valid, weight, 0.0)
    mo_ref[...] = jnp.where(valid, first, 0.0)
    vo_ref[...] = jnp.where(valid, second, 0.0)


def adam(meta, master, moment_one, moment_two, came, parts):
    rows = 32
    units = master.shape[1]

    def block(width):
        return pl.BlockSpec((rows, width), lambda i: (i, 0))

    return pl.pallas_call(
        adam_kernel,
        grid=(pl.cdiv(HALF, rows),),
        in_specs=[smem()] + [block(units)] * 3 + [block(WIDE)] * 9,
        out_specs=[block(units)] * 3,
        out_shape=[jax.ShapeDtypeStruct(master.shape, F32)] * 3,
        scratch_shapes=[pltpu.VMEM((rows, units), F32), pltpu.VMEM((rows, WIDE), F32)],
        compiler_params=pltpu.CompilerParams(vmem_limit_bytes=VMEM),
        name="adam",
    )(meta, master, moment_one, moment_two, came, *parts[0], *parts[1])


def rms_scale(values):
    return lax.rsqrt(jnp.sum(values * values, axis=(0, 2), keepdims=True) / D + EPS_NORM)


def rms_backward(grad_out, normed, scale, gain):
    grad_normed = grad_out * gain
    inner = jnp.sum(grad_normed * normed, axis=(0, 2), keepdims=True) / D
    return scale * (grad_normed - normed * inner), jnp.sum(grad_out * normed, axis=1)


def adam_step(weight, first, second, grad, rate, decay):
    first_new = BETA * first + (1.0 - BETA) * grad
    second_new = BETA * second + (1.0 - BETA) * grad * grad
    inverse = 1.0 / (1.0 - BETA**STEP)
    update = (first_new * inverse) / (jnp.sqrt(second_new * inverse) + EPS_ADAM)
    return (weight - rate * (update + decay * weight), first_new, second_new)


def stage(*values):
    return lax.optimization_barrier(values)


def shards(
    tokens, cotangent, segments, owner, master, moment_one, moment_two, gains, gain_one, gain_two
):
    core = lax.axis_index("core")
    yl = lax.axis_index("yl")
    z = lax.axis_index("z")
    x = lax.axis_index(X)
    y = lax.axis_index("yh") * 2 + yl
    count = jnp.sum((owner == (y // 2 * RING + x) * 2 + core).astype(jnp.int32)) - yl * HALF
    place = jnp.stack([core, z, x, y]).astype(jnp.int32)
    meta = jnp.stack([core, z, x, y, count]).astype(jnp.int32)
    along = (Y, X)
    across = (X, Y)

    def add_core(keep, other):
        return (keep.astype(F32) + other.astype(F32)).astype(LOW)

    def split_z(block):
        return lax.all_to_all(block, "z", split_axis=0, concat_axis=0, tiled=True)

    def sum_z(block):
        return jnp.sum(block.astype(F32), axis=0)

    def all_z(block):
        return split_z(jnp.broadcast_to(block[None], (RING, *block.shape)))

    own, send = pack(place, owner, master)
    got = swap_core(send)
    first = jnp.where(core == 0, own, got)
    second = jnp.where(core == 0, got, own)
    first, second, owner, tokens, cotangent = stage(first, second, owner, tokens, cotangent)

    near_first = near(first, X)
    near_second = near(second, Y)
    numbers = jnp.zeros((8, D), LOW).at[0, :SEQ].set(segments.astype(LOW))
    tokens = swap_sequences(jnp.concatenate([tokens, numbers], axis=0))
    onehot = (owner[:, None] == jnp.arange(16, dtype=jnp.int32)[None, :]).astype(jnp.int32)
    rank = jnp.sum((jnp.cumsum(onehot, axis=0) - onehot) * onehot, axis=1)
    slot = (owner * CAP + rank)[:, None]
    ids = slot_ids(x, y)
    parts = jnp.concatenate([three_parts(gains), jnp.zeros((10, D), LOW)], axis=0)
    near_first, near_second, slot, ids, parts, cotangent = stage(
        near_first, near_second, slot, ids, parts, cotangent
    )

    blocks = [
        (first, *near_first, *halves(*near_first, X, WIDE_CUT)),
        (second, *near_second, *halves(*near_second, Y, WIDE_CUT)),
    ]
    attn = [assemble(b, 0) for b in blocks]
    attn, blocks, tokens, cotangent = stage(attn, blocks, tokens, cotangent)

    attn_near = [near(b, axis) for b, axis in zip(attn, along)]
    position = jnp.arange(SEQ, dtype=F32)
    freq = jnp.exp(-jnp.log(THETA) * (2.0 * jnp.arange(HD // 2, dtype=F32) / HD))
    angle = position[:, None] * freq[None, :]
    tables = (
        jnp.concatenate([jnp.cos(angle)] * 2, axis=1),
        jnp.concatenate([jnp.sin(angle)] * 2, axis=1),
    )
    segment = tokens[128, :SEQ].astype(jnp.int32)
    segs = (segment[:, None], segment[None, :])
    down = [assemble(b, 1) for b in blocks]
    cotangent = swap_sequences(cotangent)
    attn_near, down, tables, segs, tokens, cotangent = stage(
        attn_near, down, tables, segs, tokens, cotangent
    )
    down_near = [near(b, axis) for b, axis in zip(down, along)]
    xn_own, inputs, gain = tokens_to_slots(meta, slot, ids, tokens, gains, parts)
    gate = [assemble(b, 2) for b in blocks]
    turned = (slot.reshape(1, D), ids)
    down_near, blocks, gate, turned, xn_own, inputs, gain, cotangent = stage(
        down_near, blocks, gate, turned, xn_own, inputs, gain, cotangent
    )
    pair_far = [far(q[0], d[1], axis) for q, d, axis in zip(attn_near, down_near, along)]
    up = [assemble(b, 3) for b in blocks]
    xn_got = swap_core(xn_own)
    cot_own, cot_z = cot_to_slots(meta, slot, ids, cotangent)
    pair_far, gate, up, xn_got, cot_own, cot_z = stage(pair_far, gate, up, xn_got, cot_own, cot_z)
    w_attn = []
    w_down = []
    for kind in range(2):
        w_attn += [attn[kind], *attn_near[kind], pair_far[kind][0]]
        w_down += [down[kind], *down_near[kind], pair_far[kind][1]]

    gate_near = [near(b, axis) for b, axis in zip(gate, along)]
    *qkv, attended, keep, send = attention_forward(meta, xn_own, xn_got, tables, segs, w_attn)
    cot_got = swap_core(cot_own)
    gate_near, up, keep, send, cot_got = stage(gate_near, up, keep, send, cot_got)
    up_near = [near(b, axis) for b, axis in zip(up, along)]
    got = split_z(add_core(keep, swap_core(send)))
    grad_act = down_back(meta, cot_own, cot_got, w_down)
    up_near, gate_near, got, grad_act = stage(up_near, gate_near, got, grad_act)
    gu_far = [far(g[0], u[1], axis) for g, u, axis in zip(gate_near, up_near, along)]
    hidden = inputs + sum_z(got)
    scale_two = rms_scale(hidden)
    normed_two = hidden * scale_two
    xn_two = all_z((normed_two * gain[:, 1:2]).astype(LOW))
    gu_far, xn_two = stage(gu_far, xn_two)
    xn_two_got = swap_core(xn_two)
    left_sent = merge(xn_two, cot_own)
    xn_two, xn_two_got, grad_act, left_sent = stage(xn_two, xn_two_got, grad_act, left_sent)
    w_gu = []
    for kind in range(2):
        w_gu += [gate[kind], up[kind]]
        w_gu += [gate_near[kind][0], up_near[kind][0], gate_near[kind][1], up_near[kind][1]]
        w_gu += [*gu_far[kind]]

    act, grad_gu, keep, send = feed_forward(meta, xn_two, xn_two_got, grad_act, w_gu)
    def exchange(block, axis):
        return lax.all_to_all(block, axis, split_axis=0, concat_axis=0, tiled=True)

    lefts = [exchange(left_sent[0], Y)]
    act, grad_gu, keep, send, lefts = stage(act, grad_gu, keep, send, lefts)
    gu_near = [near(grad_gu, axis) for axis in along]
    got = split_z(add_core(keep, swap_core(send)))
    keep_mlp, send_mlp = down_forward(meta, act, w_down)
    gu_near, got, keep_mlp, send_mlp, act = stage(gu_near, got, keep_mlp, send_mlp, act)
    act_near = [near(act, axis) for axis in along]
    lefts_got = [swap_core(lefts[0])]
    mlp_both = add_core(keep_mlp, swap_core(send_mlp))
    grad_xn_two = sum_z(got)
    grad_norm_two, gain_grad_two = rms_backward(grad_xn_two, normed_two, scale_two, gain[:, 1:2])
    grad_hidden = cot_z + grad_norm_two
    grad_branch = all_z(grad_hidden.astype(LOW))
    act_near, grad_branch, grad_hidden, gain_grad_two, left_sent, lefts_got, gu_near, mlp_both = stage(
        act_near, grad_branch, grad_hidden, gain_grad_two, left_sent, lefts_got, gu_near, mlp_both
    )
    grad_branch_got = swap_core(grad_branch)
    ends = [far(a[0], g[1], axis) for a, g, axis in zip(act_near, gu_near, along)]
    lefts.append(exchange(left_sent[1], X))

    xns = (xn_own, xn_got)
    keep, send, *terms = attention_backward(
        meta, grad_branch, grad_branch_got, tables, segs, (*qkv, attended), xns, w_attn
    )
    attn_terms = (terms[:4], terms[4:])
    mlp = lax.psum_scatter(mlp_both, "z", scatter_dimension=0, tiled=True)[0]
    ends, keep, send, attn_terms, lefts, mlp = stage(ends, keep, send, attn_terms, lefts, mlp)

    def direct(first, second, axes):
        _, back, ahead, last = first
        _, back_two, ahead_two, last_two = second
        one = (move(ahead, axes[0], 1), move(back, axes[0], -1), move(last, axes[0], 2))
        up = move(ahead_two, axes[1], 1)
        down = move(back_two, axes[1], -1)
        return one, up, down, last_two

    attn_nears = [
        (move(t[2], axis, 1), move(t[1], axis, -1)) for t, axis in zip(attn_terms, along)
    ]

    def rights_of(kind):
        rights = (act, grad_gu)
        for n in range(2):
            rights += (act_near[kind][n], gu_near[kind][n])
        return rights + tuple(ends[kind])

    ffn_sums = [ffn_terms(meta, lefts[0], lefts_got[0], rights_of(0), 3)]
    lefts_got.append(swap_core(lefts[1]))
    got = split_z(add_core(keep, swap_core(send)))
    attn_nears, attn_terms, lefts, lefts_got, ffn_sums, got = stage(
        attn_nears, attn_terms, lefts, lefts_got, ffn_sums, got
    )
    attn_others = [
        (*n, move(t[3], axis, 2)) for n, t, axis in zip(attn_nears, attn_terms, along)
    ]
    ffn_sums.append(ffn_terms(meta, lefts[1], lefts_got[1], rights_of(1), 2))
    grad_xn_one = sum_z(got)
    scale_one = rms_scale(inputs)
    grad_norm_one, gain_grad_one = rms_backward(
        grad_xn_one, inputs * scale_one, scale_one, gain[:, 0:1]
    )
    grad_tokens_z = (grad_hidden + grad_norm_one).astype(LOW)
    output_z = (hidden + mlp.astype(F32)).astype(LOW)
    gain_grads = three_parts(jnp.stack([gain_grad_one, gain_grad_two], axis=0))
    gain_grads = jnp.swapaxes(gain_grads, 0, 1)
    blank = jnp.zeros((PIECES, 10, LANES), LOW)
    last = from_slots(
        jnp.concatenate([output_z, grad_tokens_z, gain_grads, blank], axis=1), *turned
    )
    attn_others, ffn_sums, last = stage(attn_others, ffn_sums, last)
    blocks = [fill((t[0], *o), f) for t, o, f in zip(attn_terms, attn_others, ffn_sums)]
    part = lax.all_gather(last, "z", axis=0, tiled=False)
    one, up, down, last_two = direct(*blocks, across)
    up, down, last_two = stage(up, down, last_two)
    others = (one, (up, down, move(last_two, across[1], 2)))
    others, owns = stage(others, [b[0] for b in blocks])
    totals = [(b, *o) for b, o in zip(owns, others)]
    send, totals = stage(finish(meta, totals), totals)
    came = swap_core(send)
    moved = swap_sequences(jnp.swapaxes(part[:, :64].reshape(RING, 2, 32, D), 0, 1))
    gain_grads = part[:, 64:70].astype(F32).sum(axis=0)
    gain_grads = gain_grads[:2] + gain_grads[2:4] + gain_grads[4:6]
    gain_other = swap_core(gain_grads)
    came, gain_other, totals = stage(came, gain_other, totals)

    def sum_along(value, axis):
        back, ahead = near(value, axis)
        return (value + move(value, axis, 2)) + (back + ahead)

    gain_grads = sum_along(gain_grads + gain_other, X)
    new_master, new_one, new_two = adam(meta, master, moment_one, moment_two, came, totals)
    gain_grads, new_master, moved = stage(gain_grads, new_master, moved)
    gain_grads = sum_along(gain_grads, Y)
    output = moved[0].reshape(128, D)
    grad_tokens = moved[1].reshape(128, D)
    new_gains, new_gain_one, new_gain_two = adam_step(
        gains, gain_one, gain_two, gain_grads, LEARN_GAIN, 0.0
    )
    return (
        output,
        grad_tokens,
        new_master,
        new_one,
        new_two,
        new_gains,
        new_gain_one,
        new_gain_two,
    )


def solution(mesh):
    fine = Mesh(mesh.devices.reshape(2, 4, 2, 2, 4), ("yh", "x", "core", "yl", "z"))
    rows = ("yh", "x", "core", "yl")
    in_specs = (
        P(rows, None),
        P(rows, None),
        P(("yh", "x", "core")),
        P(),
        P(rows, "z"),
        P(rows, "z"),
        P(rows, "z"),
        P(),
        P(),
        P(),
    )
    out_specs = (
        P(rows, None),
        P(rows, None),
        P(rows, "z"),
        P(rows, "z"),
        P(rows, "z"),
        P(),
        P(),
        P(),
    )
    return jax.shard_map(shards, mesh=fine, in_specs=in_specs, out_specs=out_specs, check_vma=False)
```

```python
import functools

import jax
import jax.numpy as jnp
from jax import lax
from jax.experimental import pallas as pl
from jax.experimental.pallas import tpu as pltpu
from jax.sharding import Mesh
from jax.sharding import PartitionSpec as P

HD = 80
STEP = 5
D = 2560
CAP = 240
HALF = 120
SEQ = 256
RING = 4

EPS_NORM = 1e-05
EPS_ADAM = 1e-08
THETA = 1000000.0
BETA = 0.5
LEARN = 0.05
LEARN_GAIN = 0.2
DECAY = 0.1
NEG_BIG = -1e30

X = "x"
Y = ("yh", "yl")
OFFSETS = (0, -1, 1, 2)
LOW = jnp.bfloat16
F32 = jnp.float32

HEADS = 4
QW = 320
KW = 80
FW = 896
ATTN = 896
GU = 2 * FW
WIDE = ATTN + 3 * FW
WIDE_CUT = 1792
MAP = (
    (0, 320, QW),
    (640, 640, KW),
    (800, 720, KW),
    (960, 1792, FW),
    (2752, 2688, FW),
    (4544, 0, QW),
    (5184, 896, FW),
)
PIECES = 8
BLK = 4 * HALF
LANES = 512
VMEM = 60 * 1024 * 1024


def dot(left, right, left_axis, right_axis):
    return lax.dot_general(
        left, right, (((left_axis,), (right_axis,)), ((), ())), preferred_element_type=F32
    )


def move(block, axis, distance):
    route = [(i, (i + distance) % RING) for i in range(RING)]
    return lax.ppermute(block, axis, route)


def swap_core(block):
    return lax.ppermute(block, "core", [(0, 1), (1, 0)])


def swap_sequences(block):
    return lax.ppermute(block, ("core", "yl"), [(0, 0), (1, 2), (2, 1), (3, 3)])


def near(block, axis):
    return move(block, axis, 1), move(block, axis, -1)


def far(back, ahead, axis):
    return move(back, axis, 1), move(ahead, axis, -1)


def halves(back, ahead, axis, cut):
    return far(back[:, :cut], ahead[:, cut:], axis)


def slot_ids(x, y):
    offsets = jnp.array(OFFSETS, jnp.int32)
    every = jnp.arange(RING, dtype=jnp.int32)
    rows = jnp.arange(HALF, dtype=jnp.int32)

    def slots(xx, yy, core):
        return (((yy // 2) * RING + xx) * 2 + core) * CAP + (yy % 2) * HALF

    first = slots(((x + offsets) % RING)[None, :, None], every[:, None, None], 0) + rows
    second = slots(every[:, None, None], ((y + offsets) % RING)[None, :, None], 1) + rows
    ids = jnp.concatenate([first, second], axis=0).reshape(PIECES, 1, BLK)
    return jnp.pad(ids, ((0, 0), (0, 0), (0, LANES - BLK)), constant_values=-1)


def three_parts(values):
    high = lax.reduce_precision(values, 8, 7)
    rest = values - high
    middle = lax.reduce_precision(rest, 8, 7)
    return jnp.concatenate([high, middle, rest - middle], axis=0).astype(LOW)


def whole():
    return pl.BlockSpec(memory_space=pltpu.VMEM)


def hbm():
    return pl.BlockSpec(memory_space=pl.ANY)


def smem():
    return pl.BlockSpec(memory_space=pltpu.SMEM)


def cost(flops, size):
    return pl.CostEstimate(flops=flops, bytes_accessed=size, transcendentals=0)


def pack_kernel(meta_ref, owner_ref, master_ref, own_ref, send_ref):
    is_low = meta_ref[0] == 0
    share = (meta_ref[3] // 2 * RING + meta_ref[2]) * 2 + meta_ref[0]
    count = jnp.sum((owner_ref[...] == share).astype(jnp.int32)) - lax.rem(meta_ref[3], 2) * HALF
    valid = lax.broadcasted_iota(jnp.int32, (HALF, 1), 0) < count
    blank = jnp.zeros((HALF, ATTN - 800), LOW)
    own_ref[:, 800:ATTN] = blank
    send_ref[:, 800:ATTN] = blank
    for start, at, width in MAP:
        low = jnp.where(valid, master_ref[:, start : start + width], 0.0)
        high = jnp.where(valid, master_ref[:, start + width : start + 2 * width], 0.0)
        own_ref[:, at : at + width] = jnp.where(is_low, low, high).astype(LOW)
        send_ref[:, at : at + width] = jnp.where(is_low, high, low).astype(LOW)


def pack(meta, owner, master):
    return pl.pallas_call(
        pack_kernel,
        in_specs=[smem(), whole(), whole()],
        out_specs=[whole()] * 2,
        out_shape=[jax.ShapeDtypeStruct((HALF, WIDE), LOW)] * 2,
        compiler_params=pltpu.CompilerParams(vmem_limit_bytes=VMEM),
        name="pack",
    )(meta, owner.reshape(20, 128), master)


def assemble_kernel(*refs):
    out = refs[4]
    for k, ref in enumerate(refs[:4]):
        out[k * HALF : (k + 1) * HALF, :] = ref[...]


def assemble(blocks, j):
    block, back, ahead, one, two = blocks
    specs = [pl.BlockSpec((HALF, FW), lambda i: (0, j))] * 3
    specs += [pl.BlockSpec((HALF, FW), lambda i: (0, j % 2))]
    return pl.pallas_call(
        assemble_kernel,
        grid=(1,),
        in_specs=specs,
        out_specs=pl.BlockSpec((BLK, FW), lambda i: (0, 0)),
        out_shape=jax.ShapeDtypeStruct((BLK, FW), LOW),
        compiler_params=pltpu.CompilerParams(vmem_limit_bytes=VMEM),
        cost_estimate=cost(0, 0),
        name="assemble",
    )(block, back, ahead, one if j < 2 else two)


def one_hot(slot_ref, ids_ref):
    return jnp.where(slot_ref[...] == ids_ref[0], 1.0, 0.0).astype(LOW)


def tokens_kernel(meta_ref, slot_ref, ids_ref, tokens_ref, gains_ref, parts_ref, xn_ref, in_ref, gain_ref, rows):
    @pl.when(pl.program_id(0) == 0)
    def _():
        at = pl.multiple_of(meta_ref[1] * 32, 32)
        tokens = tokens_ref[:128].astype(F32)
        scale = lax.rsqrt(jnp.sum(tokens * tokens, axis=1, keepdims=True) / D + EPS_NORM)
        rows[:128] = (tokens * scale * gains_ref[0:1]).astype(LOW)
        rows[128:160] = tokens_ref[pl.ds(at, 32)]
        rows[160:] = parts_ref[...]

    placed = dot(rows[...], one_hot(slot_ref, ids_ref), 1, 0)
    xn_ref[0] = placed[:128].astype(LOW)
    in_ref[0] = placed[128:160]
    gain_ref[0] = placed[160:162] + placed[162:164] + placed[164:166]


def cot_kernel(meta_ref, slot_ref, ids_ref, cot_ref, out_ref, z_ref, rows):
    @pl.when(pl.program_id(0) == 0)
    def _():
        rows[:128] = cot_ref[...]
        rows[128:] = cot_ref[pl.ds(pl.multiple_of(meta_ref[1] * 32, 32), 32)]

    placed = dot(rows[...], one_hot(slot_ref, ids_ref), 1, 0)
    out_ref[0] = placed[:128].astype(LOW)
    z_ref[0] = placed[128:]


def to_slots(kernel, meta, slot, ids, args, outs, rows, name):
    def same(shape):
        return pl.BlockSpec(shape, lambda p: (0, 0))

    return pl.pallas_call(
        kernel,
        grid=(PIECES,),
        in_specs=[
            smem(),
            same((D, 1)),
            pl.BlockSpec((1, 1, LANES), lambda p: (p, 0, 0)),
            *(same(a.shape) for a in args),
        ],
        out_specs=[pl.BlockSpec((1, n, LANES), lambda p: (p, 0, 0)) for n, _ in outs],
        out_shape=[jax.ShapeDtypeStruct((PIECES, n, LANES), kind) for n, kind in outs],
        scratch_shapes=[pltpu.VMEM((rows, D), LOW)],
        compiler_params=pltpu.CompilerParams(vmem_limit_bytes=VMEM),
        cost_estimate=cost(0, 0),
        name=name,
    )(meta, slot, ids, *args)


def tokens_to_slots(meta, slot, ids, tokens, gains, parts):
    outs = [(128, LOW), (32, F32), (2, F32)]
    args = (tokens, gains, parts)
    return to_slots(tokens_kernel, meta, slot, ids, args, outs, 176, "tokens_to_slots")


def cot_to_slots(meta, slot, ids, cotangent):
    outs = [(128, LOW), (32, F32)]
    return to_slots(cot_kernel, meta, slot, ids, (cotangent,), outs, 160, "cotangent_to_slots")


def unplace_kernel(slot_ref, ids_ref, rows_ref, out_ref, acc):
    ids = jnp.transpose(jnp.broadcast_to(ids_ref[0], (8, LANES)))[:, :1]
    place = jnp.where(ids == slot_ref[...], 1.0, 0.0).astype(LOW)

    @pl.when(pl.program_id(0) == 0)
    def _():
        acc[...] = jnp.zeros_like(acc)

    acc[...] += dot(rows_ref[0], place, 1, 0)

    @pl.when(pl.program_id(0) == PIECES - 1)
    def _():
        out_ref[...] = acc[...].astype(LOW)


def from_slots(rows, slot, ids):
    n = rows.shape[1]
    return pl.pallas_call(
        unplace_kernel,
        grid=(PIECES,),
        in_specs=[
            pl.BlockSpec((1, D), lambda p: (0, 0)),
            pl.BlockSpec((1, 1, LANES), lambda p: (p, 0, 0)),
            pl.BlockSpec((1, n, LANES), lambda p: (p, 0, 0)),
        ],
        out_specs=pl.BlockSpec((n, D), lambda p: (0, 0)),
        out_shape=jax.ShapeDtypeStruct((n, D), LOW),
        scratch_shapes=[pltpu.VMEM((n, D), F32)],
        compiler_params=pltpu.CompilerParams(vmem_limit_bytes=VMEM),
        cost_estimate=cost(0, 0),
        name="from_slots",
    )(slot, ids, rows)


def start_weights(meta_ref, refs, held, sems):
    x = meta_ref[2]
    y = meta_ref[3]
    for base, at, group in ((0, y, refs[:4]), (RING, x, refs[4:])):
        for ref, offset in zip(group, OFFSETS):
            p = base + lax.rem(at + offset + RING, RING)
            pltpu.make_async_copy(ref, held.at[p], sems.at[p]).start()


def piece_at(meta_ref, n):
    kind = n // RING
    k = lax.rem(n, RING)
    offset = jnp.where(k == 1, 3, jnp.where(k == 2, 1, jnp.where(k == 3, 2, 0)))
    at = jnp.where(kind == 0, meta_ref[3], meta_ref[2])
    return kind * RING + lax.rem(at + offset, RING)


def wait_weights(held, sems, p):
    pltpu.make_async_copy(held.at[p], held.at[p], sems.at[p]).wait()


def split_rows(value, scratch, core, p, keep_ref, send_ref):
    scratch[:, :BLK] = value.astype(LOW)
    for z in range(RING):
        keep_ref[z, p] = scratch[pl.ds(pl.multiple_of(core * 128 + 32 * z, 32), 32), :]
        send_ref[z, p] = scratch[pl.ds(pl.multiple_of((1 - core) * 128 + 32 * z, 32), 32), :]


def join_rows(is_low, own, got):
    return jnp.concatenate(
        [jnp.where(is_low, own, got), jnp.where(is_low, got, own)], axis=0
    )


def rope(values, cosine, sine):
    half = HD // 2
    turned = jnp.concatenate([-values[:, half:], values[:, :half]], axis=1)
    return values * cosine + turned * sine


def head_probs(query, keys, mask):
    scores = dot(query, keys, 1, 1) * HD ** (-0.5)
    scores = jnp.where(mask, scores, NEG_BIG)
    weight = jnp.exp(scores - jnp.max(scores, axis=1, keepdims=True))
    return weight / jnp.sum(weight, axis=1, keepdims=True)


def causal_mask(seg_col, seg_row):
    rows = lax.broadcasted_iota(jnp.int32, (SEQ, SEQ), 0)
    cols = lax.broadcasted_iota(jnp.int32, (SEQ, SEQ), 1)
    return (seg_col == seg_row) & (cols <= rows)


def attention_kernel(
    meta_ref, own_ref, got_ref, cos_ref, sin_ref, segc_ref, segr_ref, *rest
):
    w_refs = rest[:8]
    q_ref, k_ref, v_ref, o_ref, keep_ref, send_ref, held, acc, part, sems = rest[8:]
    core = meta_ref[0]
    is_low = core == 0
    start_weights(meta_ref, w_refs, held, sems)
    acc[...] = jnp.zeros_like(acc)
    part[:, BLK:] = jnp.zeros((SEQ, LANES - BLK), LOW)

    def project(n, carry):
        p = piece_at(meta_ref, n)
        wait_weights(held, sems, p)
        rows = join_rows(is_low, own_ref[p], got_ref[p])
        acc[...] += dot(rows[:, :BLK], held[p, :, 256:], 1, 0)
        return carry

    lax.fori_loop(0, PIECES, project, 0)
    cosine = cos_ref[...]
    sine = sin_ref[...]
    mask = causal_mask(segc_ref[...], segr_ref[...])
    projected = acc[...]
    keys = rope(projected[:, 384:464], cosine, sine).astype(LOW)
    values = projected[:, 464:544].astype(LOW)
    k_ref[...] = keys
    v_ref[...] = values
    outs = []
    for h in range(HEADS):
        query = rope(projected[:, 64 + h * HD : 64 + (h + 1) * HD], cosine, sine).astype(LOW)
        q_ref[h] = query
        probs = head_probs(query, keys, mask)
        outs.append(dot(probs.astype(LOW), values, 1, 0))
    outs.append(jnp.zeros((SEQ, 64), F32))
    attended = jnp.concatenate(outs, axis=1).astype(LOW)
    o_ref[...] = attended

    def spread(p, carry):
        split_rows(dot(attended, held[p, :, :384], 1, 1), part, core, p, keep_ref, send_ref)
        return carry

    lax.fori_loop(0, PIECES, spread, 0)


def split_shapes():
    return [
        jax.ShapeDtypeStruct((RING, PIECES, 32, LANES), LOW),
        jax.ShapeDtypeStruct((RING, PIECES, 32, LANES), LOW),
    ]


def attention_forward(meta, own, got, tables, segs, w_attn):
    return pl.pallas_call(
        attention_kernel,
        in_specs=[smem()] + [whole()] * 6 + [hbm()] * 8,
        out_specs=[whole()] * 6,
        out_shape=[
            jax.ShapeDtypeStruct((HEADS, SEQ, HD), LOW),
            jax.ShapeDtypeStruct((SEQ, HD), LOW),
            jax.ShapeDtypeStruct((SEQ, HD), LOW),
            jax.ShapeDtypeStruct((SEQ, 384), LOW),
        ]
        + split_shapes(),
        scratch_shapes=[
            pltpu.VMEM((PIECES, BLK, ATTN), LOW),
            pltpu.VMEM((SEQ, ATTN - 256), F32),
            pltpu.VMEM((SEQ, LANES), LOW),
            pltpu.SemaphoreType.DMA((PIECES,)),
        ],
        compiler_params=pltpu.CompilerParams(vmem_limit_bytes=VMEM),
        cost_estimate=cost(0, 0),
        name="attention_forward",
    )(meta, own, got, *tables, *segs, *w_attn)


def put_blocks(ref, value):
    for k in range(RING):
        ref[k] = value[k * HALF : (k + 1) * HALF].astype(LOW)


def attention_back_kernel(
    meta_ref, own_ref, got_ref, cos_ref, sin_ref, segc_ref, segr_ref, q_ref, k_ref, v_ref, o_ref, xc_ref, xc_got_ref, *rest
):
    w_refs = rest[:8]
    keep_ref, send_ref = rest[8:10]
    outs = rest[10:18]
    held, acc, part, sems = rest[18:]
    core = meta_ref[0]
    is_low = core == 0
    start_weights(meta_ref, w_refs, held, sems)
    acc[...] = jnp.zeros_like(acc)
    part[:, BLK:] = jnp.zeros((SEQ, LANES - BLK), LOW)

    def project(n, carry):
        p = piece_at(meta_ref, n)
        wait_weights(held, sems, p)
        own = jnp.concatenate([own_ref[z, p] for z in range(RING)], axis=0)
        got = jnp.concatenate([got_ref[z, p] for z in range(RING)], axis=0)
        acc[...] += dot(join_rows(is_low, own, got)[:, :BLK], held[p, :, :384], 1, 0)
        return carry

    lax.fori_loop(0, PIECES, project, 0)
    cosine = cos_ref[...]
    sine = -sin_ref[...]
    mask = causal_mask(segc_ref[...], segr_ref[...])
    grad_att = acc[...]
    keys = k_ref[...]
    values = v_ref[...]
    factor = HD ** (-0.5)
    grads = []
    grad_keys = jnp.zeros((SEQ, HD), F32)
    grad_values = jnp.zeros((SEQ, HD), F32)
    for h in range(HEADS):
        query = q_ref[h]
        grad_o = grad_att[:, h * HD : (h + 1) * HD].astype(LOW)
        probs = head_probs(query, keys, mask)
        grad_probs = dot(grad_o, values, 1, 1)
        inner = jnp.sum(probs * grad_probs, axis=1, keepdims=True)
        grad_scores = (probs * (grad_probs - inner)).astype(LOW)
        grads.append(rope(dot(grad_scores, keys, 1, 0) * factor, cosine, sine))
        grad_keys += dot(grad_scores, query, 0, 0)
        grad_values += dot(probs.astype(LOW), grad_o, 0, 0)
    grads.append(rope(grad_keys * factor, cosine, sine))
    grads.append(grad_values)
    zeros = [jnp.zeros((SEQ, 64), F32)]
    ends = [jnp.zeros((SEQ, 96), F32)]
    grad_qkv = jnp.concatenate(zeros + grads + ends, axis=1).astype(LOW)

    def spread(p, carry):
        split_rows(dot(grad_qkv, held[p, :, 256:], 1, 1), part, core, p, keep_ref, send_ref)
        return carry

    lax.fori_loop(0, PIECES, spread, 0)

    for kind in range(2):
        for k in range(RING):
            q = kind * RING + lax.rem(meta_ref[3 - kind] + OFFSETS[k] + RING, RING)
            own = jnp.concatenate([own_ref[z, q] for z in range(RING)], axis=0)
            got = jnp.concatenate([got_ref[z, q] for z in range(RING)], axis=0)
            grad = join_rows(is_low, own, got)[:, :BLK]
            xn = join_rows(is_low, xc_ref[q], xc_got_ref[q])[:, :BLK]
            one = dot(grad, o_ref[...], 0, 0)
            two = dot(xn, grad_qkv, 0, 0)
            terms = jnp.concatenate([one[:, :QW], two[:, 64:]], axis=1)
            put_blocks(outs[RING * kind + k], terms)


def attention_backward(meta, own, got, tables, segs, qkvo, xcs, w_attn):
    return pl.pallas_call(
        attention_back_kernel,
        in_specs=[smem()] + [whole()] * 12 + [hbm()] * 8,
        out_specs=[whole()] * 10,
        out_shape=split_shapes() + [jax.ShapeDtypeStruct((RING, HALF, ATTN), LOW)] * 8,
        scratch_shapes=[
            pltpu.VMEM((PIECES, BLK, ATTN), LOW),
            pltpu.VMEM((SEQ, 384), F32),
            pltpu.VMEM((SEQ, LANES), LOW),
            pltpu.SemaphoreType.DMA((PIECES,)),
        ],
        compiler_params=pltpu.CompilerParams(vmem_limit_bytes=VMEM),
        cost_estimate=cost(0, 0),
        name="attention_backward",
    )(meta, own, got, *tables, *segs, *qkvo, *xcs, *w_attn)


def down_back_kernel(meta_ref, cot_own_ref, cot_got_ref, *rest):
    w_refs = rest[:8]
    out_ref, held, sems = rest[8:]
    is_low = meta_ref[0] == 0
    start_weights(meta_ref, w_refs, held, sems)
    out_ref[...] = jnp.zeros_like(out_ref)

    def project(n, carry):
        p = piece_at(meta_ref, n)
        wait_weights(held, sems, p)
        cot = join_rows(is_low, cot_own_ref[p], cot_got_ref[p])
        out_ref[...] += dot(cot[:, :BLK], held[p], 1, 0)
        return carry

    lax.fori_loop(0, PIECES, project, 0)


def down_back(meta, cot_own, cot_got, w_down):
    return pl.pallas_call(
        down_back_kernel,
        in_specs=[smem()] + [whole()] * 2 + [hbm()] * 8,
        out_specs=whole(),
        out_shape=jax.ShapeDtypeStruct((SEQ, FW), F32),
        scratch_shapes=[
            pltpu.VMEM((PIECES, BLK, FW), LOW),
            pltpu.SemaphoreType.DMA((PIECES,)),
        ],
        compiler_params=pltpu.CompilerParams(vmem_limit_bytes=VMEM),
        cost_estimate=cost(0, 0),
        name="down_backward",
    )(meta, cot_own, cot_got, *w_down)


def down_kernel(meta_ref, act_ref, *rest):
    w_refs = rest[:8]
    keep_ref, send_ref, held, part, sems = rest[8:]
    core = meta_ref[0]
    start_weights(meta_ref, w_refs, held, sems)
    part[:, BLK:] = jnp.zeros((SEQ, LANES - BLK), LOW)

    def spread(n, carry):
        p = piece_at(meta_ref, n)
        wait_weights(held, sems, p)
        split_rows(dot(act_ref[...], held[p], 1, 1), part, core, p, keep_ref, send_ref)
        return carry

    lax.fori_loop(0, PIECES, spread, 0)


def down_forward(meta, act, w_down):
    return pl.pallas_call(
        down_kernel,
        in_specs=[smem(), whole()] + [hbm()] * 8,
        out_specs=[whole()] * 2,
        out_shape=split_shapes(),
        scratch_shapes=[
            pltpu.VMEM((PIECES, BLK, FW), LOW),
            pltpu.VMEM((SEQ, LANES), LOW),
            pltpu.SemaphoreType.DMA((PIECES,)),
        ],
        compiler_params=pltpu.CompilerParams(vmem_limit_bytes=VMEM),
        cost_estimate=cost(0, 0),
        name="down_forward",
    )(meta, act, *w_down)


def start_ffn(meta_ref, refs, held, sems):
    x = meta_ref[2]
    y = meta_ref[3]
    for base, at, group in ((0, y, refs[:8]), (RING, x, refs[8:])):
        for k, offset in enumerate(OFFSETS):
            p = base + lax.rem(at + offset + RING, RING)
            for j in range(2):
                into = held.at[p, :, pl.ds(j * FW, FW)]
                pltpu.make_async_copy(group[2 * k + j], into, sems.at[p]).start()


def ffn_kernel(meta_ref, own_ref, got_ref, grad_act_ref, *rest):
    w_refs = rest[:16]
    act_ref, grad_ref, keep_ref, send_ref, held, acc, part, sems = rest[16:]
    core = meta_ref[0]
    is_low = core == 0
    start_ffn(meta_ref, w_refs, held, sems)
    acc[...] = jnp.zeros_like(acc)
    part[:, BLK:] = jnp.zeros((SEQ, LANES - BLK), LOW)

    def project(n, carry):
        p = piece_at(meta_ref, n)
        wait_weights(held, sems, p)
        own = jnp.concatenate([own_ref[z, p] for z in range(RING)], axis=0)
        got = jnp.concatenate([got_ref[z, p] for z in range(RING)], axis=0)
        acc[...] += dot(join_rows(is_low, own, got)[:, :BLK], held[p], 1, 0)
        return carry

    lax.fori_loop(0, PIECES, project, 0)

    def units(t, carry):
        at = pl.multiple_of(t * 128, 128)
        grad_act = grad_act_ref[:, pl.ds(at, 128)]
        gate = acc[:, pl.ds(at, 128)]
        up = acc[:, pl.ds(at + FW, 128)]
        sigmoid = 1.0 / (1.0 + jnp.exp(-gate))
        silu = gate * sigmoid
        act_ref[:, pl.ds(at, 128)] = (silu * up).astype(LOW)
        grad_gate = grad_act * up * sigmoid * (1.0 + gate * (1.0 - sigmoid))
        grad_ref[:, pl.ds(at, 128)] = grad_gate.astype(LOW)
        grad_ref[:, pl.ds(at + FW, 128)] = (grad_act * silu).astype(LOW)
        return carry

    lax.fori_loop(0, FW // 128, units, 0)

    def spread(p, carry):
        split_rows(dot(grad_ref[...], held[p], 1, 1), part, core, p, keep_ref, send_ref)
        return carry

    lax.fori_loop(0, PIECES, spread, 0)


def feed_forward(meta, own, got, grad_act, w_gu):
    return pl.pallas_call(
        ffn_kernel,
        in_specs=[smem()] + [whole()] * 3 + [hbm()] * 16,
        out_specs=[whole()] * 4,
        out_shape=[
            jax.ShapeDtypeStruct((SEQ, FW), LOW),
            jax.ShapeDtypeStruct((SEQ, GU), LOW),
        ]
        + split_shapes(),
        scratch_shapes=[
            pltpu.VMEM((PIECES, BLK, GU), LOW),
            pltpu.VMEM((SEQ, GU), F32),
            pltpu.VMEM((SEQ, LANES), LOW),
            pltpu.SemaphoreType.DMA((PIECES,)),
        ],
        compiler_params=pltpu.CompilerParams(vmem_limit_bytes=VMEM),
        cost_estimate=cost(0, 0),
        name="feed_forward",
    )(meta, own, got, grad_act, *w_gu)


def halves_of(part_ref, xc_ref, q, at):
    rows = jnp.concatenate([part_ref[z, q] for z in range(RING)], axis=0)
    return rows[:, :BLK], xc_ref[q, at : at + 128][:, :BLK]


def merge_kernel(part_ref, xc_ref, one_ref, two_ref):
    for p in range(RING):
        for ref, q in ((one_ref, p), (two_ref, RING + p)):
            for z in range(RING):
                ref[p, 32 * z : 32 * z + 32] = part_ref[z, q]
            ref[p, 128:] = xc_ref[q]


def merge(part, cot):
    return pl.pallas_call(
        merge_kernel,
        in_specs=[whole()] * 2,
        out_specs=[whole()] * 2,
        out_shape=[jax.ShapeDtypeStruct((RING, 256, LANES), LOW)] * 2,
        compiler_params=pltpu.CompilerParams(vmem_limit_bytes=VMEM),
        cost_estimate=cost(0, 0),
        name="merge",
    )(part, cot)


def ffn_terms_kernel(meta_ref, own_ref, got_ref, *rest, axis):
    rights = rest[:8]
    outs = rest[8:12]
    acc = rest[12]
    is_low = meta_ref[0] == 0
    at = meta_ref[axis]
    for k, offset in enumerate(OFFSETS):
        source = lax.rem(at + offset + RING, RING)
        xn = join_rows(is_low, own_ref[source, :128], got_ref[source, :128])[:, :BLK]
        cot = join_rows(is_low, own_ref[source, 128:], got_ref[source, 128:])[:, :BLK]
        down = dot(cot, rights[2 * k][...], 0, 0)
        both = dot(xn, rights[2 * k + 1][...], 0, 0)
        if k == 0:
            acc[:, :FW] = down
            acc[:, FW:] = both
        else:
            acc[:, :FW] += down
            acc[:, FW:] += both
    for k, ref in enumerate(outs):
        ref[:, ATTN:] = acc[k * HALF : (k + 1) * HALF, :].astype(LOW)


def ffn_terms(meta, own, got, rights, axis):
    return pl.pallas_call(
        functools.partial(ffn_terms_kernel, axis=axis),
        in_specs=[smem()] + [whole()] * 10,
        out_specs=[whole()] * 4,
        out_shape=[jax.ShapeDtypeStruct((HALF, WIDE), LOW)] * 4,
        scratch_shapes=[pltpu.VMEM((BLK, 3 * FW), F32)],
        compiler_params=pltpu.CompilerParams(vmem_limit_bytes=VMEM),
        cost_estimate=cost(0, 0),
        name="terms_feed_forward",
    )(meta, own, got, *rights)


def fill_kernel(*refs):
    for k, ref in enumerate(refs[8:]):
        total = refs[0][k].astype(F32)
        for part in refs[1:4]:
            total = total + part[k].astype(F32)
        ref[...] = total.astype(LOW)


def fill(attn, ffn):
    return pl.pallas_call(
        fill_kernel,
        grid=(1,),
        in_specs=[pl.BlockSpec((RING, HALF, ATTN), lambda i: (0, 0, 0))] * 4 + [hbm()] * 4,
        out_specs=[pl.BlockSpec((HALF, ATTN), lambda i: (0, 0))] * 4,
        out_shape=[jax.ShapeDtypeStruct((HALF, WIDE), LOW)] * 4,
        input_output_aliases={4 + k: k for k in range(4)},
        compiler_params=pltpu.CompilerParams(vmem_limit_bytes=VMEM),
        cost_estimate=cost(0, 0),
        name="fill",
    )(*attn, *ffn)


def fetch_kind(is_first, refs, held, sem):
    for kind in range(2):

        @pl.when(is_first if kind == 0 else jnp.logical_not(is_first))
        def _():
            for k in range(RING):
                pltpu.make_async_copy(refs[RING * kind + k], held.at[k], sem).start()

    pltpu.make_async_copy(held, held, sem).wait()


def finish_kernel(meta_ref, *refs):
    out_ref, held, sem = refs[8:]
    fetch_kind(meta_ref[0] == 1, refs[:8], held, sem)
    total = held[0].astype(F32)
    for k in range(1, RING):
        total = total + held[k].astype(F32)
    out_ref[...] = total.astype(LOW)


def finish(meta, parts):
    return pl.pallas_call(
        finish_kernel,
        in_specs=[smem()] + [hbm()] * 8,
        out_specs=whole(),
        out_shape=jax.ShapeDtypeStruct((HALF, WIDE), LOW),
        scratch_shapes=[pltpu.VMEM((RING, HALF, WIDE), LOW), pltpu.SemaphoreType.DMA],
        compiler_params=pltpu.CompilerParams(vmem_limit_bytes=VMEM),
        cost_estimate=cost(0, 0),
        name="finish_other",
    )(meta, *parts[0], *parts[1])


def pick_sum(is_first, refs):
    total = jnp.where(is_first, refs[0][...], refs[4][...]).astype(F32)
    for k in range(1, 4):
        total = total + jnp.where(is_first, refs[k][...], refs[4 + k][...]).astype(F32)
    return total


def adam_kernel(meta_ref, w_ref, m_ref, v_ref, came, *rest):
    parts = rest[:8]
    wo_ref, mo_ref, vo_ref, grad, stay = rest[8:]
    is_low = meta_ref[0] == 0
    stay[...] = pick_sum(is_low, parts)
    rows = w_ref.shape[0]
    for start, at, width in MAP:
        mine = stay[:, at : at + width]
        other = came[:, at : at + width].astype(F32)
        grad[:, start : start + width] = jnp.where(is_low, mine, other)
        grad[:, start + width : start + 2 * width] = jnp.where(is_low, other, mine)
    row = pl.program_id(0) * rows + lax.broadcasted_iota(jnp.int32, (rows, 1), 0)
    valid = row < meta_ref[4]
    weight, first, second = adam_step(
        w_ref[...], m_ref[...], v_ref[...], grad[...], LEARN, DECAY
    )
    wo_ref[...] = jnp.where(valid, weight, 0.0)
    mo_ref[...] = jnp.where(valid, first, 0.0)
    vo_ref[...] = jnp.where(valid, second, 0.0)


def adam(meta, master, moment_one, moment_two, came, parts):
    rows = 32
    units = master.shape[1]

    def block(width):
        return pl.BlockSpec((rows, width), lambda i: (i, 0))

    return pl.pallas_call(
        adam_kernel,
        grid=(pl.cdiv(HALF, rows),),
        in_specs=[smem()] + [block(units)] * 3 + [block(WIDE)] * 9,
        out_specs=[block(units)] * 3,
        out_shape=[jax.ShapeDtypeStruct(master.shape, F32)] * 3,
        scratch_shapes=[pltpu.VMEM((rows, units), F32), pltpu.VMEM((rows, WIDE), F32)],
        compiler_params=pltpu.CompilerParams(vmem_limit_bytes=VMEM),
        name="adam",
    )(meta, master, moment_one, moment_two, came, *parts[0], *parts[1])


def rms_scale(values):
    return lax.rsqrt(jnp.sum(values * values, axis=(0, 2), keepdims=True) / D + EPS_NORM)


def rms_backward(grad_out, normed, scale, gain):
    grad_normed = grad_out * gain
    inner = jnp.sum(grad_normed * normed, axis=(0, 2), keepdims=True) / D
    return scale * (grad_normed - normed * inner), jnp.sum(grad_out * normed, axis=1)


def adam_step(weight, first, second, grad, rate, decay):
    first_new = BETA * first + (1.0 - BETA) * grad
    second_new = BETA * second + (1.0 - BETA) * grad * grad
    inverse = 1.0 / (1.0 - BETA**STEP)
    update = (first_new * inverse) / (jnp.sqrt(second_new * inverse) + EPS_ADAM)
    return (weight - rate * (update + decay * weight), first_new, second_new)


def stage(*values):
    return lax.optimization_barrier(values)


def shards(
    tokens, cotangent, segments, owner, master, moment_one, moment_two, gains, gain_one, gain_two
):
    core = lax.axis_index("core")
    yl = lax.axis_index("yl")
    z = lax.axis_index("z")
    x = lax.axis_index(X)
    y = lax.axis_index("yh") * 2 + yl
    count = jnp.sum((owner == (y // 2 * RING + x) * 2 + core).astype(jnp.int32)) - yl * HALF
    place = jnp.stack([core, z, x, y]).astype(jnp.int32)
    meta = jnp.stack([core, z, x, y, count]).astype(jnp.int32)
    along = (Y, X)
    across = (X, Y)

    def add_core(keep, other):
        return (keep.astype(F32) + other.astype(F32)).astype(LOW)

    def split_z(block):
        return lax.all_to_all(block, "z", split_axis=0, concat_axis=0, tiled=True)

    def sum_z(block):
        return jnp.sum(block.astype(F32), axis=0)

    def all_z(block):
        return split_z(jnp.broadcast_to(block[None], (RING, *block.shape)))

    own, send = pack(place, owner, master)
    got = swap_core(send)
    first = jnp.where(core == 0, own, got)
    second = jnp.where(core == 0, got, own)
    first, second, owner, tokens, cotangent = stage(first, second, owner, tokens, cotangent)

    near_first = near(first, X)
    near_second = near(second, Y)
    numbers = jnp.zeros((8, D), LOW).at[0, :SEQ].set(segments.astype(LOW))
    tokens = swap_sequences(jnp.concatenate([tokens, numbers], axis=0))
    onehot = (owner[:, None] == jnp.arange(16, dtype=jnp.int32)[None, :]).astype(jnp.int32)
    rank = jnp.sum((jnp.cumsum(onehot, axis=0) - onehot) * onehot, axis=1)
    slot = (owner * CAP + rank)[:, None]
    ids = slot_ids(x, y)
    parts = jnp.concatenate([three_parts(gains), jnp.zeros((10, D), LOW)], axis=0)
    near_first, near_second, slot, ids, parts, cotangent = stage(
        near_first, near_second, slot, ids, parts, cotangent
    )

    blocks = [
        (first, *near_first, *halves(*near_first, X, WIDE_CUT)),
        (second, *near_second, *halves(*near_second, Y, WIDE_CUT)),
    ]
    attn = [assemble(b, 0) for b in blocks]
    attn, blocks, tokens, cotangent = stage(attn, blocks, tokens, cotangent)

    attn_near = [near(b, axis) for b, axis in zip(attn, along)]
    position = jnp.arange(SEQ, dtype=F32)
    freq = jnp.exp(-jnp.log(THETA) * (2.0 * jnp.arange(HD // 2, dtype=F32) / HD))
    angle = position[:, None] * freq[None, :]
    tables = (
        jnp.concatenate([jnp.cos(angle)] * 2, axis=1),
        jnp.concatenate([jnp.sin(angle)] * 2, axis=1),
    )
    segment = tokens[128, :SEQ].astype(jnp.int32)
    segs = (segment[:, None], segment[None, :])
    down = [assemble(b, 1) for b in blocks]
    cotangent = swap_sequences(cotangent)
    attn_near, down, tables, segs, tokens, cotangent = stage(
        attn_near, down, tables, segs, tokens, cotangent
    )
    down_near = [near(b, axis) for b, axis in zip(down, along)]
    xn_own, inputs, gain = tokens_to_slots(meta, slot, ids, tokens, gains, parts)
    gate = [assemble(b, 2) for b in blocks]
    turned = (slot.reshape(1, D), ids)
    down_near, blocks, gate, turned, xn_own, inputs, gain, cotangent = stage(
        down_near, blocks, gate, turned, xn_own, inputs, gain, cotangent
    )
    pair_far = [far(q[0], d[1], axis) for q, d, axis in zip(attn_near, down_near, along)]
    up = [assemble(b, 3) for b in blocks]
    xn_got = swap_core(xn_own)
    cot_own, cot_z = cot_to_slots(meta, slot, ids, cotangent)
    pair_far, gate, up, xn_got, cot_own, cot_z = stage(pair_far, gate, up, xn_got, cot_own, cot_z)
    w_attn = []
    w_down = []
    for kind in range(2):
        w_attn += [attn[kind], *attn_near[kind], pair_far[kind][0]]
        w_down += [down[kind], *down_near[kind], pair_far[kind][1]]

    gate_near = [near(b, axis) for b, axis in zip(gate, along)]
    *qkv, attended, keep, send = attention_forward(meta, xn_own, xn_got, tables, segs, w_attn)
    cot_got = swap_core(cot_own)
    gate_near, up, keep, send, cot_got = stage(gate_near, up, keep, send, cot_got)
    up_near = [near(b, axis) for b, axis in zip(up, along)]
    got = split_z(add_core(keep, swap_core(send)))
    grad_act = down_back(meta, cot_own, cot_got, w_down)
    up_near, gate_near, got, grad_act = stage(up_near, gate_near, got, grad_act)
    gu_far = [far(g[0], u[1], axis) for g, u, axis in zip(gate_near, up_near, along)]
    hidden = inputs + sum_z(got)
    scale_two = rms_scale(hidden)
    normed_two = hidden * scale_two
    xn_two = all_z((normed_two * gain[:, 1:2]).astype(LOW))
    gu_far, xn_two = stage(gu_far, xn_two)
    xn_two_got = swap_core(xn_two)
    left_sent = merge(xn_two, cot_own)
    xn_two, xn_two_got, grad_act, left_sent = stage(xn_two, xn_two_got, grad_act, left_sent)
    w_gu = []
    for kind in range(2):
        w_gu += [gate[kind], up[kind]]
        w_gu += [gate_near[kind][0], up_near[kind][0], gate_near[kind][1], up_near[kind][1]]
        w_gu += [*gu_far[kind]]

    act, grad_gu, keep, send = feed_forward(meta, xn_two, xn_two_got, grad_act, w_gu)
    def exchange(block, axis):
        return lax.all_to_all(block, axis, split_axis=0, concat_axis=0, tiled=True)

    lefts = [exchange(left_sent[0], Y)]
    act, grad_gu, keep, send, lefts = stage(act, grad_gu, keep, send, lefts)
    gu_near = [near(grad_gu, axis) for axis in along]
    got = split_z(add_core(keep, swap_core(send)))
    keep_mlp, send_mlp = down_forward(meta, act, w_down)
    gu_near, got, keep_mlp, send_mlp, act = stage(gu_near, got, keep_mlp, send_mlp, act)
    act_near = [near(act, axis) for axis in along]
    lefts_got = [swap_core(lefts[0])]
    mlp_both = add_core(keep_mlp, swap_core(send_mlp))
    grad_xn_two = sum_z(got)
    grad_norm_two, gain_grad_two = rms_backward(grad_xn_two, normed_two, scale_two, gain[:, 1:2])
    grad_hidden = cot_z + grad_norm_two
    grad_branch = lax.all_gather(grad_hidden.astype(LOW), "z", axis=0, tiled=False)
    lefts.append(exchange(left_sent[1], X))
    act_near, grad_branch, grad_hidden, gain_grad_two, lefts, lefts_got, gu_near, mlp_both = stage(
        act_near, grad_branch, grad_hidden, gain_grad_two, lefts, lefts_got, gu_near, mlp_both
    )
    grad_branch_got = swap_core(grad_branch)
    ends = [far(a[0], g[1], axis) for a, g, axis in zip(act_near, gu_near, along)]

    xns = (xn_own, xn_got)
    keep, send, *terms = attention_backward(
        meta, grad_branch, grad_branch_got, tables, segs, (*qkv, attended), xns, w_attn
    )
    attn_terms = (terms[:4], terms[4:])
    mlp = lax.psum_scatter(mlp_both, "z", scatter_dimension=0, tiled=True)[0]
    ends, keep, send, attn_terms, lefts, mlp = stage(ends, keep, send, attn_terms, lefts, mlp)

    def direct(first, second, axes):
        _, back, ahead, last = first
        _, back_two, ahead_two, last_two = second
        one = (move(ahead, axes[0], 1), move(back, axes[0], -1), move(last, axes[0], 2))
        up = move(ahead_two, axes[1], 1)
        down = move(back_two, axes[1], -1)
        return one, up, down, last_two

    attn_nears = [
        (move(t[2], axis, 1), move(t[1], axis, -1)) for t, axis in zip(attn_terms, along)
    ]

    def rights_of(kind):
        rights = (act, grad_gu)
        for n in range(2):
            rights += (act_near[kind][n], gu_near[kind][n])
        return rights + tuple(ends[kind])

    ffn_sums = [ffn_terms(meta, lefts[0], lefts_got[0], rights_of(0), 3)]
    lefts_got.append(swap_core(lefts[1]))
    got = split_z(add_core(keep, swap_core(send)))
    attn_nears, attn_terms, lefts, lefts_got, ffn_sums, got = stage(
        attn_nears, attn_terms, lefts, lefts_got, ffn_sums, got
    )
    attn_others = [
        (*n, move(t[3], axis, 2)) for n, t, axis in zip(attn_nears, attn_terms, along)
    ]
    ffn_sums.append(ffn_terms(meta, lefts[1], lefts_got[1], rights_of(1), 2))
    grad_xn_one = sum_z(got)
    scale_one = rms_scale(inputs)
    grad_norm_one, gain_grad_one = rms_backward(
        grad_xn_one, inputs * scale_one, scale_one, gain[:, 0:1]
    )
    grad_tokens_z = (grad_hidden + grad_norm_one).astype(LOW)
    output_z = (hidden + mlp.astype(F32)).astype(LOW)
    gain_grads = three_parts(jnp.stack([gain_grad_one, gain_grad_two], axis=0))
    gain_grads = jnp.swapaxes(gain_grads, 0, 1)
    blank = jnp.zeros((PIECES, 10, LANES), LOW)
    last = from_slots(
        jnp.concatenate([output_z, grad_tokens_z, gain_grads, blank], axis=1), *turned
    )
    attn_others, ffn_sums, last = stage(attn_others, ffn_sums, last)
    blocks = [fill((t[0], *o), f) for t, o, f in zip(attn_terms, attn_others, ffn_sums)]
    part = lax.all_gather(last, "z", axis=0, tiled=False)
    one, up, down, last_two = direct(*blocks, across)
    up, down, last_two = stage(up, down, last_two)
    others = (one, (up, down, move(last_two, across[1], 2)))
    others, owns = stage(others, [b[0] for b in blocks])
    totals = [(b, *o) for b, o in zip(owns, others)]
    send, totals = stage(finish(meta, totals), totals)
    came = swap_core(send)
    moved = swap_sequences(jnp.swapaxes(part[:, :64].reshape(RING, 2, 32, D), 0, 1))
    gain_grads = part[:, 64:70].astype(F32).sum(axis=0)
    gain_grads = gain_grads[:2] + gain_grads[2:4] + gain_grads[4:6]
    gain_other = swap_core(gain_grads)
    came, gain_other, totals = stage(came, gain_other, totals)

    def sum_along(value, axis):
        back, ahead = near(value, axis)
        return (value + move(value, axis, 2)) + (back + ahead)

    gain_grads = sum_along(gain_grads + gain_other, X)
    new_master, new_one, new_two = adam(meta, master, moment_one, moment_two, came, totals)
    gain_grads, new_master, moved = stage(gain_grads, new_master, moved)
    gain_grads = sum_along(gain_grads, Y)
    output = moved[0].reshape(128, D)
    grad_tokens = moved[1].reshape(128, D)
    new_gains, new_gain_one, new_gain_two = adam_step(
        gains, gain_one, gain_two, gain_grads, LEARN_GAIN, 0.0
    )
    return (
        output,
        grad_tokens,
        new_master,
        new_one,
        new_two,
        new_gains,
        new_gain_one,
        new_gain_two,
    )


def solution(mesh):
    fine = Mesh(mesh.devices.reshape(2, 4, 2, 2, 4), ("yh", "x", "core", "yl", "z"))
    rows = ("yh", "x", "core", "yl")
    in_specs = (
        P(rows, None),
        P(rows, None),
        P(("yh", "x", "core")),
        P(),
        P(rows, "z"),
        P(rows, "z"),
        P(rows, "z"),
        P(),
        P(),
        P(),
    )
    out_specs = (
        P(rows, None),
        P(rows, None),
        P(rows, "z"),
        P(rows, "z"),
        P(rows, "z"),
        P(),
        P(),
        P(),
    )
    return jax.shard_map(shards, mesh=fine, in_specs=in_specs, out_specs=out_specs, check_vma=False)
```

```python
import functools

import jax
import jax.numpy as jnp
from jax import lax
from jax.experimental import pallas as pl
from jax.experimental.pallas import tpu as pltpu
from jax.sharding import Mesh
from jax.sharding import PartitionSpec as P

HD = 80
STEP = 5
D = 2560
CAP = 240
HALF = 120
SEQ = 256
RING = 4

EPS_NORM = 1e-05
EPS_ADAM = 1e-08
THETA = 1000000.0
BETA = 0.5
LEARN = 0.05
LEARN_GAIN = 0.2
DECAY = 0.1
NEG_BIG = -1e30

X = "x"
Y = ("yh", "yl")
OFFSETS = (0, -1, 1, 2)
LOW = jnp.bfloat16
F32 = jnp.float32

HEADS = 4
QW = 320
KW = 80
FW = 896
ATTN = 896
GU = 2 * FW
WIDE = ATTN + 3 * FW
WIDE_CUT = 1792
MAP = (
    (0, 320, QW),
    (640, 640, KW),
    (800, 720, KW),
    (960, 1792, FW),
    (2752, 2688, FW),
    (4544, 0, QW),
    (5184, 896, FW),
)
PIECES = 8
BLK = 4 * HALF
LANES = 512
VMEM = 60 * 1024 * 1024


def dot(left, right, left_axis, right_axis):
    return lax.dot_general(
        left, right, (((left_axis,), (right_axis,)), ((), ())), preferred_element_type=F32
    )


def move(block, axis, distance):
    route = [(i, (i + distance) % RING) for i in range(RING)]
    return lax.ppermute(block, axis, route)


def swap_core(block):
    return lax.ppermute(block, "core", [(0, 1), (1, 0)])


def swap_sequences(block):
    return lax.ppermute(block, ("core", "yl"), [(0, 0), (1, 2), (2, 1), (3, 3)])


def near(block, axis):
    return move(block, axis, 1), move(block, axis, -1)


def far(back, ahead, axis):
    return move(back, axis, 1), move(ahead, axis, -1)


def halves(back, ahead, axis, cut):
    return far(back[:, :cut], ahead[:, cut:], axis)


def slot_ids(x, y):
    offsets = jnp.array(OFFSETS, jnp.int32)
    every = jnp.arange(RING, dtype=jnp.int32)
    rows = jnp.arange(HALF, dtype=jnp.int32)

    def slots(xx, yy, core):
        return (((yy // 2) * RING + xx) * 2 + core) * CAP + (yy % 2) * HALF

    first = slots(((x + offsets) % RING)[None, :, None], every[:, None, None], 0) + rows
    second = slots(every[:, None, None], ((y + offsets) % RING)[None, :, None], 1) + rows
    ids = jnp.concatenate([first, second], axis=0).reshape(PIECES, 1, BLK)
    return jnp.pad(ids, ((0, 0), (0, 0), (0, LANES - BLK)), constant_values=-1)


def ranks(onehot):
    blocks = onehot.reshape(20, 128, 16)
    row = jnp.arange(128, dtype=jnp.int32)
    earlier = (row[None, :] < row[:, None]).astype(LOW)
    within = jnp.einsum("ij,bjf->bif", earlier, blocks.astype(LOW), preferred_element_type=F32)
    totals = jnp.sum(blocks, axis=1).astype(LOW)
    before = dot(earlier[:20, :20], totals, 1, 0)
    counts = (within + before[:, None, :]) * blocks.astype(F32)
    return jnp.sum(counts, axis=2).astype(jnp.int32).reshape(-1)


def three_parts(values):
    high = lax.reduce_precision(values, 8, 7)
    rest = values - high
    middle = lax.reduce_precision(rest, 8, 7)
    return jnp.concatenate([high, middle, rest - middle], axis=0).astype(LOW)


def whole():
    return pl.BlockSpec(memory_space=pltpu.VMEM)


def hbm():
    return pl.BlockSpec(memory_space=pl.ANY)


def smem():
    return pl.BlockSpec(memory_space=pltpu.SMEM)


def cost(flops, size):
    return pl.CostEstimate(flops=flops, bytes_accessed=size, transcendentals=0)


def pack_kernel(meta_ref, owner_ref, master_ref, own_ref, send_ref):
    is_low = meta_ref[0] == 0
    share = (meta_ref[3] // 2 * RING + meta_ref[2]) * 2 + meta_ref[0]
    count = jnp.sum((owner_ref[...] == share).astype(jnp.int32)) - lax.rem(meta_ref[3], 2) * HALF
    valid = lax.broadcasted_iota(jnp.int32, (HALF, 1), 0) < count
    blank = jnp.zeros((HALF, ATTN - 800), LOW)
    own_ref[:, 800:ATTN] = blank
    send_ref[:, 800:ATTN] = blank
    for start, at, width in MAP:
        low = jnp.where(valid, master_ref[:, start : start + width], 0.0)
        high = jnp.where(valid, master_ref[:, start + width : start + 2 * width], 0.0)
        own_ref[:, at : at + width] = jnp.where(is_low, low, high).astype(LOW)
        send_ref[:, at : at + width] = jnp.where(is_low, high, low).astype(LOW)


def pack(meta, owner, master):
    return pl.pallas_call(
        pack_kernel,
        in_specs=[smem(), whole(), whole()],
        out_specs=[whole()] * 2,
        out_shape=[jax.ShapeDtypeStruct((HALF, WIDE), LOW)] * 2,
        compiler_params=pltpu.CompilerParams(vmem_limit_bytes=VMEM),
        name="pack",
    )(meta, owner.reshape(20, 128), master)


def assemble_kernel(*refs):
    out = refs[4]
    for k, ref in enumerate(refs[:4]):
        out[k * HALF : (k + 1) * HALF, :] = ref[...]


def assemble(blocks, j):
    block, back, ahead, one, two = blocks
    specs = [pl.BlockSpec((HALF, FW), lambda i: (0, j))] * 3
    specs += [pl.BlockSpec((HALF, FW), lambda i: (0, j % 2))]
    return pl.pallas_call(
        assemble_kernel,
        grid=(1,),
        in_specs=specs,
        out_specs=pl.BlockSpec((BLK, FW), lambda i: (0, 0)),
        out_shape=jax.ShapeDtypeStruct((BLK, FW), LOW),
        compiler_params=pltpu.CompilerParams(vmem_limit_bytes=VMEM),
        cost_estimate=cost(0, 0),
        name="assemble",
    )(block, back, ahead, one if j < 2 else two)


def one_hot(slot_ref, ids_ref):
    return jnp.where(slot_ref[...] == ids_ref[0], 1.0, 0.0).astype(LOW)


def tokens_kernel(meta_ref, slot_ref, ids_ref, tokens_ref, gains_ref, parts_ref, xn_ref, in_ref, gain_ref, rows):
    @pl.when(pl.program_id(0) == 0)
    def _():
        at = pl.multiple_of(meta_ref[1] * 32, 32)
        tokens = tokens_ref[:128].astype(F32)
        scale = lax.rsqrt(jnp.sum(tokens * tokens, axis=1, keepdims=True) / D + EPS_NORM)
        rows[:128] = (tokens * scale * gains_ref[0:1]).astype(LOW)
        rows[128:160] = tokens_ref[pl.ds(at, 32)]
        rows[160:] = parts_ref[...]

    placed = dot(rows[...], one_hot(slot_ref, ids_ref), 1, 0)
    xn_ref[0] = placed[:128].astype(LOW)
    in_ref[0] = placed[128:160]
    gain_ref[0] = placed[160:162] + placed[162:164] + placed[164:166]


def cot_kernel(meta_ref, slot_ref, ids_ref, cot_ref, out_ref, z_ref, rows):
    @pl.when(pl.program_id(0) == 0)
    def _():
        rows[:128] = cot_ref[...]
        rows[128:] = cot_ref[pl.ds(pl.multiple_of(meta_ref[1] * 32, 32), 32)]

    placed = dot(rows[...], one_hot(slot_ref, ids_ref), 1, 0)
    out_ref[0] = placed[:128].astype(LOW)
    z_ref[0] = placed[128:]


def to_slots(kernel, meta, slot, ids, args, outs, rows, name):
    def same(shape):
        return pl.BlockSpec(shape, lambda p: (0, 0))

    return pl.pallas_call(
        kernel,
        grid=(PIECES,),
        in_specs=[
            smem(),
            same((D, 1)),
            pl.BlockSpec((1, 1, LANES), lambda p: (p, 0, 0)),
            *(same(a.shape) for a in args),
        ],
        out_specs=[pl.BlockSpec((1, n, LANES), lambda p: (p, 0, 0)) for n, _ in outs],
        out_shape=[jax.ShapeDtypeStruct((PIECES, n, LANES), kind) for n, kind in outs],
        scratch_shapes=[pltpu.VMEM((rows, D), LOW)],
        compiler_params=pltpu.CompilerParams(vmem_limit_bytes=VMEM),
        cost_estimate=cost(0, 0),
        name=name,
    )(meta, slot, ids, *args)


def tokens_to_slots(meta, slot, ids, tokens, gains, parts):
    outs = [(128, LOW), (32, F32), (2, F32)]
    args = (tokens, gains, parts)
    return to_slots(tokens_kernel, meta, slot, ids, args, outs, 176, "tokens_to_slots")


def cot_to_slots(meta, slot, ids, cotangent):
    outs = [(128, LOW), (32, F32)]
    return to_slots(cot_kernel, meta, slot, ids, (cotangent,), outs, 160, "cotangent_to_slots")


def unplace_kernel(slot_ref, ids_ref, rows_ref, out_ref, acc):
    ids = jnp.transpose(jnp.broadcast_to(ids_ref[0], (8, LANES)))[:, :1]
    place = jnp.where(ids == slot_ref[...], 1.0, 0.0).astype(LOW)

    @pl.when(pl.program_id(0) == 0)
    def _():
        acc[...] = jnp.zeros_like(acc)

    acc[...] += dot(rows_ref[0], place, 1, 0)

    @pl.when(pl.program_id(0) == PIECES - 1)
    def _():
        out_ref[...] = acc[...].astype(LOW)


def from_slots(rows, slot, ids):
    n = rows.shape[1]
    return pl.pallas_call(
        unplace_kernel,
        grid=(PIECES,),
        in_specs=[
            pl.BlockSpec((1, D), lambda p: (0, 0)),
            pl.BlockSpec((1, 1, LANES), lambda p: (p, 0, 0)),
            pl.BlockSpec((1, n, LANES), lambda p: (p, 0, 0)),
        ],
        out_specs=pl.BlockSpec((n, D), lambda p: (0, 0)),
        out_shape=jax.ShapeDtypeStruct((n, D), LOW),
        scratch_shapes=[pltpu.VMEM((n, D), F32)],
        compiler_params=pltpu.CompilerParams(vmem_limit_bytes=VMEM),
        cost_estimate=cost(0, 0),
        name="from_slots",
    )(slot, ids, rows)


def start_weights(meta_ref, refs, held, sems):
    x = meta_ref[2]
    y = meta_ref[3]
    for base, at, group in ((0, y, refs[:4]), (RING, x, refs[4:])):
        for ref, offset in zip(group, OFFSETS):
            p = base + lax.rem(at + offset + RING, RING)
            pltpu.make_async_copy(ref, held.at[p], sems.at[p]).start()


def piece_at(meta_ref, n):
    kind = n // RING
    k = lax.rem(n, RING)
    offset = jnp.where(k == 1, 3, jnp.where(k == 2, 1, jnp.where(k == 3, 2, 0)))
    at = jnp.where(kind == 0, meta_ref[3], meta_ref[2])
    return kind * RING + lax.rem(at + offset, RING)


def wait_weights(held, sems, p):
    pltpu.make_async_copy(held.at[p], held.at[p], sems.at[p]).wait()


def split_rows(value, scratch, core, p, keep_ref, send_ref):
    scratch[:, :BLK] = value.astype(LOW)
    for z in range(RING):
        keep_ref[z, p] = scratch[pl.ds(pl.multiple_of(core * 128 + 32 * z, 32), 32), :]
        send_ref[z, p] = scratch[pl.ds(pl.multiple_of((1 - core) * 128 + 32 * z, 32), 32), :]


def join_rows(is_low, own, got):
    return jnp.concatenate(
        [jnp.where(is_low, own, got), jnp.where(is_low, got, own)], axis=0
    )


def rope(values, cosine, sine):
    half = HD // 2
    turned = jnp.concatenate([-values[:, half:], values[:, :half]], axis=1)
    return values * cosine + turned * sine


def head_probs(query, keys, mask):
    scores = dot(query, keys, 1, 1) * HD ** (-0.5)
    scores = jnp.where(mask, scores, NEG_BIG)
    weight = jnp.exp(scores - jnp.max(scores, axis=1, keepdims=True))
    return weight / jnp.sum(weight, axis=1, keepdims=True)


def causal_mask(seg_col, seg_row):
    rows = lax.broadcasted_iota(jnp.int32, (SEQ, SEQ), 0)
    cols = lax.broadcasted_iota(jnp.int32, (SEQ, SEQ), 1)
    return (seg_col == seg_row) & (cols <= rows)


def attention_kernel(
    meta_ref, own_ref, got_ref, cos_ref, sin_ref, segc_ref, segr_ref, *rest
):
    w_refs = rest[:8]
    q_ref, k_ref, v_ref, o_ref, keep_ref, send_ref, held, acc, part, sems = rest[8:]
    core = meta_ref[0]
    is_low = core == 0
    start_weights(meta_ref, w_refs, held, sems)
    acc[...] = jnp.zeros_like(acc)
    part[:, BLK:] = jnp.zeros((SEQ, LANES - BLK), LOW)

    def project(n, carry):
        p = piece_at(meta_ref, n)
        wait_weights(held, sems, p)
        rows = join_rows(is_low, own_ref[p], got_ref[p])
        acc[...] += dot(rows[:, :BLK], held[p, :, 256:], 1, 0)
        return carry

    lax.fori_loop(0, PIECES, project, 0)
    cosine = cos_ref[...]
    sine = sin_ref[...]
    mask = causal_mask(segc_ref[...], segr_ref[...])
    projected = acc[...]
    keys = rope(projected[:, 384:464], cosine, sine).astype(LOW)
    values = projected[:, 464:544].astype(LOW)
    k_ref[...] = keys
    v_ref[...] = values
    outs = []
    for h in range(HEADS):
        query = rope(projected[:, 64 + h * HD : 64 + (h + 1) * HD], cosine, sine).astype(LOW)
        q_ref[h] = query
        probs = head_probs(query, keys, mask)
        outs.append(dot(probs.astype(LOW), values, 1, 0))
    outs.append(jnp.zeros((SEQ, 64), F32))
    attended = jnp.concatenate(outs, axis=1).astype(LOW)
    o_ref[...] = attended

    def spread(p, carry):
        split_rows(dot(attended, held[p, :, :384], 1, 1), part, core, p, keep_ref, send_ref)
        return carry

    lax.fori_loop(0, PIECES, spread, 0)


def split_shapes():
    return [
        jax.ShapeDtypeStruct((RING, PIECES, 32, LANES), LOW),
        jax.ShapeDtypeStruct((RING, PIECES, 32, LANES), LOW),
    ]


def attention_forward(meta, own, got, tables, segs, w_attn):
    return pl.pallas_call(
        attention_kernel,
        in_specs=[smem()] + [whole()] * 6 + [hbm()] * 8,
        out_specs=[whole()] * 6,
        out_shape=[
            jax.ShapeDtypeStruct((HEADS, SEQ, HD), LOW),
            jax.ShapeDtypeStruct((SEQ, HD), LOW),
            jax.ShapeDtypeStruct((SEQ, HD), LOW),
            jax.ShapeDtypeStruct((SEQ, 384), LOW),
        ]
        + split_shapes(),
        scratch_shapes=[
            pltpu.VMEM((PIECES, BLK, ATTN), LOW),
            pltpu.VMEM((SEQ, ATTN - 256), F32),
            pltpu.VMEM((SEQ, LANES), LOW),
            pltpu.SemaphoreType.DMA((PIECES,)),
        ],
        compiler_params=pltpu.CompilerParams(vmem_limit_bytes=VMEM),
        cost_estimate=cost(0, 0),
        name="attention_forward",
    )(meta, own, got, *tables, *segs, *w_attn)


def put_blocks(ref, value):
    for k in range(RING):
        ref[k] = value[k * HALF : (k + 1) * HALF].astype(LOW)


def attention_back_kernel(
    meta_ref, own_ref, got_ref, cos_ref, sin_ref, segc_ref, segr_ref, q_ref, k_ref, v_ref, o_ref, xc_ref, xc_got_ref, *rest
):
    w_refs = rest[:8]
    keep_ref, send_ref = rest[8:10]
    outs = rest[10:18]
    held, acc, part, sems = rest[18:]
    core = meta_ref[0]
    is_low = core == 0
    start_weights(meta_ref, w_refs, held, sems)
    acc[...] = jnp.zeros_like(acc)
    part[:, BLK:] = jnp.zeros((SEQ, LANES - BLK), LOW)

    def project(n, carry):
        p = piece_at(meta_ref, n)
        wait_weights(held, sems, p)
        own = jnp.concatenate([own_ref[z, p] for z in range(RING)], axis=0)
        got = jnp.concatenate([got_ref[z, p] for z in range(RING)], axis=0)
        acc[...] += dot(join_rows(is_low, own, got)[:, :BLK], held[p, :, :384], 1, 0)
        return carry

    lax.fori_loop(0, PIECES, project, 0)
    cosine = cos_ref[...]
    sine = -sin_ref[...]
    mask = causal_mask(segc_ref[...], segr_ref[...])
    grad_att = acc[...]
    keys = k_ref[...]
    values = v_ref[...]
    factor = HD ** (-0.5)
    grads = []
    grad_keys = jnp.zeros((SEQ, HD), F32)
    grad_values = jnp.zeros((SEQ, HD), F32)
    for h in range(HEADS):
        query = q_ref[h]
        grad_o = grad_att[:, h * HD : (h + 1) * HD].astype(LOW)
        probs = head_probs(query, keys, mask)
        grad_probs = dot(grad_o, values, 1, 1)
        inner = jnp.sum(probs * grad_probs, axis=1, keepdims=True)
        grad_scores = (probs * (grad_probs - inner)).astype(LOW)
        grads.append(rope(dot(grad_scores, keys, 1, 0) * factor, cosine, sine))
        grad_keys += dot(grad_scores, query, 0, 0)
        grad_values += dot(probs.astype(LOW), grad_o, 0, 0)
    grads.append(rope(grad_keys * factor, cosine, sine))
    grads.append(grad_values)
    zeros = [jnp.zeros((SEQ, 64), F32)]
    ends = [jnp.zeros((SEQ, 96), F32)]
    grad_qkv = jnp.concatenate(zeros + grads + ends, axis=1).astype(LOW)

    def spread(p, carry):
        split_rows(dot(grad_qkv, held[p, :, 256:], 1, 1), part, core, p, keep_ref, send_ref)
        return carry

    lax.fori_loop(0, PIECES, spread, 0)

    for kind in range(2):
        for k in range(RING):
            q = kind * RING + lax.rem(meta_ref[3 - kind] + OFFSETS[k] + RING, RING)
            own = jnp.concatenate([own_ref[z, q] for z in range(RING)], axis=0)
            got = jnp.concatenate([got_ref[z, q] for z in range(RING)], axis=0)
            grad = join_rows(is_low, own, got)[:, :BLK]
            xn = join_rows(is_low, xc_ref[q], xc_got_ref[q])[:, :BLK]
            one = dot(grad, o_ref[...], 0, 0)
            two = dot(xn, grad_qkv, 0, 0)
            terms = jnp.concatenate([one[:, :QW], two[:, 64:]], axis=1)
            put_blocks(outs[RING * kind + k], terms)


def attention_backward(meta, own, got, tables, segs, qkvo, xcs, w_attn):
    return pl.pallas_call(
        attention_back_kernel,
        in_specs=[smem()] + [whole()] * 12 + [hbm()] * 8,
        out_specs=[whole()] * 10,
        out_shape=split_shapes() + [jax.ShapeDtypeStruct((RING, HALF, ATTN), LOW)] * 8,
        scratch_shapes=[
            pltpu.VMEM((PIECES, BLK, ATTN), LOW),
            pltpu.VMEM((SEQ, 384), F32),
            pltpu.VMEM((SEQ, LANES), LOW),
            pltpu.SemaphoreType.DMA((PIECES,)),
        ],
        compiler_params=pltpu.CompilerParams(vmem_limit_bytes=VMEM),
        cost_estimate=cost(0, 0),
        name="attention_backward",
    )(meta, own, got, *tables, *segs, *qkvo, *xcs, *w_attn)


def down_back_kernel(meta_ref, cot_own_ref, cot_got_ref, *rest):
    w_refs = rest[:8]
    out_ref, held, sems = rest[8:]
    is_low = meta_ref[0] == 0
    start_weights(meta_ref, w_refs, held, sems)
    out_ref[...] = jnp.zeros_like(out_ref)

    def project(n, carry):
        p = piece_at(meta_ref, n)
        wait_weights(held, sems, p)
        cot = join_rows(is_low, cot_own_ref[p], cot_got_ref[p])
        out_ref[...] += dot(cot[:, :BLK], held[p], 1, 0)
        return carry

    lax.fori_loop(0, PIECES, project, 0)


def down_back(meta, cot_own, cot_got, w_down):
    return pl.pallas_call(
        down_back_kernel,
        in_specs=[smem()] + [whole()] * 2 + [hbm()] * 8,
        out_specs=whole(),
        out_shape=jax.ShapeDtypeStruct((SEQ, FW), F32),
        scratch_shapes=[
            pltpu.VMEM((PIECES, BLK, FW), LOW),
            pltpu.SemaphoreType.DMA((PIECES,)),
        ],
        compiler_params=pltpu.CompilerParams(vmem_limit_bytes=VMEM),
        cost_estimate=cost(0, 0),
        name="down_backward",
    )(meta, cot_own, cot_got, *w_down)


def down_kernel(meta_ref, act_ref, *rest):
    w_refs = rest[:8]
    keep_ref, send_ref, held, part, sems = rest[8:]
    core = meta_ref[0]
    start_weights(meta_ref, w_refs, held, sems)
    part[:, BLK:] = jnp.zeros((SEQ, LANES - BLK), LOW)

    def spread(n, carry):
        p = piece_at(meta_ref, n)
        wait_weights(held, sems, p)
        split_rows(dot(act_ref[...], held[p], 1, 1), part, core, p, keep_ref, send_ref)
        return carry

    lax.fori_loop(0, PIECES, spread, 0)


def down_forward(meta, act, w_down):
    return pl.pallas_call(
        down_kernel,
        in_specs=[smem(), whole()] + [hbm()] * 8,
        out_specs=[whole()] * 2,
        out_shape=split_shapes(),
        scratch_shapes=[
            pltpu.VMEM((PIECES, BLK, FW), LOW),
            pltpu.VMEM((SEQ, LANES), LOW),
            pltpu.SemaphoreType.DMA((PIECES,)),
        ],
        compiler_params=pltpu.CompilerParams(vmem_limit_bytes=VMEM),
        cost_estimate=cost(0, 0),
        name="down_forward",
    )(meta, act, *w_down)


def start_ffn(meta_ref, refs, held, sems):
    x = meta_ref[2]
    y = meta_ref[3]
    for base, at, group in ((0, y, refs[:8]), (RING, x, refs[8:])):
        for k, offset in enumerate(OFFSETS):
            p = base + lax.rem(at + offset + RING, RING)
            for j in range(2):
                into = held.at[p, :, pl.ds(j * FW, FW)]
                pltpu.make_async_copy(group[2 * k + j], into, sems.at[p]).start()


def ffn_kernel(meta_ref, own_ref, got_ref, grad_act_ref, *rest):
    w_refs = rest[:16]
    act_ref, grad_ref, keep_ref, send_ref, held, acc, part, sems = rest[16:]
    core = meta_ref[0]
    is_low = core == 0
    start_ffn(meta_ref, w_refs, held, sems)
    acc[...] = jnp.zeros_like(acc)
    part[:, BLK:] = jnp.zeros((SEQ, LANES - BLK), LOW)

    def project(n, carry):
        p = piece_at(meta_ref, n)
        wait_weights(held, sems, p)
        own = jnp.concatenate([own_ref[z, p] for z in range(RING)], axis=0)
        got = jnp.concatenate([got_ref[z, p] for z in range(RING)], axis=0)
        acc[...] += dot(join_rows(is_low, own, got)[:, :BLK], held[p], 1, 0)
        return carry

    lax.fori_loop(0, PIECES, project, 0)

    def units(t, carry):
        at = pl.multiple_of(t * 128, 128)
        grad_act = grad_act_ref[:, pl.ds(at, 128)]
        gate = acc[:, pl.ds(at, 128)]
        up = acc[:, pl.ds(at + FW, 128)]
        sigmoid = 1.0 / (1.0 + jnp.exp(-gate))
        silu = gate * sigmoid
        act_ref[:, pl.ds(at, 128)] = (silu * up).astype(LOW)
        grad_gate = grad_act * up * sigmoid * (1.0 + gate * (1.0 - sigmoid))
        grad_ref[:, pl.ds(at, 128)] = grad_gate.astype(LOW)
        grad_ref[:, pl.ds(at + FW, 128)] = (grad_act * silu).astype(LOW)
        return carry

    lax.fori_loop(0, FW // 128, units, 0)

    def spread(p, carry):
        split_rows(dot(grad_ref[...], held[p], 1, 1), part, core, p, keep_ref, send_ref)
        return carry

    lax.fori_loop(0, PIECES, spread, 0)


def feed_forward(meta, own, got, grad_act, w_gu):
    return pl.pallas_call(
        ffn_kernel,
        in_specs=[smem()] + [whole()] * 3 + [hbm()] * 16,
        out_specs=[whole()] * 4,
        out_shape=[
            jax.ShapeDtypeStruct((SEQ, FW), LOW),
            jax.ShapeDtypeStruct((SEQ, GU), LOW),
        ]
        + split_shapes(),
        scratch_shapes=[
            pltpu.VMEM((PIECES, BLK, GU), LOW),
            pltpu.VMEM((SEQ, GU), F32),
            pltpu.VMEM((SEQ, LANES), LOW),
            pltpu.SemaphoreType.DMA((PIECES,)),
        ],
        compiler_params=pltpu.CompilerParams(vmem_limit_bytes=VMEM),
        cost_estimate=cost(0, 0),
        name="feed_forward",
    )(meta, own, got, grad_act, *w_gu)


def halves_of(part_ref, xc_ref, q, at):
    rows = jnp.concatenate([part_ref[z, q] for z in range(RING)], axis=0)
    return rows[:, :BLK], xc_ref[q, at : at + 128][:, :BLK]


def merge_kernel(part_ref, xc_ref, one_ref, two_ref):
    for p in range(RING):
        for ref, q in ((one_ref, p), (two_ref, RING + p)):
            for z in range(RING):
                ref[p, 32 * z : 32 * z + 32] = part_ref[z, q]
            ref[p, 128:] = xc_ref[q]


def merge(part, cot):
    return pl.pallas_call(
        merge_kernel,
        in_specs=[whole()] * 2,
        out_specs=[whole()] * 2,
        out_shape=[jax.ShapeDtypeStruct((RING, 256, LANES), LOW)] * 2,
        compiler_params=pltpu.CompilerParams(vmem_limit_bytes=VMEM),
        cost_estimate=cost(0, 0),
        name="merge",
    )(part, cot)


def ffn_terms_kernel(meta_ref, own_ref, got_ref, *rest, axis):
    rights = rest[:8]
    outs = rest[8:12]
    acc = rest[12]
    is_low = meta_ref[0] == 0
    at = meta_ref[axis]
    for k, offset in enumerate(OFFSETS):
        source = lax.rem(at + offset + RING, RING)
        xn = join_rows(is_low, own_ref[source, :128], got_ref[source, :128])[:, :BLK]
        cot = join_rows(is_low, own_ref[source, 128:], got_ref[source, 128:])[:, :BLK]
        down = dot(cot, rights[2 * k][...], 0, 0)
        both = dot(xn, rights[2 * k + 1][...], 0, 0)
        if k == 0:
            acc[:, :FW] = down
            acc[:, FW:] = both
        else:
            acc[:, :FW] += down
            acc[:, FW:] += both
    for k, ref in enumerate(outs):
        ref[:, ATTN:] = acc[k * HALF : (k + 1) * HALF, :].astype(LOW)


def ffn_terms(meta, own, got, rights, axis):
    return pl.pallas_call(
        functools.partial(ffn_terms_kernel, axis=axis),
        in_specs=[smem()] + [whole()] * 10,
        out_specs=[whole()] * 4,
        out_shape=[jax.ShapeDtypeStruct((HALF, WIDE), LOW)] * 4,
        scratch_shapes=[pltpu.VMEM((BLK, 3 * FW), F32)],
        compiler_params=pltpu.CompilerParams(vmem_limit_bytes=VMEM),
        cost_estimate=cost(0, 0),
        name="terms_feed_forward",
    )(meta, own, got, *rights)


def fill_kernel(*refs):
    for k, ref in enumerate(refs[8:]):
        total = refs[0][k].astype(F32)
        for part in refs[1:4]:
            total = total + part[k].astype(F32)
        ref[...] = total.astype(LOW)


def fill(attn, ffn):
    return pl.pallas_call(
        fill_kernel,
        grid=(1,),
        in_specs=[pl.BlockSpec((RING, HALF, ATTN), lambda i: (0, 0, 0))] * 4 + [hbm()] * 4,
        out_specs=[pl.BlockSpec((HALF, ATTN), lambda i: (0, 0))] * 4,
        out_shape=[jax.ShapeDtypeStruct((HALF, WIDE), LOW)] * 4,
        input_output_aliases={4 + k: k for k in range(4)},
        compiler_params=pltpu.CompilerParams(vmem_limit_bytes=VMEM),
        cost_estimate=cost(0, 0),
        name="fill",
    )(*attn, *ffn)


def fetch_kind(is_first, refs, held, sem):
    for kind in range(2):

        @pl.when(is_first if kind == 0 else jnp.logical_not(is_first))
        def _():
            for k in range(RING):
                pltpu.make_async_copy(refs[RING * kind + k], held.at[k], sem).start()

    pltpu.make_async_copy(held, held, sem).wait()


def finish_kernel(meta_ref, *refs):
    out_ref, held, sem = refs[8:]
    fetch_kind(meta_ref[0] == 1, refs[:8], held, sem)
    total = held[0].astype(F32)
    for k in range(1, RING):
        total = total + held[k].astype(F32)
    out_ref[...] = total.astype(LOW)


def finish(meta, parts):
    return pl.pallas_call(
        finish_kernel,
        in_specs=[smem()] + [hbm()] * 8,
        out_specs=whole(),
        out_shape=jax.ShapeDtypeStruct((HALF, WIDE), LOW),
        scratch_shapes=[pltpu.VMEM((RING, HALF, WIDE), LOW), pltpu.SemaphoreType.DMA],
        compiler_params=pltpu.CompilerParams(vmem_limit_bytes=VMEM),
        cost_estimate=cost(0, 0),
        name="finish_other",
    )(meta, *parts[0], *parts[1])


def pick_sum(is_first, refs):
    total = jnp.where(is_first, refs[0][...], refs[4][...]).astype(F32)
    for k in range(1, 4):
        total = total + jnp.where(is_first, refs[k][...], refs[4 + k][...]).astype(F32)
    return total


def adam_kernel(meta_ref, w_ref, m_ref, v_ref, came, *rest):
    parts = rest[:8]
    wo_ref, mo_ref, vo_ref, grad, stay = rest[8:]
    is_low = meta_ref[0] == 0
    stay[...] = pick_sum(is_low, parts)
    rows = w_ref.shape[0]
    for start, at, width in MAP:
        mine = stay[:, at : at + width]
        other = came[:, at : at + width].astype(F32)
        grad[:, start : start + width] = jnp.where(is_low, mine, other)
        grad[:, start + width : start + 2 * width] = jnp.where(is_low, other, mine)
    row = pl.program_id(0) * rows + lax.broadcasted_iota(jnp.int32, (rows, 1), 0)
    valid = row < meta_ref[4]
    weight, first, second = adam_step(
        w_ref[...], m_ref[...], v_ref[...], grad[...], LEARN, DECAY
    )
    wo_ref[...] = jnp.where(valid, weight, 0.0)
    mo_ref[...] = jnp.where(valid, first, 0.0)
    vo_ref[...] = jnp.where(valid, second, 0.0)


def adam(meta, master, moment_one, moment_two, came, parts):
    rows = 32
    units = master.shape[1]

    def block(width):
        return pl.BlockSpec((rows, width), lambda i: (i, 0))

    return pl.pallas_call(
        adam_kernel,
        grid=(pl.cdiv(HALF, rows),),
        in_specs=[smem()] + [block(units)] * 3 + [block(WIDE)] * 9,
        out_specs=[block(units)] * 3,
        out_shape=[jax.ShapeDtypeStruct(master.shape, F32)] * 3,
        scratch_shapes=[pltpu.VMEM((rows, units), F32), pltpu.VMEM((rows, WIDE), F32)],
        compiler_params=pltpu.CompilerParams(vmem_limit_bytes=VMEM),
        name="adam",
    )(meta, master, moment_one, moment_two, came, *parts[0], *parts[1])


def rms_scale(values):
    return lax.rsqrt(jnp.sum(values * values, axis=(0, 2), keepdims=True) / D + EPS_NORM)


def rms_backward(grad_out, normed, scale, gain):
    grad_normed = grad_out * gain
    inner = jnp.sum(grad_normed * normed, axis=(0, 2), keepdims=True) / D
    return scale * (grad_normed - normed * inner), jnp.sum(grad_out * normed, axis=1)


def adam_step(weight, first, second, grad, rate, decay):
    first_new = BETA * first + (1.0 - BETA) * grad
    second_new = BETA * second + (1.0 - BETA) * grad * grad
    inverse = 1.0 / (1.0 - BETA**STEP)
    update = (first_new * inverse) / (jnp.sqrt(second_new * inverse) + EPS_ADAM)
    return (weight - rate * (update + decay * weight), first_new, second_new)


def stage(*values):
    return lax.optimization_barrier(values)


def shards(
    tokens, cotangent, segments, owner, master, moment_one, moment_two, gains, gain_one, gain_two
):
    core = lax.axis_index("core")
    yl = lax.axis_index("yl")
    z = lax.axis_index("z")
    x = lax.axis_index(X)
    y = lax.axis_index("yh") * 2 + yl
    count = jnp.sum((owner == (y // 2 * RING + x) * 2 + core).astype(jnp.int32)) - yl * HALF
    place = jnp.stack([core, z, x, y]).astype(jnp.int32)
    meta = jnp.stack([core, z, x, y, count]).astype(jnp.int32)
    along = (Y, X)
    across = (X, Y)

    def add_core(keep, other):
        return (keep.astype(F32) + other.astype(F32)).astype(LOW)

    def split_z(block):
        return lax.all_to_all(block, "z", split_axis=0, concat_axis=0, tiled=True)

    def sum_z(block):
        return jnp.sum(block.astype(F32), axis=0)

    def all_z(block):
        return split_z(jnp.broadcast_to(block[None], (RING, *block.shape)))

    own, send = pack(place, owner, master)
    got = swap_core(send)
    first = jnp.where(core == 0, own, got)
    second = jnp.where(core == 0, got, own)
    first, second, owner, tokens, cotangent = stage(first, second, owner, tokens, cotangent)

    near_first = near(first, X)
    near_second = near(second, Y)
    numbers = jnp.zeros((8, D), LOW).at[0, :SEQ].set(segments.astype(LOW))
    tokens = swap_sequences(jnp.concatenate([tokens, numbers], axis=0))
    onehot = (owner[:, None] == jnp.arange(16, dtype=jnp.int32)[None, :]).astype(jnp.int32)
    rank = ranks(onehot)
    slot = (owner * CAP + rank)[:, None]
    ids = slot_ids(x, y)
    parts = jnp.concatenate([three_parts(gains), jnp.zeros((10, D), LOW)], axis=0)
    near_first, near_second, slot, ids, parts, cotangent = stage(
        near_first, near_second, slot, ids, parts, cotangent
    )

    blocks = [
        (first, *near_first, *halves(*near_first, X, WIDE_CUT)),
        (second, *near_second, *halves(*near_second, Y, WIDE_CUT)),
    ]
    attn = [assemble(b, 0) for b in blocks]
    attn, blocks, tokens, cotangent = stage(attn, blocks, tokens, cotangent)

    attn_near = [near(b, axis) for b, axis in zip(attn, along)]
    position = jnp.arange(SEQ, dtype=F32)
    freq = jnp.exp(-jnp.log(THETA) * (2.0 * jnp.arange(HD // 2, dtype=F32) / HD))
    angle = position[:, None] * freq[None, :]
    tables = (
        jnp.concatenate([jnp.cos(angle)] * 2, axis=1),
        jnp.concatenate([jnp.sin(angle)] * 2, axis=1),
    )
    segment = tokens[128, :SEQ].astype(jnp.int32)
    segs = (segment[:, None], segment[None, :])
    down = [assemble(b, 1) for b in blocks]
    cotangent = swap_sequences(cotangent)
    attn_near, down, tables, segs, tokens, cotangent = stage(
        attn_near, down, tables, segs, tokens, cotangent
    )
    down_near = [near(b, axis) for b, axis in zip(down, along)]
    xn_own, inputs, gain = tokens_to_slots(meta, slot, ids, tokens, gains, parts)
    gate = [assemble(b, 2) for b in blocks]
    turned = (slot.reshape(1, D), ids)
    down_near, blocks, gate, turned, xn_own, inputs, gain, cotangent = stage(
        down_near, blocks, gate, turned, xn_own, inputs, gain, cotangent
    )
    pair_far = [far(q[0], d[1], axis) for q, d, axis in zip(attn_near, down_near, along)]
    up = [assemble(b, 3) for b in blocks]
    xn_got = swap_core(xn_own)
    cot_own, cot_z = cot_to_slots(meta, slot, ids, cotangent)
    pair_far, gate, up, xn_got, cot_own, cot_z = stage(pair_far, gate, up, xn_got, cot_own, cot_z)
    w_attn = []
    w_down = []
    for kind in range(2):
        w_attn += [attn[kind], *attn_near[kind], pair_far[kind][0]]
        w_down += [down[kind], *down_near[kind], pair_far[kind][1]]

    gate_near = [near(b, axis) for b, axis in zip(gate, along)]
    *qkv, attended, keep, send = attention_forward(meta, xn_own, xn_got, tables, segs, w_attn)
    cot_got = swap_core(cot_own)
    gate_near, up, keep, send, cot_got = stage(gate_near, up, keep, send, cot_got)
    up_near = [near(b, axis) for b, axis in zip(up, along)]
    got = split_z(add_core(keep, swap_core(send)))
    grad_act = down_back(meta, cot_own, cot_got, w_down)
    up_near, gate_near, got, grad_act = stage(up_near, gate_near, got, grad_act)
    gu_far = [far(g[0], u[1], axis) for g, u, axis in zip(gate_near, up_near, along)]
    hidden = inputs + sum_z(got)
    scale_two = rms_scale(hidden)
    normed_two = hidden * scale_two
    xn_two = all_z((normed_two * gain[:, 1:2]).astype(LOW))
    gu_far, xn_two = stage(gu_far, xn_two)
    xn_two_got = swap_core(xn_two)
    left_sent = merge(xn_two, cot_own)
    xn_two, xn_two_got, grad_act, left_sent = stage(xn_two, xn_two_got, grad_act, left_sent)
    w_gu = []
    for kind in range(2):
        w_gu += [gate[kind], up[kind]]
        w_gu += [gate_near[kind][0], up_near[kind][0], gate_near[kind][1], up_near[kind][1]]
        w_gu += [*gu_far[kind]]

    act, grad_gu, keep, send = feed_forward(meta, xn_two, xn_two_got, grad_act, w_gu)
    def exchange(block, axis):
        return lax.all_to_all(block, axis, split_axis=0, concat_axis=0, tiled=True)

    lefts = [exchange(left_sent[0], Y)]
    act, grad_gu, keep, send, lefts = stage(act, grad_gu, keep, send, lefts)
    gu_near = [near(grad_gu, axis) for axis in along]
    got = split_z(add_core(keep, swap_core(send)))
    keep_mlp, send_mlp = down_forward(meta, act, w_down)
    gu_near, got, keep_mlp, send_mlp, act = stage(gu_near, got, keep_mlp, send_mlp, act)
    act_near = [near(act, axis) for axis in along]
    lefts_got = [swap_core(lefts[0])]
    mlp_both = add_core(keep_mlp, swap_core(send_mlp))
    grad_xn_two = sum_z(got)
    grad_norm_two, gain_grad_two = rms_backward(grad_xn_two, normed_two, scale_two, gain[:, 1:2])
    grad_hidden = cot_z + grad_norm_two
    grad_branch = lax.all_gather(grad_hidden.astype(LOW), "z", axis=0, tiled=False)
    lefts.append(exchange(left_sent[1], X))
    act_near, grad_branch, grad_hidden, gain_grad_two, lefts, lefts_got, gu_near, mlp_both = stage(
        act_near, grad_branch, grad_hidden, gain_grad_two, lefts, lefts_got, gu_near, mlp_both
    )
    grad_branch_got = swap_core(grad_branch)
    ends = [far(a[0], g[1], axis) for a, g, axis in zip(act_near, gu_near, along)]

    xns = (xn_own, xn_got)
    keep, send, *terms = attention_backward(
        meta, grad_branch, grad_branch_got, tables, segs, (*qkv, attended), xns, w_attn
    )
    attn_terms = (terms[:4], terms[4:])
    mlp = lax.psum_scatter(mlp_both, "z", scatter_dimension=0, tiled=True)[0]
    ends, keep, send, attn_terms, lefts, mlp = stage(ends, keep, send, attn_terms, lefts, mlp)

    def direct(first, second, axes):
        _, back, ahead, last = first
        _, back_two, ahead_two, last_two = second
        one = (move(ahead, axes[0], 1), move(back, axes[0], -1), move(last, axes[0], 2))
        up = move(ahead_two, axes[1], 1)
        down = move(back_two, axes[1], -1)
        return one, up, down, last_two

    attn_nears = [
        (move(t[2], axis, 1), move(t[1], axis, -1)) for t, axis in zip(attn_terms, along)
    ]

    def rights_of(kind):
        rights = (act, grad_gu)
        for n in range(2):
            rights += (act_near[kind][n], gu_near[kind][n])
        return rights + tuple(ends[kind])

    ffn_sums = [ffn_terms(meta, lefts[0], lefts_got[0], rights_of(0), 3)]
    lefts_got.append(swap_core(lefts[1]))
    got = split_z(add_core(keep, swap_core(send)))
    attn_nears, attn_terms, lefts, lefts_got, ffn_sums, got = stage(
        attn_nears, attn_terms, lefts, lefts_got, ffn_sums, got
    )
    attn_others = [
        (*n, move(t[3], axis, 2)) for n, t, axis in zip(attn_nears, attn_terms, along)
    ]
    ffn_sums.append(ffn_terms(meta, lefts[1], lefts_got[1], rights_of(1), 2))
    grad_xn_one = sum_z(got)
    scale_one = rms_scale(inputs)
    grad_norm_one, gain_grad_one = rms_backward(
        grad_xn_one, inputs * scale_one, scale_one, gain[:, 0:1]
    )
    grad_tokens_z = (grad_hidden + grad_norm_one).astype(LOW)
    output_z = (hidden + mlp.astype(F32)).astype(LOW)
    gain_grads = three_parts(jnp.stack([gain_grad_one, gain_grad_two], axis=0))
    gain_grads = jnp.swapaxes(gain_grads, 0, 1)
    blank = jnp.zeros((PIECES, 10, LANES), LOW)
    last = from_slots(
        jnp.concatenate([output_z, grad_tokens_z, gain_grads, blank], axis=1), *turned
    )
    attn_others, ffn_sums, last = stage(attn_others, ffn_sums, last)
    blocks = [fill((t[0], *o), f) for t, o, f in zip(attn_terms, attn_others, ffn_sums)]
    part = lax.all_gather(last, "z", axis=0, tiled=False)
    one, up, down, last_two = direct(*blocks, across)
    up, down, last_two = stage(up, down, last_two)
    others = (one, (up, down, move(last_two, across[1], 2)))
    others, owns = stage(others, [b[0] for b in blocks])
    totals = [(b, *o) for b, o in zip(owns, others)]
    send, totals = stage(finish(meta, totals), totals)
    came = swap_core(send)
    moved = swap_sequences(jnp.swapaxes(part[:, :64].reshape(RING, 2, 32, D), 0, 1))
    gain_grads = part[:, 64:70].astype(F32).sum(axis=0)
    gain_grads = gain_grads[:2] + gain_grads[2:4] + gain_grads[4:6]
    gain_other = swap_core(gain_grads)
    came, gain_other, totals = stage(came, gain_other, totals)

    def sum_along(value, axis):
        back, ahead = near(value, axis)
        return (value + move(value, axis, 2)) + (back + ahead)

    gain_grads = sum_along(gain_grads + gain_other, X)
    new_master, new_one, new_two = adam(meta, master, moment_one, moment_two, came, totals)
    gain_grads, new_master, moved = stage(gain_grads, new_master, moved)
    gain_grads = sum_along(gain_grads, Y)
    output = moved[0].reshape(128, D)
    grad_tokens = moved[1].reshape(128, D)
    new_gains, new_gain_one, new_gain_two = adam_step(
        gains, gain_one, gain_two, gain_grads, LEARN_GAIN, 0.0
    )
    return (
        output,
        grad_tokens,
        new_master,
        new_one,
        new_two,
        new_gains,
        new_gain_one,
        new_gain_two,
    )


def solution(mesh):
    fine = Mesh(mesh.devices.reshape(2, 4, 2, 2, 4), ("yh", "x", "core", "yl", "z"))
    rows = ("yh", "x", "core", "yl")
    in_specs = (
        P(rows, None),
        P(rows, None),
        P(("yh", "x", "core")),
        P(),
        P(rows, "z"),
        P(rows, "z"),
        P(rows, "z"),
        P(),
        P(),
        P(),
    )
    out_specs = (
        P(rows, None),
        P(rows, None),
        P(rows, "z"),
        P(rows, "z"),
        P(rows, "z"),
        P(),
        P(),
        P(),
    )
    return jax.shard_map(shards, mesh=fine, in_specs=in_specs, out_specs=out_specs, check_vma=False)
```

```python
import functools

import jax
import jax.numpy as jnp
from jax import lax
from jax.experimental import pallas as pl
from jax.experimental.pallas import tpu as pltpu
from jax.sharding import Mesh
from jax.sharding import PartitionSpec as P

HD = 80
STEP = 5
D = 2560
CAP = 240
HALF = 120
SEQ = 256
RING = 4

EPS_NORM = 1e-05
EPS_ADAM = 1e-08
THETA = 1000000.0
BETA = 0.5
LEARN = 0.05
LEARN_GAIN = 0.2
DECAY = 0.1
NEG_BIG = -1e30

X = "x"
Y = ("yh", "yl")
OFFSETS = (0, -1, 1, 2)
LOW = jnp.bfloat16
F32 = jnp.float32

HEADS = 4
QW = 320
KW = 80
FW = 896
ATTN = 896
GU = 2 * FW
WIDE = ATTN + 3 * FW
WIDE_CUT = 1792
MAP = (
    (0, 320, QW),
    (640, 640, KW),
    (800, 720, KW),
    (960, 1792, FW),
    (2752, 2688, FW),
    (4544, 0, QW),
    (5184, 896, FW),
)
PIECES = 8
BLK = 4 * HALF
LANES = 512
VMEM = 60 * 1024 * 1024


def dot(left, right, left_axis, right_axis):
    return lax.dot_general(
        left, right, (((left_axis,), (right_axis,)), ((), ())), preferred_element_type=F32
    )


def move(block, axis, distance):
    route = [(i, (i + distance) % RING) for i in range(RING)]
    return lax.ppermute(block, axis, route)


def swap_core(block):
    return lax.ppermute(block, "core", [(0, 1), (1, 0)])


def swap_sequences(block):
    return lax.ppermute(block, ("core", "yl"), [(0, 0), (1, 2), (2, 1), (3, 3)])


def near(block, axis):
    return move(block, axis, 1), move(block, axis, -1)


def far(back, ahead, axis):
    return move(back, axis, 1), move(ahead, axis, -1)


def halves(back, ahead, axis, cut):
    return far(back[:, :cut], ahead[:, cut:], axis)


def slot_ids(x, y):
    offsets = jnp.array(OFFSETS, jnp.int32)
    every = jnp.arange(RING, dtype=jnp.int32)
    rows = jnp.arange(HALF, dtype=jnp.int32)

    def slots(xx, yy, core):
        return (((yy // 2) * RING + xx) * 2 + core) * CAP + (yy % 2) * HALF

    first = slots(((x + offsets) % RING)[None, :, None], every[:, None, None], 0) + rows
    second = slots(every[:, None, None], ((y + offsets) % RING)[None, :, None], 1) + rows
    ids = jnp.concatenate([first, second], axis=0).reshape(PIECES, 1, BLK)
    return jnp.pad(ids, ((0, 0), (0, 0), (0, LANES - BLK)), constant_values=-1)


def ranks(onehot):
    blocks = onehot.reshape(20, 128, 16)
    row = jnp.arange(128, dtype=jnp.int32)
    earlier = (row[None, :] < row[:, None]).astype(LOW)
    within = jnp.einsum("ij,bjf->bif", earlier, blocks.astype(LOW), preferred_element_type=F32)
    totals = jnp.sum(blocks, axis=1).astype(LOW)
    before = dot(earlier[:20, :20], totals, 1, 0)
    counts = (within + before[:, None, :]) * blocks.astype(F32)
    return jnp.sum(counts, axis=2).astype(jnp.int32).reshape(-1)


def three_parts(values):
    high = lax.reduce_precision(values, 8, 7)
    rest = values - high
    middle = lax.reduce_precision(rest, 8, 7)
    return jnp.concatenate([high, middle, rest - middle], axis=0).astype(LOW)


def whole():
    return pl.BlockSpec(memory_space=pltpu.VMEM)


def hbm():
    return pl.BlockSpec(memory_space=pl.ANY)


def smem():
    return pl.BlockSpec(memory_space=pltpu.SMEM)


def cost(flops, size):
    return pl.CostEstimate(flops=flops, bytes_accessed=size, transcendentals=0)


def pack_kernel(meta_ref, owner_ref, master_ref, own_ref, send_ref):
    is_low = meta_ref[0] == 0
    share = (meta_ref[3] // 2 * RING + meta_ref[2]) * 2 + meta_ref[0]
    count = jnp.sum((owner_ref[...] == share).astype(jnp.int32)) - lax.rem(meta_ref[3], 2) * HALF
    valid = lax.broadcasted_iota(jnp.int32, (HALF, 1), 0) < count
    blank = jnp.zeros((HALF, ATTN - 800), LOW)
    own_ref[:, 800:ATTN] = blank
    send_ref[:, 800:ATTN] = blank
    for start, at, width in MAP:
        low = jnp.where(valid, master_ref[:, start : start + width], 0.0)
        high = jnp.where(valid, master_ref[:, start + width : start + 2 * width], 0.0)
        own_ref[:, at : at + width] = jnp.where(is_low, low, high).astype(LOW)
        send_ref[:, at : at + width] = jnp.where(is_low, high, low).astype(LOW)


def pack(meta, owner, master):
    return pl.pallas_call(
        pack_kernel,
        in_specs=[smem(), whole(), whole()],
        out_specs=[whole()] * 2,
        out_shape=[jax.ShapeDtypeStruct((HALF, WIDE), LOW)] * 2,
        compiler_params=pltpu.CompilerParams(vmem_limit_bytes=VMEM),
        name="pack",
    )(meta, owner.reshape(20, 128), master)


def assemble_kernel(*refs):
    out = refs[4]
    for k, ref in enumerate(refs[:4]):
        out[k * HALF : (k + 1) * HALF, :] = ref[...]


def assemble(blocks, j):
    block, back, ahead, one, two = blocks
    specs = [pl.BlockSpec((HALF, FW), lambda i: (0, j))] * 3
    specs += [pl.BlockSpec((HALF, FW), lambda i: (0, j % 2))]
    return pl.pallas_call(
        assemble_kernel,
        grid=(1,),
        in_specs=specs,
        out_specs=pl.BlockSpec((BLK, FW), lambda i: (0, 0)),
        out_shape=jax.ShapeDtypeStruct((BLK, FW), LOW),
        compiler_params=pltpu.CompilerParams(vmem_limit_bytes=VMEM),
        cost_estimate=cost(0, 0),
        name="assemble",
    )(block, back, ahead, one if j < 2 else two)


def one_hot(slot_ref, ids_ref):
    return jnp.where(slot_ref[...] == ids_ref[0], 1.0, 0.0).astype(LOW)


def tokens_kernel(meta_ref, slot_ref, ids_ref, tokens_ref, gains_ref, parts_ref, xn_ref, in_ref, gain_ref, rows):
    @pl.when(pl.program_id(0) == 0)
    def _():
        at = pl.multiple_of(meta_ref[1] * 32, 32)
        tokens = tokens_ref[:128].astype(F32)
        scale = lax.rsqrt(jnp.sum(tokens * tokens, axis=1, keepdims=True) / D + EPS_NORM)
        rows[:128] = (tokens * scale * gains_ref[0:1]).astype(LOW)
        rows[128:160] = tokens_ref[pl.ds(at, 32)]
        rows[160:] = parts_ref[...]

    placed = dot(rows[...], one_hot(slot_ref, ids_ref), 1, 0)
    xn_ref[0] = placed[:128].astype(LOW)
    in_ref[0] = placed[128:160]
    gain_ref[0] = placed[160:162] + placed[162:164] + placed[164:166]


def cot_kernel(meta_ref, slot_ref, ids_ref, cot_ref, out_ref, z_ref, rows):
    @pl.when(pl.program_id(0) == 0)
    def _():
        rows[:128] = cot_ref[...]
        rows[128:] = cot_ref[pl.ds(pl.multiple_of(meta_ref[1] * 32, 32), 32)]

    placed = dot(rows[...], one_hot(slot_ref, ids_ref), 1, 0)
    out_ref[0] = placed[:128].astype(LOW)
    z_ref[0] = placed[128:]


def to_slots(kernel, meta, slot, ids, args, outs, rows, name):
    def same(shape):
        return pl.BlockSpec(shape, lambda p: (0, 0))

    return pl.pallas_call(
        kernel,
        grid=(PIECES,),
        in_specs=[
            smem(),
            same((D, 1)),
            pl.BlockSpec((1, 1, LANES), lambda p: (p, 0, 0)),
            *(same(a.shape) for a in args),
        ],
        out_specs=[pl.BlockSpec((1, n, LANES), lambda p: (p, 0, 0)) for n, _ in outs],
        out_shape=[jax.ShapeDtypeStruct((PIECES, n, LANES), kind) for n, kind in outs],
        scratch_shapes=[pltpu.VMEM((rows, D), LOW)],
        compiler_params=pltpu.CompilerParams(vmem_limit_bytes=VMEM),
        cost_estimate=cost(0, 0),
        name=name,
    )(meta, slot, ids, *args)


def tokens_to_slots(meta, slot, ids, tokens, gains, parts):
    outs = [(128, LOW), (32, F32), (2, F32)]
    args = (tokens, gains, parts)
    return to_slots(tokens_kernel, meta, slot, ids, args, outs, 176, "tokens_to_slots")


def cot_to_slots(meta, slot, ids, cotangent):
    outs = [(128, LOW), (32, F32)]
    return to_slots(cot_kernel, meta, slot, ids, (cotangent,), outs, 160, "cotangent_to_slots")


def unplace_kernel(slot_ref, ids_ref, rows_ref, out_ref, acc):
    ids = jnp.transpose(jnp.broadcast_to(ids_ref[0], (8, LANES)))[:, :1]
    place = jnp.where(ids == slot_ref[...], 1.0, 0.0).astype(LOW)

    @pl.when(pl.program_id(0) == 0)
    def _():
        acc[...] = jnp.zeros_like(acc)

    acc[...] += dot(rows_ref[0], place, 1, 0)

    @pl.when(pl.program_id(0) == PIECES - 1)
    def _():
        out_ref[...] = acc[...].astype(LOW)


def from_slots(rows, slot, ids):
    n = rows.shape[1]
    return pl.pallas_call(
        unplace_kernel,
        grid=(PIECES,),
        in_specs=[
            pl.BlockSpec((1, D), lambda p: (0, 0)),
            pl.BlockSpec((1, 1, LANES), lambda p: (p, 0, 0)),
            pl.BlockSpec((1, n, LANES), lambda p: (p, 0, 0)),
        ],
        out_specs=pl.BlockSpec((n, D), lambda p: (0, 0)),
        out_shape=jax.ShapeDtypeStruct((n, D), LOW),
        scratch_shapes=[pltpu.VMEM((n, D), F32)],
        compiler_params=pltpu.CompilerParams(vmem_limit_bytes=VMEM),
        cost_estimate=cost(0, 0),
        name="from_slots",
    )(slot, ids, rows)


def start_weights(meta_ref, refs, held, sems):
    x = meta_ref[2]
    y = meta_ref[3]
    for base, at, group in ((0, y, refs[:4]), (RING, x, refs[4:])):
        for ref, offset in zip(group, OFFSETS):
            p = base + lax.rem(at + offset + RING, RING)
            pltpu.make_async_copy(ref, held.at[p], sems.at[p]).start()


def piece_at(meta_ref, n):
    kind = n // RING
    k = lax.rem(n, RING)
    offset = jnp.where(k == 1, 3, jnp.where(k == 2, 1, jnp.where(k == 3, 2, 0)))
    at = jnp.where(kind == 0, meta_ref[3], meta_ref[2])
    return kind * RING + lax.rem(at + offset, RING)


def wait_weights(held, sems, p):
    pltpu.make_async_copy(held.at[p], held.at[p], sems.at[p]).wait()


def split_rows(value, scratch, core, p, keep_ref, send_ref):
    scratch[:, :BLK] = value.astype(LOW)
    for z in range(RING):
        keep_ref[z, p] = scratch[pl.ds(pl.multiple_of(core * 128 + 32 * z, 32), 32), :]
        send_ref[z, p] = scratch[pl.ds(pl.multiple_of((1 - core) * 128 + 32 * z, 32), 32), :]


def join_rows(is_low, own, got):
    return jnp.concatenate(
        [jnp.where(is_low, own, got), jnp.where(is_low, got, own)], axis=0
    )


def rope(values, cosine, sine):
    half = HD // 2
    turned = jnp.concatenate([-values[:, half:], values[:, :half]], axis=1)
    return values * cosine + turned * sine


def head_probs(query, keys, mask):
    scores = dot(query, keys, 1, 1) * HD ** (-0.5)
    scores = jnp.where(mask, scores, NEG_BIG)
    weight = jnp.exp(scores - jnp.max(scores, axis=1, keepdims=True))
    return weight / jnp.sum(weight, axis=1, keepdims=True)


def causal_mask(seg_col, seg_row):
    rows = lax.broadcasted_iota(jnp.int32, (SEQ, SEQ), 0)
    cols = lax.broadcasted_iota(jnp.int32, (SEQ, SEQ), 1)
    return (seg_col == seg_row) & (cols <= rows)


def attention_kernel(
    meta_ref, own_ref, got_ref, cos_ref, sin_ref, segc_ref, segr_ref, *rest
):
    w_refs = rest[:8]
    q_ref, k_ref, v_ref, o_ref, keep_ref, send_ref, held, acc, part, sems = rest[8:]
    core = meta_ref[0]
    is_low = core == 0
    start_weights(meta_ref, w_refs, held, sems)
    acc[...] = jnp.zeros_like(acc)
    part[:, BLK:] = jnp.zeros((SEQ, LANES - BLK), LOW)

    def project(n, carry):
        p = piece_at(meta_ref, n)
        wait_weights(held, sems, p)
        rows = join_rows(is_low, own_ref[p], got_ref[p])
        acc[...] += dot(rows[:, :BLK], held[p, :, 256:], 1, 0)
        return carry

    lax.fori_loop(0, PIECES, project, 0)
    cosine = cos_ref[...]
    sine = sin_ref[...]
    mask = causal_mask(segc_ref[...], segr_ref[...])
    projected = acc[...]
    keys = rope(projected[:, 384:464], cosine, sine).astype(LOW)
    values = projected[:, 464:544].astype(LOW)
    k_ref[...] = keys
    v_ref[...] = values
    outs = []
    for h in range(HEADS):
        query = rope(projected[:, 64 + h * HD : 64 + (h + 1) * HD], cosine, sine).astype(LOW)
        q_ref[h] = query
        probs = head_probs(query, keys, mask)
        outs.append(dot(probs.astype(LOW), values, 1, 0))
    outs.append(jnp.zeros((SEQ, 64), F32))
    attended = jnp.concatenate(outs, axis=1).astype(LOW)
    o_ref[...] = attended

    def spread(p, carry):
        split_rows(dot(attended, held[p, :, :384], 1, 1), part, core, p, keep_ref, send_ref)
        return carry

    lax.fori_loop(0, PIECES, spread, 0)


def split_shapes():
    return [
        jax.ShapeDtypeStruct((RING, PIECES, 32, LANES), LOW),
        jax.ShapeDtypeStruct((RING, PIECES, 32, LANES), LOW),
    ]


def attention_forward(meta, own, got, tables, segs, w_attn):
    return pl.pallas_call(
        attention_kernel,
        in_specs=[smem()] + [whole()] * 6 + [hbm()] * 8,
        out_specs=[whole()] * 6,
        out_shape=[
            jax.ShapeDtypeStruct((HEADS, SEQ, HD), LOW),
            jax.ShapeDtypeStruct((SEQ, HD), LOW),
            jax.ShapeDtypeStruct((SEQ, HD), LOW),
            jax.ShapeDtypeStruct((SEQ, 384), LOW),
        ]
        + split_shapes(),
        scratch_shapes=[
            pltpu.VMEM((PIECES, BLK, ATTN), LOW),
            pltpu.VMEM((SEQ, ATTN - 256), F32),
            pltpu.VMEM((SEQ, LANES), LOW),
            pltpu.SemaphoreType.DMA((PIECES,)),
        ],
        compiler_params=pltpu.CompilerParams(vmem_limit_bytes=VMEM),
        cost_estimate=cost(0, 0),
        name="attention_forward",
    )(meta, own, got, *tables, *segs, *w_attn)


def put_blocks(ref, value):
    for k in range(RING):
        ref[k] = value[k * HALF : (k + 1) * HALF].astype(LOW)


def attention_back_kernel(
    meta_ref, own_ref, got_ref, cos_ref, sin_ref, segc_ref, segr_ref, q_ref, k_ref, v_ref, o_ref, xc_ref, xc_got_ref, *rest
):
    w_refs = rest[:8]
    keep_ref, send_ref = rest[8:10]
    outs = rest[10:18]
    held, acc, part, sems = rest[18:]
    core = meta_ref[0]
    is_low = core == 0
    start_weights(meta_ref, w_refs, held, sems)
    acc[...] = jnp.zeros_like(acc)
    part[:, BLK:] = jnp.zeros((SEQ, LANES - BLK), LOW)

    def project(n, carry):
        p = piece_at(meta_ref, n)
        wait_weights(held, sems, p)
        own = jnp.concatenate([own_ref[z, p] for z in range(RING)], axis=0)
        got = jnp.concatenate([got_ref[z, p] for z in range(RING)], axis=0)
        acc[...] += dot(join_rows(is_low, own, got)[:, :BLK], held[p, :, :384], 1, 0)
        return carry

    lax.fori_loop(0, PIECES, project, 0)
    cosine = cos_ref[...]
    sine = -sin_ref[...]
    mask = causal_mask(segc_ref[...], segr_ref[...])
    grad_att = acc[...]
    keys = k_ref[...]
    values = v_ref[...]
    factor = HD ** (-0.5)
    grads = []
    grad_keys = jnp.zeros((SEQ, HD), F32)
    grad_values = jnp.zeros((SEQ, HD), F32)
    for h in range(HEADS):
        query = q_ref[h]
        grad_o = grad_att[:, h * HD : (h + 1) * HD].astype(LOW)
        probs = head_probs(query, keys, mask)
        grad_probs = dot(grad_o, values, 1, 1)
        inner = jnp.sum(probs * grad_probs, axis=1, keepdims=True)
        grad_scores = (probs * (grad_probs - inner)).astype(LOW)
        grads.append(rope(dot(grad_scores, keys, 1, 0) * factor, cosine, sine))
        grad_keys += dot(grad_scores, query, 0, 0)
        grad_values += dot(probs.astype(LOW), grad_o, 0, 0)
    grads.append(rope(grad_keys * factor, cosine, sine))
    grads.append(grad_values)
    zeros = [jnp.zeros((SEQ, 64), F32)]
    ends = [jnp.zeros((SEQ, 96), F32)]
    grad_qkv = jnp.concatenate(zeros + grads + ends, axis=1).astype(LOW)

    def spread(p, carry):
        split_rows(dot(grad_qkv, held[p, :, 256:], 1, 1), part, core, p, keep_ref, send_ref)
        return carry

    lax.fori_loop(0, PIECES, spread, 0)

    for kind in range(2):
        for k in range(RING):
            q = kind * RING + lax.rem(meta_ref[3 - kind] + OFFSETS[k] + RING, RING)
            own = jnp.concatenate([own_ref[z, q] for z in range(RING)], axis=0)
            got = jnp.concatenate([got_ref[z, q] for z in range(RING)], axis=0)
            grad = join_rows(is_low, own, got)[:, :BLK]
            xn = join_rows(is_low, xc_ref[q], xc_got_ref[q])[:, :BLK]
            one = dot(grad, o_ref[...], 0, 0)
            two = dot(xn, grad_qkv, 0, 0)
            terms = jnp.concatenate([one[:, :QW], two[:, 64:]], axis=1)
            put_blocks(outs[RING * kind + k], terms)


def attention_backward(meta, own, got, tables, segs, qkvo, xcs, w_attn):
    return pl.pallas_call(
        attention_back_kernel,
        in_specs=[smem()] + [whole()] * 12 + [hbm()] * 8,
        out_specs=[whole()] * 10,
        out_shape=split_shapes() + [jax.ShapeDtypeStruct((RING, HALF, ATTN), LOW)] * 8,
        scratch_shapes=[
            pltpu.VMEM((PIECES, BLK, ATTN), LOW),
            pltpu.VMEM((SEQ, 384), F32),
            pltpu.VMEM((SEQ, LANES), LOW),
            pltpu.SemaphoreType.DMA((PIECES,)),
        ],
        compiler_params=pltpu.CompilerParams(vmem_limit_bytes=VMEM),
        cost_estimate=cost(0, 0),
        name="attention_backward",
    )(meta, own, got, *tables, *segs, *qkvo, *xcs, *w_attn)


def down_back_kernel(meta_ref, cot_own_ref, cot_got_ref, *rest):
    w_refs = rest[:8]
    out_ref, held, sems = rest[8:]
    is_low = meta_ref[0] == 0
    start_weights(meta_ref, w_refs, held, sems)
    out_ref[...] = jnp.zeros_like(out_ref)

    def project(n, carry):
        p = piece_at(meta_ref, n)
        wait_weights(held, sems, p)
        cot = join_rows(is_low, cot_own_ref[p], cot_got_ref[p])
        out_ref[...] += dot(cot[:, :BLK], held[p], 1, 0)
        return carry

    lax.fori_loop(0, PIECES, project, 0)


def down_back(meta, cot_own, cot_got, w_down):
    return pl.pallas_call(
        down_back_kernel,
        in_specs=[smem()] + [whole()] * 2 + [hbm()] * 8,
        out_specs=whole(),
        out_shape=jax.ShapeDtypeStruct((SEQ, FW), F32),
        scratch_shapes=[
            pltpu.VMEM((PIECES, BLK, FW), LOW),
            pltpu.SemaphoreType.DMA((PIECES,)),
        ],
        compiler_params=pltpu.CompilerParams(vmem_limit_bytes=VMEM),
        cost_estimate=cost(0, 0),
        name="down_backward",
    )(meta, cot_own, cot_got, *w_down)


def down_kernel(meta_ref, act_ref, *rest):
    w_refs = rest[:8]
    keep_ref, send_ref, held, part, sems = rest[8:]
    core = meta_ref[0]
    start_weights(meta_ref, w_refs, held, sems)
    part[:, BLK:] = jnp.zeros((SEQ, LANES - BLK), LOW)

    def spread(n, carry):
        p = piece_at(meta_ref, n)
        wait_weights(held, sems, p)
        split_rows(dot(act_ref[...], held[p], 1, 1), part, core, p, keep_ref, send_ref)
        return carry

    lax.fori_loop(0, PIECES, spread, 0)


def down_forward(meta, act, w_down):
    return pl.pallas_call(
        down_kernel,
        in_specs=[smem(), whole()] + [hbm()] * 8,
        out_specs=[whole()] * 2,
        out_shape=split_shapes(),
        scratch_shapes=[
            pltpu.VMEM((PIECES, BLK, FW), LOW),
            pltpu.VMEM((SEQ, LANES), LOW),
            pltpu.SemaphoreType.DMA((PIECES,)),
        ],
        compiler_params=pltpu.CompilerParams(vmem_limit_bytes=VMEM),
        cost_estimate=cost(0, 0),
        name="down_forward",
    )(meta, act, *w_down)


def start_ffn(meta_ref, refs, held, sems):
    x = meta_ref[2]
    y = meta_ref[3]
    for base, at, group in ((0, y, refs[:8]), (RING, x, refs[8:])):
        for k, offset in enumerate(OFFSETS):
            p = base + lax.rem(at + offset + RING, RING)
            for j in range(2):
                into = held.at[p, :, pl.ds(j * FW, FW)]
                pltpu.make_async_copy(group[2 * k + j], into, sems.at[p]).start()


def ffn_kernel(meta_ref, own_ref, got_ref, grad_act_ref, *rest):
    w_refs = rest[:16]
    act_ref, grad_ref, keep_ref, send_ref, held, acc, part, sems = rest[16:]
    core = meta_ref[0]
    is_low = core == 0
    start_ffn(meta_ref, w_refs, held, sems)
    acc[...] = jnp.zeros_like(acc)
    part[:, BLK:] = jnp.zeros((SEQ, LANES - BLK), LOW)

    def project(n, carry):
        p = piece_at(meta_ref, n)
        wait_weights(held, sems, p)
        own = jnp.concatenate([own_ref[z, p] for z in range(RING)], axis=0)
        got = jnp.concatenate([got_ref[z, p] for z in range(RING)], axis=0)
        acc[...] += dot(join_rows(is_low, own, got)[:, :BLK], held[p], 1, 0)
        return carry

    lax.fori_loop(0, PIECES, project, 0)

    def units(t, carry):
        at = pl.multiple_of(t * 128, 128)
        grad_act = grad_act_ref[:, pl.ds(at, 128)]
        gate = acc[:, pl.ds(at, 128)]
        up = acc[:, pl.ds(at + FW, 128)]
        sigmoid = 1.0 / (1.0 + jnp.exp(-gate))
        silu = gate * sigmoid
        act_ref[:, pl.ds(at, 128)] = (silu * up).astype(LOW)
        grad_gate = grad_act * up * sigmoid * (1.0 + gate * (1.0 - sigmoid))
        grad_ref[:, pl.ds(at, 128)] = grad_gate.astype(LOW)
        grad_ref[:, pl.ds(at + FW, 128)] = (grad_act * silu).astype(LOW)
        return carry

    lax.fori_loop(0, FW // 128, units, 0)

    def spread(p, carry):
        split_rows(dot(grad_ref[...], held[p], 1, 1), part, core, p, keep_ref, send_ref)
        return carry

    lax.fori_loop(0, PIECES, spread, 0)


def feed_forward(meta, own, got, grad_act, w_gu):
    return pl.pallas_call(
        ffn_kernel,
        in_specs=[smem()] + [whole()] * 3 + [hbm()] * 16,
        out_specs=[whole()] * 4,
        out_shape=[
            jax.ShapeDtypeStruct((SEQ, FW), LOW),
            jax.ShapeDtypeStruct((SEQ, GU), LOW),
        ]
        + split_shapes(),
        scratch_shapes=[
            pltpu.VMEM((PIECES, BLK, GU), LOW),
            pltpu.VMEM((SEQ, GU), F32),
            pltpu.VMEM((SEQ, LANES), LOW),
            pltpu.SemaphoreType.DMA((PIECES,)),
        ],
        compiler_params=pltpu.CompilerParams(vmem_limit_bytes=VMEM),
        cost_estimate=cost(0, 0),
        name="feed_forward",
    )(meta, own, got, grad_act, *w_gu)


def halves_of(part_ref, xc_ref, q, at):
    rows = jnp.concatenate([part_ref[z, q] for z in range(RING)], axis=0)
    return rows[:, :BLK], xc_ref[q, at : at + 128][:, :BLK]


def merge_kernel(rows_ref, *refs, parted):
    one_ref, two_ref = refs[-2:]
    for p in range(RING):
        for ref, q in ((one_ref, p), (two_ref, RING + p)):
            if parted:
                for z in range(RING):
                    ref[p, 32 * z : 32 * z + 32] = rows_ref[z, q]
            else:
                ref[p] = rows_ref[q]


def merge(rows, into=()):
    at = 0 if into else 1
    return pl.pallas_call(
        functools.partial(merge_kernel, parted=bool(into)),
        grid=(1,),
        in_specs=[pl.BlockSpec(rows.shape, lambda i: (0,) * rows.ndim)] + [hbm()] * len(into),
        out_specs=[pl.BlockSpec((RING, 128, LANES), lambda i: (0, at, 0))] * 2,
        out_shape=[jax.ShapeDtypeStruct((RING, 256, LANES), LOW)] * 2,
        input_output_aliases={1 + k: k for k in range(len(into))},
        compiler_params=pltpu.CompilerParams(vmem_limit_bytes=VMEM),
        cost_estimate=cost(0, 0),
        name="merge",
    )(rows, *into)


def ffn_terms_kernel(meta_ref, own_ref, got_ref, *rest, axis):
    rights = rest[:8]
    outs = rest[8:12]
    acc = rest[12]
    is_low = meta_ref[0] == 0
    at = meta_ref[axis]
    for k, offset in enumerate(OFFSETS):
        source = lax.rem(at + offset + RING, RING)
        xn = join_rows(is_low, own_ref[source, :128], got_ref[source, :128])[:, :BLK]
        cot = join_rows(is_low, own_ref[source, 128:], got_ref[source, 128:])[:, :BLK]
        down = dot(cot, rights[2 * k][...], 0, 0)
        both = dot(xn, rights[2 * k + 1][...], 0, 0)
        if k == 0:
            acc[:, :FW] = down
            acc[:, FW:] = both
        else:
            acc[:, :FW] += down
            acc[:, FW:] += both
    for k, ref in enumerate(outs):
        ref[:, ATTN:] = acc[k * HALF : (k + 1) * HALF, :].astype(LOW)


def ffn_terms(meta, own, got, rights, axis):
    return pl.pallas_call(
        functools.partial(ffn_terms_kernel, axis=axis),
        in_specs=[smem()] + [whole()] * 10,
        out_specs=[whole()] * 4,
        out_shape=[jax.ShapeDtypeStruct((HALF, WIDE), LOW)] * 4,
        scratch_shapes=[pltpu.VMEM((BLK, 3 * FW), F32)],
        compiler_params=pltpu.CompilerParams(vmem_limit_bytes=VMEM),
        cost_estimate=cost(0, 0),
        name="terms_feed_forward",
    )(meta, own, got, *rights)


def fill_kernel(*refs):
    for k, ref in enumerate(refs[8:]):
        total = refs[0][k].astype(F32)
        for part in refs[1:4]:
            total = total + part[k].astype(F32)
        ref[...] = total.astype(LOW)


def fill(attn, ffn):
    return pl.pallas_call(
        fill_kernel,
        grid=(1,),
        in_specs=[pl.BlockSpec((RING, HALF, ATTN), lambda i: (0, 0, 0))] * 4 + [hbm()] * 4,
        out_specs=[pl.BlockSpec((HALF, ATTN), lambda i: (0, 0))] * 4,
        out_shape=[jax.ShapeDtypeStruct((HALF, WIDE), LOW)] * 4,
        input_output_aliases={4 + k: k for k in range(4)},
        compiler_params=pltpu.CompilerParams(vmem_limit_bytes=VMEM),
        cost_estimate=cost(0, 0),
        name="fill",
    )(*attn, *ffn)


def fetch_kind(is_first, refs, held, sem):
    for kind in range(2):

        @pl.when(is_first if kind == 0 else jnp.logical_not(is_first))
        def _():
            for k in range(RING):
                pltpu.make_async_copy(refs[RING * kind + k], held.at[k], sem).start()

    pltpu.make_async_copy(held, held, sem).wait()


def finish_kernel(meta_ref, *refs):
    out_ref, held, sem = refs[8:]
    fetch_kind(meta_ref[0] == 1, refs[:8], held, sem)
    total = held[0].astype(F32)
    for k in range(1, RING):
        total = total + held[k].astype(F32)
    out_ref[...] = total.astype(LOW)


def finish(meta, parts):
    return pl.pallas_call(
        finish_kernel,
        in_specs=[smem()] + [hbm()] * 8,
        out_specs=whole(),
        out_shape=jax.ShapeDtypeStruct((HALF, WIDE), LOW),
        scratch_shapes=[pltpu.VMEM((RING, HALF, WIDE), LOW), pltpu.SemaphoreType.DMA],
        compiler_params=pltpu.CompilerParams(vmem_limit_bytes=VMEM),
        cost_estimate=cost(0, 0),
        name="finish_other",
    )(meta, *parts[0], *parts[1])


def pick_sum(is_first, refs):
    total = jnp.where(is_first, refs[0][...], refs[4][...]).astype(F32)
    for k in range(1, 4):
        total = total + jnp.where(is_first, refs[k][...], refs[4 + k][...]).astype(F32)
    return total


def adam_kernel(meta_ref, w_ref, m_ref, v_ref, came, *rest):
    parts = rest[:8]
    wo_ref, mo_ref, vo_ref, grad, stay = rest[8:]
    is_low = meta_ref[0] == 0
    stay[...] = pick_sum(is_low, parts)
    rows = w_ref.shape[0]
    for start, at, width in MAP:
        mine = stay[:, at : at + width]
        other = came[:, at : at + width].astype(F32)
        grad[:, start : start + width] = jnp.where(is_low, mine, other)
        grad[:, start + width : start + 2 * width] = jnp.where(is_low, other, mine)
    row = pl.program_id(0) * rows + lax.broadcasted_iota(jnp.int32, (rows, 1), 0)
    valid = row < meta_ref[4]
    weight, first, second = adam_step(
        w_ref[...], m_ref[...], v_ref[...], grad[...], LEARN, DECAY
    )
    wo_ref[...] = jnp.where(valid, weight, 0.0)
    mo_ref[...] = jnp.where(valid, first, 0.0)
    vo_ref[...] = jnp.where(valid, second, 0.0)


def adam(meta, master, moment_one, moment_two, came, parts):
    rows = 32
    units = master.shape[1]

    def block(width):
        return pl.BlockSpec((rows, width), lambda i: (i, 0))

    return pl.pallas_call(
        adam_kernel,
        grid=(pl.cdiv(HALF, rows),),
        in_specs=[smem()] + [block(units)] * 3 + [block(WIDE)] * 9,
        out_specs=[block(units)] * 3,
        out_shape=[jax.ShapeDtypeStruct(master.shape, F32)] * 3,
        scratch_shapes=[pltpu.VMEM((rows, units), F32), pltpu.VMEM((rows, WIDE), F32)],
        compiler_params=pltpu.CompilerParams(vmem_limit_bytes=VMEM),
        name="adam",
    )(meta, master, moment_one, moment_two, came, *parts[0], *parts[1])


def rms_scale(values):
    return lax.rsqrt(jnp.sum(values * values, axis=(0, 2), keepdims=True) / D + EPS_NORM)


def rms_backward(grad_out, normed, scale, gain):
    grad_normed = grad_out * gain
    inner = jnp.sum(grad_normed * normed, axis=(0, 2), keepdims=True) / D
    return scale * (grad_normed - normed * inner), jnp.sum(grad_out * normed, axis=1)


def adam_step(weight, first, second, grad, rate, decay):
    first_new = BETA * first + (1.0 - BETA) * grad
    second_new = BETA * second + (1.0 - BETA) * grad * grad
    inverse = 1.0 / (1.0 - BETA**STEP)
    update = (first_new * inverse) / (jnp.sqrt(second_new * inverse) + EPS_ADAM)
    return (weight - rate * (update + decay * weight), first_new, second_new)


def stage(*values):
    return lax.optimization_barrier(values)


def shards(
    tokens, cotangent, segments, owner, master, moment_one, moment_two, gains, gain_one, gain_two
):
    core = lax.axis_index("core")
    yl = lax.axis_index("yl")
    z = lax.axis_index("z")
    x = lax.axis_index(X)
    y = lax.axis_index("yh") * 2 + yl
    count = jnp.sum((owner == (y // 2 * RING + x) * 2 + core).astype(jnp.int32)) - yl * HALF
    place = jnp.stack([core, z, x, y]).astype(jnp.int32)
    meta = jnp.stack([core, z, x, y, count]).astype(jnp.int32)
    along = (Y, X)
    across = (X, Y)

    def add_core(keep, other):
        return (keep.astype(F32) + other.astype(F32)).astype(LOW)

    def split_z(block):
        return lax.all_to_all(block, "z", split_axis=0, concat_axis=0, tiled=True)

    def sum_z(block):
        return jnp.sum(block.astype(F32), axis=0)

    def all_z(block):
        return split_z(jnp.broadcast_to(block[None], (RING, *block.shape)))

    own, send = pack(place, owner, master)
    got = swap_core(send)
    first = jnp.where(core == 0, own, got)
    second = jnp.where(core == 0, got, own)
    first, second, owner, tokens, cotangent = stage(first, second, owner, tokens, cotangent)

    near_first = near(first, X)
    near_second = near(second, Y)
    numbers = jnp.zeros((8, D), LOW).at[0, :SEQ].set(segments.astype(LOW))
    tokens = swap_sequences(jnp.concatenate([tokens, numbers], axis=0))
    onehot = (owner[:, None] == jnp.arange(16, dtype=jnp.int32)[None, :]).astype(jnp.int32)
    rank = ranks(onehot)
    slot = (owner * CAP + rank)[:, None]
    ids = slot_ids(x, y)
    parts = jnp.concatenate([three_parts(gains), jnp.zeros((10, D), LOW)], axis=0)
    near_first, near_second, slot, ids, parts, cotangent = stage(
        near_first, near_second, slot, ids, parts, cotangent
    )

    blocks = [
        (first, *near_first, *halves(*near_first, X, WIDE_CUT)),
        (second, *near_second, *halves(*near_second, Y, WIDE_CUT)),
    ]
    attn = [assemble(b, 0) for b in blocks]
    attn, blocks, tokens, cotangent = stage(attn, blocks, tokens, cotangent)

    attn_near = [near(b, axis) for b, axis in zip(attn, along)]
    position = jnp.arange(SEQ, dtype=F32)
    freq = jnp.exp(-jnp.log(THETA) * (2.0 * jnp.arange(HD // 2, dtype=F32) / HD))
    angle = position[:, None] * freq[None, :]
    tables = (
        jnp.concatenate([jnp.cos(angle)] * 2, axis=1),
        jnp.concatenate([jnp.sin(angle)] * 2, axis=1),
    )
    segment = tokens[128, :SEQ].astype(jnp.int32)
    segs = (segment[:, None], segment[None, :])
    down = [assemble(b, 1) for b in blocks]
    cotangent = swap_sequences(cotangent)
    attn_near, down, tables, segs, tokens, cotangent = stage(
        attn_near, down, tables, segs, tokens, cotangent
    )
    down_near = [near(b, axis) for b, axis in zip(down, along)]
    xn_own, inputs, gain = tokens_to_slots(meta, slot, ids, tokens, gains, parts)
    gate = [assemble(b, 2) for b in blocks]
    turned = (slot.reshape(1, D), ids)
    down_near, blocks, gate, turned, xn_own, inputs, gain, cotangent = stage(
        down_near, blocks, gate, turned, xn_own, inputs, gain, cotangent
    )
    pair_far = [far(q[0], d[1], axis) for q, d, axis in zip(attn_near, down_near, along)]
    up = [assemble(b, 3) for b in blocks]
    xn_got = swap_core(xn_own)
    cot_own, cot_z = cot_to_slots(meta, slot, ids, cotangent)
    pair_far, gate, up, xn_got, cot_own, cot_z = stage(pair_far, gate, up, xn_got, cot_own, cot_z)
    w_attn = []
    w_down = []
    for kind in range(2):
        w_attn += [attn[kind], *attn_near[kind], pair_far[kind][0]]
        w_down += [down[kind], *down_near[kind], pair_far[kind][1]]

    gate_near = [near(b, axis) for b, axis in zip(gate, along)]
    *qkv, attended, keep, send = attention_forward(meta, xn_own, xn_got, tables, segs, w_attn)
    cot_got = swap_core(cot_own)
    gate_near, up, keep, send, cot_got = stage(gate_near, up, keep, send, cot_got)
    up_near = [near(b, axis) for b, axis in zip(up, along)]
    got = split_z(add_core(keep, swap_core(send)))
    grad_act = down_back(meta, cot_own, cot_got, w_down)
    left_cot = merge(cot_own)
    up_near, gate_near, got, grad_act, left_cot = stage(
        up_near, gate_near, got, grad_act, left_cot
    )
    gu_far = [far(g[0], u[1], axis) for g, u, axis in zip(gate_near, up_near, along)]
    hidden = inputs + sum_z(got)
    scale_two = rms_scale(hidden)
    normed_two = hidden * scale_two
    xn_two = all_z((normed_two * gain[:, 1:2]).astype(LOW))
    gu_far, xn_two = stage(gu_far, xn_two)
    xn_two_got = swap_core(xn_two)
    left_sent = merge(xn_two, left_cot)
    xn_two, xn_two_got, grad_act, left_sent = stage(xn_two, xn_two_got, grad_act, left_sent)
    w_gu = []
    for kind in range(2):
        w_gu += [gate[kind], up[kind]]
        w_gu += [gate_near[kind][0], up_near[kind][0], gate_near[kind][1], up_near[kind][1]]
        w_gu += [*gu_far[kind]]

    act, grad_gu, keep, send = feed_forward(meta, xn_two, xn_two_got, grad_act, w_gu)
    def exchange(block, axis):
        return lax.all_to_all(block, axis, split_axis=0, concat_axis=0, tiled=True)

    lefts = [exchange(left_sent[0], Y)]
    act, grad_gu, keep, send, lefts = stage(act, grad_gu, keep, send, lefts)
    gu_near = [near(grad_gu, axis) for axis in along]
    got = split_z(add_core(keep, swap_core(send)))
    keep_mlp, send_mlp = down_forward(meta, act, w_down)
    gu_near, got, keep_mlp, send_mlp, act = stage(gu_near, got, keep_mlp, send_mlp, act)
    act_near = [near(act, axis) for axis in along]
    lefts_got = [swap_core(lefts[0])]
    mlp_both = add_core(keep_mlp, swap_core(send_mlp))
    grad_xn_two = sum_z(got)
    grad_norm_two, gain_grad_two = rms_backward(grad_xn_two, normed_two, scale_two, gain[:, 1:2])
    grad_hidden = cot_z + grad_norm_two
    grad_branch = lax.all_gather(grad_hidden.astype(LOW), "z", axis=0, tiled=False)
    lefts.append(exchange(left_sent[1], X))
    act_near, grad_branch, grad_hidden, gain_grad_two, lefts, lefts_got, gu_near, mlp_both = stage(
        act_near, grad_branch, grad_hidden, gain_grad_two, lefts, lefts_got, gu_near, mlp_both
    )
    grad_branch_got = swap_core(grad_branch)
    ends = [far(a[0], g[1], axis) for a, g, axis in zip(act_near, gu_near, along)]

    xns = (xn_own, xn_got)
    keep, send, *terms = attention_backward(
        meta, grad_branch, grad_branch_got, tables, segs, (*qkv, attended), xns, w_attn
    )
    attn_terms = (terms[:4], terms[4:])
    mlp = lax.psum_scatter(mlp_both, "z", scatter_dimension=0, tiled=True)[0]
    ends, keep, send, attn_terms, lefts, mlp = stage(ends, keep, send, attn_terms, lefts, mlp)

    def direct(first, second, axes):
        _, back, ahead, last = first
        _, back_two, ahead_two, last_two = second
        one = (move(ahead, axes[0], 1), move(back, axes[0], -1), move(last, axes[0], 2))
        up = move(ahead_two, axes[1], 1)
        down = move(back_two, axes[1], -1)
        return one, up, down, last_two

    attn_nears = [
        (move(t[2], axis, 1), move(t[1], axis, -1)) for t, axis in zip(attn_terms, along)
    ]

    def rights_of(kind):
        rights = (act, grad_gu)
        for n in range(2):
            rights += (act_near[kind][n], gu_near[kind][n])
        return rights + tuple(ends[kind])

    ffn_sums = [ffn_terms(meta, lefts[0], lefts_got[0], rights_of(0), 3)]
    lefts_got.append(swap_core(lefts[1]))
    got = split_z(add_core(keep, swap_core(send)))
    attn_nears, attn_terms, lefts, lefts_got, ffn_sums, got = stage(
        attn_nears, attn_terms, lefts, lefts_got, ffn_sums, got
    )
    attn_others = [
        (*n, move(t[3], axis, 2)) for n, t, axis in zip(attn_nears, attn_terms, along)
    ]
    ffn_sums.append(ffn_terms(meta, lefts[1], lefts_got[1], rights_of(1), 2))
    grad_xn_one = sum_z(got)
    scale_one = rms_scale(inputs)
    grad_norm_one, gain_grad_one = rms_backward(
        grad_xn_one, inputs * scale_one, scale_one, gain[:, 0:1]
    )
    grad_tokens_z = (grad_hidden + grad_norm_one).astype(LOW)
    output_z = (hidden + mlp.astype(F32)).astype(LOW)
    gain_grads = three_parts(jnp.stack([gain_grad_one, gain_grad_two], axis=0))
    gain_grads = jnp.swapaxes(gain_grads, 0, 1)
    blank = jnp.zeros((PIECES, 10, LANES), LOW)
    last = from_slots(
        jnp.concatenate([output_z, grad_tokens_z, gain_grads, blank], axis=1), *turned
    )
    attn_others, ffn_sums, last = stage(attn_others, ffn_sums, last)
    blocks = [fill((t[0], *o), f) for t, o, f in zip(attn_terms, attn_others, ffn_sums)]
    part = lax.all_gather(last, "z", axis=0, tiled=False)
    one, up, down, last_two = direct(*blocks, across)
    up, down, last_two = stage(up, down, last_two)
    others = (one, (up, down, move(last_two, across[1], 2)))
    others, owns = stage(others, [b[0] for b in blocks])
    totals = [(b, *o) for b, o in zip(owns, others)]
    send, totals = stage(finish(meta, totals), totals)
    came = swap_core(send)
    moved = swap_sequences(jnp.swapaxes(part[:, :64].reshape(RING, 2, 32, D), 0, 1))
    gain_grads = part[:, 64:70].astype(F32).sum(axis=0)
    gain_grads = gain_grads[:2] + gain_grads[2:4] + gain_grads[4:6]
    gain_other = swap_core(gain_grads)
    came, gain_other, totals = stage(came, gain_other, totals)

    def sum_along(value, axis):
        back, ahead = near(value, axis)
        return (value + move(value, axis, 2)) + (back + ahead)

    gain_grads = sum_along(gain_grads + gain_other, X)
    new_master, new_one, new_two = adam(meta, master, moment_one, moment_two, came, totals)
    gain_grads, new_master, moved = stage(gain_grads, new_master, moved)
    gain_grads = sum_along(gain_grads, Y)
    output = moved[0].reshape(128, D)
    grad_tokens = moved[1].reshape(128, D)
    new_gains, new_gain_one, new_gain_two = adam_step(
        gains, gain_one, gain_two, gain_grads, LEARN_GAIN, 0.0
    )
    return (
        output,
        grad_tokens,
        new_master,
        new_one,
        new_two,
        new_gains,
        new_gain_one,
        new_gain_two,
    )


def solution(mesh):
    fine = Mesh(mesh.devices.reshape(2, 4, 2, 2, 4), ("yh", "x", "core", "yl", "z"))
    rows = ("yh", "x", "core", "yl")
    in_specs = (
        P(rows, None),
        P(rows, None),
        P(("yh", "x", "core")),
        P(),
        P(rows, "z"),
        P(rows, "z"),
        P(rows, "z"),
        P(),
        P(),
        P(),
    )
    out_specs = (
        P(rows, None),
        P(rows, None),
        P(rows, "z"),
        P(rows, "z"),
        P(rows, "z"),
        P(),
        P(),
        P(),
    )
    return jax.shard_map(shards, mesh=fine, in_specs=in_specs, out_specs=out_specs, check_vma=False)
```
